32 devices in a mesh: batch: 2 (over core), inner: 4 (over y, x), outer: 4 (over z).
Axes of the slice: x: 2, y: 2, z: 4, core: 2. Of those that a mesh axis runs over, the one named last changes fastest.
Arguments:
- images: bfloat16 [32, 16, 32, 1024], P(('batch', 'inner'), None, None, 'outer'), may hold values from -6 to 6
- extents: int32 [32, 2], replicated, may hold values from 4 to 16, as said below
- first_reduce: bfloat16 [1024, 512], P('outer', 'inner'), may hold values from -0.1875 to 0.1875
- first_taps: bfloat16 [3, 3, 512, 512], P(None, None, None, ('inner', 'outer')), may hold values from -0.09375 to 0.09375
- first_expand: bfloat16 [512, 2048], P('inner', 'outer'), may hold values from -0.25 to 0.25
- first_shortcut: bfloat16 [1024, 2048], P('outer', 'inner'), may hold values from -0.1875 to 0.1875
- second_reduce: bfloat16 [2048, 512], P('outer', 'inner'), may hold values from -0.125 to 0.125
- second_taps: bfloat16 [3, 3, 512, 512], P(None, None, None, ('inner', 'outer')), may hold values from -0.09375 to 0.09375
- second_expand: bfloat16 [512, 2048], P('inner', 'outer'), may hold values from -0.25 to 0.25
- mid_gains: float32 [4, 512], replicated, may hold values from 0.1 to 1.9
- mid_shifts: float32 [4, 512], replicated, may hold values from -3 to 3
- wide_gains: float32 [3, 2048], replicated, may hold values from 0.1 to 1.9
- wide_shifts: float32 [3, 2048], replicated, may hold values from -3 to 3
- cotangent: bfloat16 [32, 8, 16, 2048], P(('batch', 'inner'), None, None, 'outer'), may hold values from -6 to 6
Outputs:
- block_output: bfloat16 [32, 8, 16, 2048], P(('batch', 'inner'), None, None, 'outer')
- grad_images: float32 [32, 16, 32, 1024], P(('batch', 'inner'), None, None, 'outer')
- grad_first_reduce: float32 [1024, 512], P('outer', 'inner')
- grad_first_taps: float32 [3, 3, 512, 512], P(None, None, None, ('inner', 'outer'))
- grad_first_expand: float32 [512, 2048], P('inner', 'outer')
- grad_first_shortcut: float32 [1024, 2048], P('outer', 'inner')
- grad_second_reduce: float32 [2048, 512], P('outer', 'inner')
- grad_second_taps: float32 [3, 3, 512, 512], P(None, None, None, ('inner', 'outer'))
- grad_second_expand: float32 [512, 2048], P('inner', 'outer')
- grad_mid_gains: float32 [4, 512], replicated
- grad_mid_shifts: float32 [4, 512], replicated
- grad_wide_gains: float32 [3, 2048], replicated
- grad_wide_shifts: float32 [3, 2048], replicated
The draws below stay inside these ranges and needn't reach their ends.
Inputs may be any that keep to these rules, and one draw needn't show every extreme that they name: `extents`: row n holds image n's height (from 4 to 8) and width (from 8 to 16) in output cells; some image is exactly 8 by 16.
All inputs are finite; a program needn't handle non-finite values.
Results may differ from the reference program's by a relative error of at most 0.017.
Values may be sent and summed in bfloat16 or wider, within the bound.
No kernel may reach another device: no remote copies, remote signals or barrier semaphores. Data moves between devices by JAX's collectives and lax.ppermute only.
A program may use at most 192 MiB of HBM per device.

```python
import jax
import jax.numpy as jnp
from jax import lax

C_IN = 1024
MID = 512
C_OUT = 2048
HO = 8
WO = 16
HI = 16
WI = 32
IMAGES = 32


def draw_extents(key, part):
    key = jax.random.fold_in(key, 11)
    key_rows, key_cols, key_full = jax.random.split(key, 3)
    heights = jax.random.randint(key_rows, (IMAGES,), HO // 2, HO + 1)
    widths = jax.random.randint(key_cols, (IMAGES,), WO // 2, WO + 1)
    chosen = jax.random.randint(key_full, (), 0, IMAGES)
    picked = jnp.arange(IMAGES) == chosen
    heights = jnp.where(picked, HO, heights)
    widths = jnp.where(picked, WO, widths)
    return jnp.stack([heights, widths], axis=1).astype(jnp.int32)


def level_of(rng, extent, cuts, low, high):
    loudness = 1.0
    for position, parts in cuts:
        draws = jax.random.uniform(jax.random.fold_in(jax.random.fold_in(rng, 6), position), (parts,), jnp.float32, low / len(cuts), high / len(cuts))
        loudness = loudness * jnp.repeat(jnp.exp(draws), extent[position] // parts).reshape((-1,) + (1,) * (len(extent) - 1 - position))
    return loudness


def noise(rng, dims, scale, reach, cuts=(), kind=jnp.bfloat16):
    gain = level_of(rng, dims, cuts, -0.22, 0.18) if cuts else 1.0
    values = jax.random.normal(rng, dims, jnp.float32) * scale * gain
    return jnp.minimum(jnp.maximum(values, -reach), reach).astype(kind)


def setup_inputs(seed: int = 0) -> dict:
    key_list = jax.random.split(jax.random.key(seed), 15)
    images = noise(key_list[0], (IMAGES, HI, WI, C_IN), 1.0, 6.0, ((0, 8), (3, 4)))
    extents = draw_extents(jax.random.fold_in(key_list[14], 71), 0)
    first_reduce = noise(key_list[2], (C_IN, MID), C_IN ** -0.5, 0.1875, ((0, 4), (1, 4)))
    first_taps = noise(key_list[3], (3, 3, MID, MID), (9 * MID) ** -0.5, 0.09375, ((3, 16),))
    first_expand = noise(key_list[4], (MID, C_OUT), MID ** -0.5, 0.25, ((0, 4), (1, 4)))
    first_shortcut = noise(key_list[5], (C_IN, C_OUT), C_IN ** -0.5, 0.1875, ((0, 4), (1, 4)))
    second_reduce = noise(key_list[6], (C_OUT, MID), C_OUT ** -0.5, 0.125, ((0, 4), (1, 4)))
    second_taps = noise(key_list[7], (3, 3, MID, MID), (9 * MID) ** -0.5, 0.09375, ((3, 16),))
    second_expand = noise(key_list[8], (MID, C_OUT), MID ** -0.5, 0.25, ((0, 4), (1, 4)))
    mid_gains = jnp.clip(1.0 + 0.18 * jax.random.normal(key_list[9], (4, MID), jnp.float32), 0.1, 1.9)
    mid_shifts = noise(key_list[10], (4, MID), 0.5, 3.0, (), jnp.float32)
    wide_gains = jnp.clip(1.0 + 0.18 * jax.random.normal(key_list[11], (3, C_OUT), jnp.float32), 0.1, 1.9)
    wide_shifts = noise(key_list[12], (3, C_OUT), 0.5, 3.0, (), jnp.float32)
    cotangent = noise(key_list[13], (IMAGES, HO, WO, C_OUT), 1.0, 6.0, ((0, 8), (3, 4)))
    return {"images": images, "extents": extents, "first_reduce": first_reduce, "first_taps": first_taps, "first_expand": first_expand, "first_shortcut": first_shortcut, "second_reduce": second_reduce, "second_taps": second_taps, "second_expand": second_expand, "mid_gains": mid_gains, "mid_shifts": mid_shifts, "wide_gains": wide_gains, "wide_shifts": wide_shifts, "cotangent": cotangent}


EPS = 1e-05
HIGH = lax.Precision.HIGHEST

@jax.custom_vjp
def low(v):
    return lax.optimization_barrier(v.astype(jnp.bfloat16)).astype(jnp.float32)

@jax.custom_vjp
def low_back(v):
    return v

def low_keep(v):
    return (low(v), None)

def low_pass(kept, grad):
    return (grad,)

def back_keep(v):
    return (v, None)

def back_low(kept, grad):
    return (low(grad),)
low.defvjp(low_keep, low_pass)
low_back.defvjp(back_keep, back_low)

def valid_mask(extents, rows_all, cols_all, factor):
    heights = extents[:, 0] * factor
    widths = extents[:, 1] * factor
    inside_rows = jnp.arange(rows_all, dtype=jnp.int32)[None, :, None] < heights[:, None, None]
    inside_cols = jnp.arange(cols_all, dtype=jnp.int32)[None, None, :] < widths[:, None, None]
    return jnp.logical_and(inside_rows, inside_cols).astype(jnp.float32)[..., None]

def pointwise(activation, weight):
    return jnp.einsum('nhwc,cd->nhwd', activation, weight, precision=HIGH)

def taps_conv(activation, weight, stride):
    padded = jnp.pad(activation, ((0, 0), (1, 1), (1, 1), (0, 0)))
    summed = jnp.zeros((activation.shape[0], HO, WO, weight.shape[3]), jnp.float32)
    for tap_row in range(3):
        for tap_col in range(3):
            window = padded[:, tap_row:tap_row + stride * (HO - 1) + 1:stride, tap_col:tap_col + stride * (WO - 1) + 1:stride, :]
            summed = summed + pointwise(window, weight[tap_row, tap_col])
    return summed

def normalize(tensor, valid_cells, cell_count, gain_row, shift_row):
    mean_row = lax.optimization_barrier(jnp.sum(tensor * valid_cells, axis=(0, 1, 2))) / cell_count
    spread = lax.optimization_barrier(jnp.sum(tensor * tensor * valid_cells, axis=(0, 1, 2))) / cell_count - mean_row * mean_row
    return (tensor - mean_row) * lax.rsqrt(spread + EPS) * gain_row + shift_row

def forward(images, first_reduce, first_taps, first_expand, first_shortcut, second_reduce, second_taps, second_expand, mid_gains, mid_shifts, wide_gains, wide_shifts, valid_in, valid_out, count_in, count_out):
    masked = images * valid_in
    z_one = low_back(pointwise(masked, first_reduce))
    act_one = low(jax.nn.gelu(normalize(z_one, valid_in, count_in, mid_gains[0], mid_shifts[0])) * valid_in)
    z_two = low_back(taps_conv(act_one, first_taps, 2))
    act_two = low(jax.nn.gelu(normalize(z_two, valid_out, count_out, mid_gains[1], mid_shifts[1])) * valid_out)
    z_three = low_back(pointwise(act_two, first_expand))
    z_short = low_back(pointwise(masked[:, 0::2, 0::2, :], first_shortcut))
    joined_one = normalize(z_three, valid_out, count_out, wide_gains[0], wide_shifts[0]) + normalize(z_short, valid_out, count_out, wide_gains[1], wide_shifts[1])
    hidden = jax.nn.gelu(joined_one) * valid_out
    z_four = low_back(pointwise(low(hidden), second_reduce))
    act_four = low(jax.nn.gelu(normalize(z_four, valid_out, count_out, mid_gains[2], mid_shifts[2])) * valid_out)
    z_five = low_back(taps_conv(act_four, second_taps, 1))
    act_five = low(jax.nn.gelu(normalize(z_five, valid_out, count_out, mid_gains[3], mid_shifts[3])) * valid_out)
    z_six = low_back(pointwise(act_five, second_expand))
    joined_two = normalize(z_six, valid_out, count_out, wide_gains[2], wide_shifts[2]) + hidden
    return jax.nn.gelu(joined_two) * valid_out

def reference(images, extents, first_reduce, first_taps, first_expand, first_shortcut, second_reduce, second_taps, second_expand, mid_gains, mid_shifts, wide_gains, wide_shifts, cotangent):
    valid_in = valid_mask(extents, HI, WI, 2)
    valid_out = valid_mask(extents, HO, WO, 1)
    count_in = jnp.sum(valid_in)
    count_out = jnp.sum(valid_out)

    def closed(image_values, reduce_one, taps_one, expand_one, shortcut_one, reduce_two, taps_two, expand_two, gains_mid, shifts_mid, gains_wide, shifts_wide):
        return forward(image_values, reduce_one, taps_one, expand_one, shortcut_one, reduce_two, taps_two, expand_two, gains_mid, shifts_mid, gains_wide, shifts_wide, valid_in, valid_out, count_in, count_out)
    result, pullback = jax.vjp(closed, images.astype(jnp.float32), first_reduce.astype(jnp.float32), first_taps.astype(jnp.float32), first_expand.astype(jnp.float32), first_shortcut.astype(jnp.float32), second_reduce.astype(jnp.float32), second_taps.astype(jnp.float32), second_expand.astype(jnp.float32), mid_gains, mid_shifts, wide_gains, wide_shifts)
    grads = pullback(cotangent.astype(jnp.float32))
    return (result.astype(jnp.bfloat16), grads[0], grads[1], grads[2], grads[3], grads[4], grads[5], grads[6], grads[7], grads[8], grads[9], grads[10], grads[11])
```

```python
import math

import jax
import jax.numpy as jnp
from jax import lax
from jax.sharding import PartitionSpec as P

EPS = 1e-05
ROOT = math.sqrt(2.0 / math.pi)
CUBE = 0.044715
F32 = jnp.float32
BF16 = jnp.bfloat16


def mm(left, right):
    return jnp.dot(left, right, preferred_element_type=F32)


def mm_nt(left, right):
    return lax.dot_general(left, right, (((1,), (1,)), ((), ())), preferred_element_type=F32)


def mm_tn(left, right):
    return lax.dot_general(left, right, (((0,), (0,)), ((), ())), preferred_element_type=F32)


def gelu(v):
    return 0.5 * v * (1.0 + jnp.tanh(ROOT * (v + CUBE * v * v * v)))


def gelu_both(v):
    t = jnp.tanh(ROOT * (v + CUBE * v * v * v))
    half = 0.5 * (1.0 + t)
    return v * half, half + 0.5 * v * (1.0 - t * t) * (ROOT * (1.0 + 3.0 * CUBE * v * v))


def gelu_slope(v):
    return gelu_both(v)[1]


def shards(
    images,
    extents,
    first_reduce,
    first_taps,
    first_expand,
    first_shortcut,
    second_reduce,
    second_taps,
    second_expand,
    mid_gains,
    mid_shifts,
    wide_gains,
    wide_shifts,
    cotangent,
):
    nb = lax.axis_size("batch")
    ni = lax.axis_size("inner")
    no = lax.axis_size("outer")
    b = lax.axis_index("batch")
    i = lax.axis_index("inner")
    o = lax.axis_index("outer")
    c = b % 2
    img_dev, hi, wi, in_part = images.shape
    ho, wo = hi // 2, wi // 2
    out_part = cotangent.shape[3]
    m = img_dev // no
    pair = 2 * m
    cells_in, cells_out = hi * wi, ho * wo
    mid = mid_gains.shape[1]
    mid_h = mid // 2
    in_h = in_part // 2
    out_h = out_part // 2
    kin_h = no * in_h
    wide_h = no * out_h

    def core_swap(x):
        return lax.ppermute(x, "batch", [(k, k ^ 1) for k in range(nb)])

    def pick(low, high):
        return jnp.where(c == 0, low, high)

    def mine(x, axis):
        h = x.shape[axis] // 2
        return pick(lax.slice_in_dim(x, 0, h, axis=axis), lax.slice_in_dim(x, h, 2 * h, axis=axis))

    def other(x, axis):
        h = x.shape[axis] // 2
        return pick(lax.slice_in_dim(x, h, 2 * h, axis=axis), lax.slice_in_dim(x, 0, h, axis=axis))

    def swap_add(x, axis):
        return mine(x, axis) + core_swap(other(x, axis))

    def join(own, recv, axis):
        return pick(jnp.concatenate([own, recv], axis), jnp.concatenate([recv, own], axis))

    def swap_full(x, axis):
        return join(x, core_swap(x), axis)

    def over_batch(x):
        total = x
        for k in range(1, nb // 2):
            total = total + lax.ppermute(x, "batch", [(j, (j + 2 * k) % nb) for j in range(nb)])
        return total

    def sums_of(rows):
        sizes = [r.shape[0] for r in rows]
        flat = jnp.concatenate(rows).reshape(-1, 128)
        copies = jnp.broadcast_to(flat[None], (ni * no,) + flat.shape)
        got = lax.all_to_all(copies, ("inner", "outer"), split_axis=0, concat_axis=0, tiled=True)
        total = over_batch(jnp.sum(got, axis=0)).reshape(-1)
        out, start = [], 0
        for s in sizes:
            out.append(total[start : start + s])
            start += s
        return out

    def to_images(x):
        return lax.all_to_all(x, "outer", split_axis=0, concat_axis=0, tiled=True)

    def gather_blocks(shard):
        rows, cols = shard.shape
        ring = [(k, (k + 1) % no) for k in range(no)]
        piece = shard
        whole = jnp.zeros((no, rows, cols), shard.dtype)
        whole = lax.dynamic_update_slice(whole, piece[None], (o, 0, 0))
        for step in range(1, no):
            piece = lax.ppermute(piece, "outer", ring)
            whole = lax.dynamic_update_slice(whole, piece[None], ((o + no - step) % no, 0, 0))
        if ni != 4:
            return lax.all_gather(whole, "inner", axis=0, tiled=False)
        h = rows // 2
        xs = [(k, k ^ 1) for k in range(4)]
        ys = [(k, k ^ 2) for k in range(4)]
        by_x = lax.ppermute(whole, "inner", xs)
        by_y = lax.ppermute(whole, "inner", ys)
        low = lax.ppermute(by_x[:, :h], "inner", ys)
        high = lax.ppermute(by_y[:, h:], "inner", xs)
        full = jnp.zeros((4, no, rows, cols), shard.dtype)
        full = lax.dynamic_update_slice(full, whole[None], (i, 0, 0, 0))
        full = lax.dynamic_update_slice(full, by_x[None], (i ^ 1, 0, 0, 0))
        full = lax.dynamic_update_slice(full, by_y[None], (i ^ 2, 0, 0, 0))
        full = lax.dynamic_update_slice(full, low[None], (i ^ 3, 0, 0, 0))
        return lax.dynamic_update_slice(full, high[None], (i ^ 3, 0, h, 0))

    def scatter_blocks(blocks):
        rows, cols = blocks.shape[2:]
        if ni != 4:
            mine_i = lax.psum_scatter(blocks.astype(F32), "inner", scatter_dimension=0, tiled=True)[0]
        else:
            h = rows // 2
            xs = [(k, k ^ 1) for k in range(4)]
            ys = [(k, k ^ 2) for k in range(4)]

            def block(k):
                return lax.dynamic_index_in_dim(blocks, k, 0, keepdims=False)

            far = block(i ^ 3)
            low = lax.ppermute(far[:, :h], "inner", xs)
            high = lax.ppermute(far[:, h:], "inner", ys)
            for_x, for_y = block(i ^ 1), block(i ^ 2)
            for_x = jnp.concatenate(
                [for_x[:, :h], (for_x[:, h:].astype(F32) + high.astype(F32)).astype(BF16)], 1
            )
            for_y = jnp.concatenate(
                [(for_y[:, :h].astype(F32) + low.astype(F32)).astype(BF16), for_y[:, h:]], 1
            )
            by_x = lax.ppermute(for_x, "inner", xs)
            by_y = lax.ppermute(for_y, "inner", ys)
            mine_i = block(i).astype(F32) + by_x.astype(F32) + by_y.astype(F32)
        parts = lax.all_to_all(
            mine_i.astype(BF16), "outer", split_axis=0, concat_axis=0, tiled=True
        )
        return over_batch(jnp.sum(parts.astype(F32), axis=0))

    def masks():
        first = ((b - c) * ni + i) * img_dev + o * m
        lows = lax.dynamic_slice_in_dim(extents, first, m, 0)
        highs = lax.dynamic_slice_in_dim(extents, first + ni * img_dev, m, 0)
        ext = jnp.concatenate([lows, highs], 0)
        return ext[:, 0], ext[:, 1]

    heights, widths = masks()
    out_cell = jnp.arange(cells_out, dtype=jnp.int32)
    out_row, out_col = out_cell // wo, out_cell % wo
    valid_out = (
        ((out_row[None] < heights[:, None]) & (out_col[None] < widths[:, None]))
        .astype(F32)
        .reshape(pair * cells_out, 1)
    )
    in_cell = jnp.arange(cells_in, dtype=jnp.int32)
    phase = in_cell // cells_out
    ph_row = 2 * (in_cell % cells_out // wo) + phase // 2
    ph_col = 2 * (in_cell % wo) + phase % 2
    valid_ph = (ph_row[None] < 2 * heights[:, None]) & (ph_col[None] < 2 * widths[:, None])
    valid_in = valid_ph.astype(F32).reshape(pair * cells_in, 1)
    source = ph_row * wi + ph_col
    order = ((source[None, :, None] == in_cell[None, None, :]) & valid_ph[:, :, None]).astype(BF16)
    count_out = jnp.sum(extents[:, 0] * extents[:, 1]).astype(F32)
    count_in = 4.0 * count_out

    def shift_matrix(dr, dc):
        rr, cc = out_row + dr, out_col + dc
        inside = (rr >= 0) & (rr < ho) & (cc >= 0) & (cc < wo)
        return ((rr * wo + cc)[:, None] == out_cell[None, :]) & inside[:, None]

    def selected(matrix, x):
        return jnp.einsum("ps,msk->mpk", matrix, x, preferred_element_type=F32).astype(BF16)

    got = to_images(images.reshape(img_dev, cells_in, in_part))
    shard_r1 = mine(first_reduce, 0)

    def taps_shard(w):
        k_half = mine(w, 2).reshape(9, mid_h, -1)
        return k_half.transpose(2, 0, 1).reshape(-1, 9 * mid_h)

    full_r1 = gather_blocks(shard_r1)
    full_t1 = gather_blocks(taps_shard(first_taps))
    full_es = gather_blocks(jnp.concatenate([mine(first_expand, 1), mine(first_shortcut, 1)], 0))
    rows_e = first_expand.shape[0]
    full_e1, full_s = full_es[:, :, :rows_e], full_es[:, :, rows_e:]
    full_r2 = gather_blocks(mine(second_reduce, 0))
    full_t2 = gather_blocks(taps_shard(second_taps))
    full_e2 = gather_blocks(mine(second_expand, 1))

    def outer_rows(full):
        r, k = full.shape[2:]
        return full.transpose(1, 2, 0, 3).reshape(no * r, ni * k)

    def inner_rows(full):
        r, k = full.shape[2:]
        return full.transpose(0, 2, 1, 3).reshape(ni * r, no * k)

    def outer_blocks(whole, r, k):
        return whole.reshape(no, r, ni, k).transpose(2, 0, 1, 3)

    def inner_blocks(whole, r, k):
        return whole.reshape(ni, r, no, k).transpose(0, 2, 1, 3)

    w_r1 = outer_rows(full_r1)
    w_t1 = full_t1.reshape(mid, 9 * mid_h)
    w_e1 = inner_rows(full_e1)
    w_s = outer_rows(full_s)
    w_r2 = outer_rows(full_r2)
    w_t2 = full_t2.reshape(mid, 9 * mid_h)
    w_e2 = inner_rows(full_e2)

    def both_images(x, lanes):
        own = mine(x, 3)
        recv = core_swap(other(x, 3))
        low, high = pick(own, recv), pick(recv, own)
        stacked = jnp.concatenate([low, high], 1)
        return stacked.transpose(1, 2, 0, 3).reshape(pair, x.shape[2], no * lanes)

    def own_images(x, lanes):
        low, high = x[:m], x[m:]
        own = pick(low, high)
        recv = core_swap(pick(high, low))
        cells = x.shape[1]
        own = own.reshape(m, cells, no, lanes)
        recv = recv.reshape(m, cells, no, lanes)
        return join(own, recv, 3).transpose(2, 0, 1, 3)

    raw = both_images(got.reshape(no, m, cells_in, in_part), in_h)
    masked = jnp.einsum("mps,msk->mpk", order, raw, preferred_element_type=F32).astype(BF16)
    masked_rows = masked.reshape(pair * cells_in, kin_h)
    strided_h = masked[:, :cells_out].reshape(pair * cells_out, kin_h)
    recv = core_swap(strided_h)
    s_low, s_high = pick(strided_h, recv), pick(recv, strided_h)
    strided = jnp.stack(
        [s_low.reshape(-1, no, in_h), s_high.reshape(-1, no, in_h)], 2
    ).reshape(pair * cells_out, no * in_part)

    def mid_half(vector):
        return mine(vector, 0)

    def wide_half(vector):
        return mine(vector.reshape(no, out_part), 1).reshape(wide_h)

    def stats(total, squares, count):
        mean = total / count
        return mean, lax.rsqrt(squares / count - mean * mean + EPS)

    def col_sums(z, valid):
        zv = z * valid
        return [jnp.sum(zv, 0), jnp.sum(zv * z, 0)]

    def xhat_of(z, st):
        return (z - st[0]) * st[1]

    gm = [mid_half(mid_gains[k]) for k in range(4)]
    sm = [mid_half(mid_shifts[k]) for k in range(4)]
    gw = [wide_half(wide_gains[k]) for k in range(3)]
    sw = [wide_half(wide_shifts[k]) for k in range(3)]

    z_one = swap_add(mm(masked_rows, w_r1), 1)
    t, q = sums_of(col_sums(z_one, valid_in))
    st_one = stats(t, q, count_in)
    act_one = (gelu(xhat_of(z_one, st_one) * gm[0] + sm[0]) * valid_in).astype(BF16)

    planes = act_one.reshape(pair, 4, cells_out, mid_h)
    shifts_down = {
        (dr, dc): shift_matrix(dr, dc).astype(BF16) for dr in (-1, 0, 1) for dc in (-1, 0, 1)
    }
    windows = []
    for p in range(3):
        for r in range(3):
            plane = planes[:, 2 * int(p != 1) + int(r != 1)]
            key = (-int(p == 0), -int(r == 0))
            windows.append(plane if key == (0, 0) else selected(shifts_down[key], plane))
    win_one = jnp.concatenate(windows, -1).reshape(pair * cells_out, 9 * mid_h)
    z_two = swap_add(mm_nt(win_one, w_t1), 1)
    t, q = sums_of(col_sums(z_two, valid_out))
    st_two = stats(t, q, count_out)
    act_two_h = (gelu(xhat_of(z_two, st_two) * gm[1] + sm[1]) * valid_out).astype(BF16)
    act_two = swap_full(act_two_h, 1)
    z_three = mm(act_two, w_e1)
    z_short = mm(strided, w_s)
    t, q, ts, qs = sums_of(col_sums(z_three, valid_out) + col_sums(z_short, valid_out))
    st_three, st_short = stats(t, q, count_out), stats(ts, qs, count_out)
    joined_one = (xhat_of(z_three, st_three) * gw[0] + sw[0]) + (
        xhat_of(z_short, st_short) * gw[1] + sw[1]
    )
    hidden = gelu(joined_one) * valid_out
    hidden_low = hidden.astype(BF16)
    z_four = swap_add(mm(hidden_low, w_r2), 1)
    t, q = sums_of(col_sums(z_four, valid_out))
    st_four = stats(t, q, count_out)
    act_four = (gelu(xhat_of(z_four, st_four) * gm[2] + sm[2]) * valid_out).astype(BF16)
    plane = act_four.reshape(pair, cells_out, mid_h)
    windows = []
    for p in range(3):
        for r in range(3):
            key = (p - 1, r - 1)
            windows.append(plane if key == (0, 0) else selected(shifts_down[key], plane))
    win_two = jnp.concatenate(windows, -1).reshape(pair * cells_out, 9 * mid_h)
    z_five = swap_add(mm_nt(win_two, w_t2), 1)
    t, q = sums_of(col_sums(z_five, valid_out))
    st_five = stats(t, q, count_out)
    act_five_h = (gelu(xhat_of(z_five, st_five) * gm[3] + sm[3]) * valid_out).astype(BF16)
    act_five = swap_full(act_five_h, 1)
    z_six = mm(act_five, w_e2)
    t, q = sums_of(col_sums(z_six, valid_out))
    st_six = stats(t, q, count_out)
    xhat_six = xhat_of(z_six, st_six)
    joined_two = xhat_six * gw[2] + sw[2] + hidden

    cot = both_images(
        to_images(cotangent.reshape(img_dev, cells_out, out_part)).reshape(
            no, m, cells_out, out_part
        ),
        out_h,
    ).reshape(pair * cells_out, wide_h)
    value, slope = gelu_both(joined_two)
    out_pair = (value * valid_out).astype(BF16).reshape(pair, cells_out, wide_h)
    block_output = to_images(
        own_images(out_pair, out_h).reshape(img_dev, cells_out, out_part)
    ).reshape(img_dev, ho, wo, out_part)
    dy_six = cot.astype(F32) * valid_out * slope

    def back(dy, xhat, gain, st, valid, shift_sum, gain_sum, count):
        return (gain * st[1] * (dy - valid * ((shift_sum + xhat * gain_sum) / count))).astype(BF16)

    def dy_sums(dy, *xhats):
        return [jnp.sum(dy, 0)] + [jnp.sum(dy * x, 0) for x in xhats]

    def to_bf16(x):
        return x.astype(BF16)

    s6, g6 = sums_of(dy_sums(dy_six, xhat_six))
    dz_six = back(dy_six, xhat_six, gw[2], st_six, valid_out, s6, g6, count_out)
    grad_e2 = scatter_blocks(
        inner_blocks(to_bf16(mm_tn(act_five, dz_six)), second_expand.shape[0], out_h)
    )
    da_five = swap_add(mm_nt(dz_six, w_e2), 1)

    xhat_five = xhat_of(z_five, st_five)
    dy_five = da_five * valid_out * gelu_slope(xhat_five * gm[3] + sm[3])
    s5, g5 = sums_of(dy_sums(dy_five, xhat_five))
    dz_five = swap_full(
        back(dy_five, xhat_five, gm[3], st_five, valid_out, s5, g5, count_out), 1
    )
    grad_t2 = scatter_blocks(
        to_bf16(mm_tn(dz_five, win_two)).reshape(ni, no, mid // (ni * no), 9 * mid_h)
    )
    dz_cells = dz_five.reshape(pair, cells_out, mid)
    da_four = 0.0
    for p in range(3):
        for r in range(3):
            key = (1 - p, 1 - r)
            moved = dz_cells if key == (0, 0) else selected(shifts_down[key], dz_cells)
            tap = 3 * p + r
            da_four = da_four + mm(
                moved.reshape(pair * cells_out, mid), w_t2[:, tap * mid_h : (tap + 1) * mid_h]
            )
    xhat_four = xhat_of(z_four, st_four)
    dy_four = da_four * valid_out * gelu_slope(xhat_four * gm[2] + sm[2])
    s4, g4 = sums_of(dy_sums(dy_four, xhat_four))
    dz_four = swap_full(
        back(dy_four, xhat_four, gm[2], st_four, valid_out, s4, g4, count_out), 1
    )
    grad_r2 = scatter_blocks(
        outer_blocks(to_bf16(mm_tn(hidden_low, dz_four)), out_h, second_reduce.shape[1])
    )
    grad_hidden = dy_six + mm_nt(dz_four, w_r2)
    dy_joined = grad_hidden * valid_out * gelu_slope(joined_one)
    xhat_three, xhat_short = xhat_of(z_three, st_three), xhat_of(z_short, st_short)
    s3, g3, gs = sums_of(dy_sums(dy_joined, xhat_three, xhat_short))
    dz_three = back(dy_joined, xhat_three, gw[0], st_three, valid_out, s3, g3, count_out)
    dz_short = back(dy_joined, xhat_short, gw[1], st_short, valid_out, s3, gs, count_out)
    grad_es = scatter_blocks(
        jnp.concatenate(
            [
                inner_blocks(to_bf16(mm_tn(act_two, dz_three)), rows_e, out_h),
                outer_blocks(to_bf16(mm_tn(strided, dz_short)), in_part, out_h),
            ],
            2,
        )
    )
    da_two = swap_add(mm_nt(dz_three, w_e1), 1)
    d_short = mm_nt(dz_short, w_s).reshape(pair * cells_out, no, in_part)
    d_short = swap_add(d_short, 2).reshape(pair, cells_out, kin_h)

    xhat_two = xhat_of(z_two, st_two)
    dy_two = da_two * valid_out * gelu_slope(xhat_two * gm[1] + sm[1])
    s2, g2 = sums_of(dy_sums(dy_two, xhat_two))
    dz_two = swap_full(back(dy_two, xhat_two, gm[1], st_two, valid_out, s2, g2, count_out), 1)
    grad_t1 = scatter_blocks(
        to_bf16(mm_tn(dz_two, win_one)).reshape(ni, no, mid // (ni * no), 9 * mid_h)
    )
    dz_cells = dz_two.reshape(pair, cells_out, mid)
    moved = {}
    for dr in (0, 1):
        for dc in (0, 1):
            y = dz_cells if (dr, dc) == (0, 0) else selected(shifts_down[(dr, dc)], dz_cells)
            moved[(dr, dc)] = y.reshape(pair * cells_out, mid)
    plane_grads = []
    for pr in range(2):
        for pc in range(2):
            total = 0.0
            for p in (1,) if pr == 0 else (0, 2):
                for r in (1,) if pc == 0 else (0, 2):
                    tap = 3 * p + r
                    total = total + mm(
                        moved[(int(p == 0), int(r == 0))],
                        w_t1[:, tap * mid_h : (tap + 1) * mid_h],
                    )
            plane_grads.append(total.reshape(pair, cells_out, mid_h))
    da_one = jnp.concatenate(plane_grads, 1).reshape(pair * cells_in, mid_h)
    xhat_one = xhat_of(z_one, st_one)
    dy_one = da_one * valid_in * gelu_slope(xhat_one * gm[0] + sm[0])
    s1, g1 = sums_of(dy_sums(dy_one, xhat_one))
    dz_one = swap_full(back(dy_one, xhat_one, gm[0], st_one, valid_in, s1, g1, count_in), 1)
    grad_r1 = scatter_blocks(
        outer_blocks(to_bf16(mm_tn(masked_rows, dz_one)), in_h, first_reduce.shape[1])
    )
    d_in = mm_nt(dz_one, w_r1).reshape(pair, cells_in, kin_h)
    d_in = jnp.concatenate([d_in[:, :cells_out] + d_short, d_in[:, cells_out:]], 1)
    d_raw = jnp.einsum(
        "mps,mpk->msk", order, d_in.astype(BF16), preferred_element_type=F32
    ).astype(BF16)
    grad_images = (
        to_images(own_images(d_raw, in_h).reshape(img_dev, cells_in, in_part))
        .astype(F32)
        .reshape(images.shape)
    )

    def taps_out(half):
        rows = half.reshape(-1, 9, mid_h).transpose(1, 0, 2)
        both = swap_full(rows, 2)
        return both.transpose(0, 2, 1).reshape(first_taps.shape)

    grad_e1_s = swap_full(grad_es, 1)
    mids = jnp.concatenate([g1, g2, g4, g5, s1, s2, s4, s5]).reshape(8, mid_h)
    mids = swap_full(mids, 1)
    wides = jnp.concatenate([g3, gs, g6, s3, s6]).reshape(5, no, out_h)
    wides = swap_full(wides, 2).reshape(5, no * out_part)
    return (
        block_output,
        grad_images,
        swap_full(grad_r1, 0),
        taps_out(grad_t1),
        grad_e1_s[:rows_e],
        grad_e1_s[rows_e:],
        swap_full(grad_r2, 0),
        taps_out(grad_t2),
        swap_full(grad_e2, 1),
        mids[:4],
        mids[4:],
        wides[:3],
        jnp.stack([wides[3], wides[3], wides[4]]),
    )


def solution(mesh):
    wide = P(("batch", "inner"), None, None, "outer")
    down = P("outer", "inner")
    up = P("inner", "outer")
    taps = P(None, None, None, ("inner", "outer"))
    whole = P()
    return jax.shard_map(
        shards,
        mesh=mesh,
        in_specs=(wide, whole, down, taps, up, down, down, taps, up)
        + (whole, whole, whole, whole, wide),
        out_specs=(wide, wide, down, taps, up, down, down, taps, up, whole, whole, whole, whole),
        check_vma=False,
    )
```

```python
import math

import jax
import jax.numpy as jnp
from jax import lax
from jax.experimental import pallas as pl
from jax.experimental.pallas import tpu as pltpu
from jax.sharding import PartitionSpec as P

EPS = 1e-05
ROOT = math.sqrt(2.0 / math.pi)
CUBE = 0.044715
F32 = jnp.float32
BF16 = jnp.bfloat16
XS = [(k, k ^ 1) for k in range(4)]
YS = [(k, k ^ 2) for k in range(4)]


def mm(left, right):
    return jnp.dot(left, right, preferred_element_type=F32)


def mm_nt(left, right):
    return lax.dot_general(left, right, (((1,), (1,)), ((), ())), preferred_element_type=F32)


def mm_tn(left, right):
    return lax.dot_general(left, right, (((0,), (0,)), ((), ())), preferred_element_type=F32)


def gelu(v):
    return 0.5 * v * (1.0 + jnp.tanh(ROOT * (v + CUBE * v * v * v)))


def gelu_both(v):
    t = jnp.tanh(ROOT * (v + CUBE * v * v * v))
    half = 0.5 * (1.0 + t)
    return v * half, half + 0.5 * v * (1.0 - t * t) * (ROOT * (1.0 + 3.0 * CUBE * v * v))


def gelu_slope(v):
    return gelu_both(v)[1]


def shards(
    images,
    extents,
    first_reduce,
    first_taps,
    first_expand,
    first_shortcut,
    second_reduce,
    second_taps,
    second_expand,
    mid_gains,
    mid_shifts,
    wide_gains,
    wide_shifts,
    cotangent,
):
    nb = lax.axis_size("batch")
    ni = lax.axis_size("inner")
    no = lax.axis_size("outer")
    b = lax.axis_index("batch")
    i = lax.axis_index("inner")
    o = lax.axis_index("outer")
    c = b % 2
    img_dev, hi, wi, in_part = images.shape
    ho, wo = hi // 2, wi // 2
    out_part = cotangent.shape[3]
    m = img_dev // no
    pair = 2 * m
    cells_in, cells_out = hi * wi, ho * wo
    mid = mid_gains.shape[1]
    mid_h = mid // 2
    in_h = in_part // 2
    out_h = out_part // 2
    kin_h = no * in_h
    wide_h = no * out_h

    def core_swap(x):
        return lax.ppermute(x, "batch", [(k, k ^ 1) for k in range(nb)])

    def pick(low, high):
        return jnp.where(c == 0, low, high)

    def mine(x, axis):
        h = x.shape[axis] // 2
        return pick(lax.slice_in_dim(x, 0, h, axis=axis), lax.slice_in_dim(x, h, 2 * h, axis=axis))

    def other(x, axis):
        h = x.shape[axis] // 2
        return pick(lax.slice_in_dim(x, h, 2 * h, axis=axis), lax.slice_in_dim(x, 0, h, axis=axis))

    def swap_add(x, axis):
        return mine(x, axis) + core_swap(other(x, axis))

    def join(own, recv, axis):
        return pick(jnp.concatenate([own, recv], axis), jnp.concatenate([recv, own], axis))

    def swap_full(x, axis):
        return join(x, core_swap(x), axis)

    def over_batch(x):
        total = x
        for k in range(1, nb // 2):
            total = total + lax.ppermute(x, "batch", [(j, (j + 2 * k) % nb) for j in range(nb)])
        return total

    def sums_of(rows):
        sizes = [r.shape[0] for r in rows]
        flat = jnp.concatenate(rows).reshape(-1, 128)
        copies = jnp.broadcast_to(flat[None], (ni * no,) + flat.shape)
        got = lax.all_to_all(copies, ("inner", "outer"), split_axis=0, concat_axis=0, tiled=True)
        total = over_batch(jnp.sum(got, axis=0)).reshape(-1)
        out, start = [], 0
        for s in sizes:
            out.append(total[start : start + s])
            start += s
        return out

    def to_images(x):
        return lax.all_to_all(x, "outer", split_axis=0, concat_axis=0, tiled=True)

    def gather_pieces(shard):
        ring = [(k, (k + 1) % no) for k in range(no)]
        pieces = [shard]
        for _ in range(1, no):
            pieces.append(lax.ppermute(pieces[-1], "outer", ring))
        whole = jnp.stack(pieces)
        h = shard.shape[0] // 2
        by_x = lax.ppermute(whole, "inner", XS)
        by_y = lax.ppermute(whole, "inner", YS)
        low = lax.ppermute(by_x[:, :h], "inner", YS)
        high = lax.ppermute(by_y[:, h:], "inner", XS)
        return whole, by_x, by_y, low, high

    def assemble(pieces, segments):
        rows, cols = pieces[0].shape[1:]
        h = rows // 2
        spans = [(0, 0, rows), (1, 0, rows), (2, 0, rows), (3, 0, h), (3, h, rows)]
        plan = []
        for src, (far, lo, hi_row) in enumerate(spans):
            for d in range(no):
                for dst, (first, count, _, place) in enumerate(segments):
                    a, z = max(lo, first), min(hi_row, first + count)
                    if a < z:
                        plan.append((src, far, d, a - lo, z - a, dst, a - first, place))
        n_src, n_dst = len(spans), len(segments)

        def kernel(where, *refs):
            sources, targets = refs[:n_src], refs[n_src:]
            me_i, me_o = where[0], where[1]
            for src, far, d, begin, count, dst, offset, place in plan:
                row, col, row_unit, col_unit = place(me_i ^ far, lax.rem(me_o + (no - d), no))
                targets[dst][
                    pl.ds(pl.multiple_of(row * row_unit, row_unit) + offset, count),
                    pl.ds(pl.multiple_of(col * col_unit, col_unit), cols),
                ] = sources[src][d, begin : begin + count, :]

        return pl.pallas_call(
            kernel,
            out_shape=[jax.ShapeDtypeStruct(seg[2], BF16) for seg in segments],
            in_specs=[pl.BlockSpec(memory_space=pltpu.SMEM)]
            + [pl.BlockSpec(memory_space=pltpu.VMEM)] * n_src,
            out_specs=[pl.BlockSpec(memory_space=pltpu.VMEM)] * n_dst,
            compiler_params=pltpu.CompilerParams(vmem_limit_bytes=24 << 20),
        )(jnp.stack([i, o]).astype(jnp.int32), *pieces)

    def scatter_blocks(blocks):
        rows, cols = blocks.shape[2:]
        if ni != 4:
            mine_i = lax.psum_scatter(blocks.astype(F32), "inner", scatter_dimension=0, tiled=True)[0]
        else:
            h = rows // 2
            def block(k):
                return lax.dynamic_index_in_dim(blocks, k, 0, keepdims=False)

            far = block(i ^ 3)
            low = lax.ppermute(far[:, :h], "inner", XS)
            high = lax.ppermute(far[:, h:], "inner", YS)
            for_x, for_y = block(i ^ 1), block(i ^ 2)
            for_x = jnp.concatenate(
                [for_x[:, :h], (for_x[:, h:].astype(F32) + high.astype(F32)).astype(BF16)], 1
            )
            for_y = jnp.concatenate(
                [(for_y[:, :h].astype(F32) + low.astype(F32)).astype(BF16), for_y[:, h:]], 1
            )
            by_x = lax.ppermute(for_x, "inner", XS)
            by_y = lax.ppermute(for_y, "inner", YS)
            mine_i = block(i).astype(F32) + by_x.astype(F32) + by_y.astype(F32)
        parts = lax.all_to_all(
            mine_i.astype(BF16), "outer", split_axis=0, concat_axis=0, tiled=True
        )
        return over_batch(jnp.sum(parts.astype(F32), axis=0))

    def masks():
        first = ((b - c) * ni + i) * img_dev + o * m
        lows = lax.dynamic_slice_in_dim(extents, first, m, 0)
        highs = lax.dynamic_slice_in_dim(extents, first + ni * img_dev, m, 0)
        ext = jnp.concatenate([lows, highs], 0)
        return ext[:, 0], ext[:, 1]

    heights, widths = masks()
    out_cell = jnp.arange(cells_out, dtype=jnp.int32)
    out_row, out_col = out_cell // wo, out_cell % wo
    valid_out = (
        ((out_row[None] < heights[:, None]) & (out_col[None] < widths[:, None]))
        .astype(F32)
        .reshape(pair * cells_out, 1)
    )
    in_cell = jnp.arange(cells_in, dtype=jnp.int32)
    phase = in_cell // cells_out
    ph_row = 2 * (in_cell % cells_out // wo) + phase // 2
    ph_col = 2 * (in_cell % wo) + phase % 2
    valid_ph = (ph_row[None] < 2 * heights[:, None]) & (ph_col[None] < 2 * widths[:, None])
    valid_in = valid_ph.astype(F32).reshape(pair * cells_in, 1)
    source = ph_row * wi + ph_col
    order = ((source[None, :, None] == in_cell[None, None, :]) & valid_ph[:, :, None]).astype(BF16)
    count_out = jnp.sum(extents[:, 0] * extents[:, 1]).astype(F32)
    count_in = 4.0 * count_out

    def shift_matrix(dr, dc):
        rr, cc = out_row + dr, out_col + dc
        inside = (rr >= 0) & (rr < ho) & (cc >= 0) & (cc < wo)
        return ((rr * wo + cc)[:, None] == out_cell[None, :]) & inside[:, None]

    def selected(matrix, x):
        return jnp.einsum("ps,msk->mpk", matrix, x, preferred_element_type=F32).astype(BF16)

    got = to_images(images.reshape(img_dev, cells_in, in_part))

    def taps_shard(w):
        k_half = mine(w, 2).reshape(9, mid_h, -1)
        return k_half.transpose(2, 0, 1).reshape(-1, 9 * mid_h)

    def down_place(r, k):
        return lambda at_i, at_o: (at_o, at_i, r, k)

    def up_place(r, k):
        return lambda at_i, at_o: (at_i, at_o, r, k)

    def taps_place(r, k):
        return lambda at_i, at_o: (at_i * no + at_o, 0, r, k)

    def gathered(*entries):
        shard = entries[0][0] if len(entries) == 1 else jnp.concatenate([e[0] for e in entries], 0)
        segments, first = [], 0
        for part, place in entries:
            r, k = part.shape
            at = place(r, k)
            shape = {down_place: (no * r, ni * k), up_place: (ni * r, no * k)}.get(
                place, (ni * no * r, k)
            )
            segments.append((first, r, shape, at))
            first += r
        return assemble(gather_pieces(shard), segments)

    (w_r1,) = gathered((mine(first_reduce, 0), down_place))
    (w_t1,) = gathered((taps_shard(first_taps), taps_place))
    w_e1, w_s = gathered((mine(first_expand, 1), up_place), (mine(first_shortcut, 1), down_place))
    (w_r2,) = gathered((mine(second_reduce, 0), down_place))
    (w_t2,) = gathered((taps_shard(second_taps), taps_place))
    (w_e2,) = gathered((mine(second_expand, 1), up_place))
    rows_e = first_expand.shape[0]

    def outer_blocks(whole, r, k):
        return whole.reshape(no, r, ni, k).transpose(2, 0, 1, 3)

    def inner_blocks(whole, r, k):
        return whole.reshape(ni, r, no, k).transpose(0, 2, 1, 3)

    def both_images(x, lanes):
        own = mine(x, 3)
        recv = core_swap(other(x, 3))
        low, high = pick(own, recv), pick(recv, own)
        stacked = jnp.concatenate([low, high], 1)
        return stacked.transpose(1, 2, 0, 3).reshape(pair, x.shape[2], no * lanes)

    def own_images(x, lanes):
        low, high = x[:m], x[m:]
        own = pick(low, high)
        recv = core_swap(pick(high, low))
        cells = x.shape[1]
        own = own.reshape(m, cells, no, lanes)
        recv = recv.reshape(m, cells, no, lanes)
        return join(own, recv, 3).transpose(2, 0, 1, 3)

    raw = both_images(got.reshape(no, m, cells_in, in_part), in_h)
    masked = jnp.einsum("mps,msk->mpk", order, raw, preferred_element_type=F32).astype(BF16)
    masked_rows = masked.reshape(pair * cells_in, kin_h)
    strided_h = masked[:, :cells_out].reshape(pair * cells_out, kin_h)
    recv = core_swap(strided_h)
    s_low, s_high = pick(strided_h, recv), pick(recv, strided_h)
    strided = jnp.stack(
        [s_low.reshape(-1, no, in_h), s_high.reshape(-1, no, in_h)], 2
    ).reshape(pair * cells_out, no * in_part)

    def mid_half(vector):
        return mine(vector, 0)

    def wide_half(vector):
        return mine(vector.reshape(no, out_part), 1).reshape(wide_h)

    def stats(total, squares, count):
        mean = total / count
        return mean, lax.rsqrt(squares / count - mean * mean + EPS)

    def col_sums(z, valid):
        zv = z * valid
        return [jnp.sum(zv, 0), jnp.sum(zv * z, 0)]

    def xhat_of(z, st):
        return (z - st[0]) * st[1]

    gm = [mid_half(mid_gains[k]) for k in range(4)]
    sm = [mid_half(mid_shifts[k]) for k in range(4)]
    gw = [wide_half(wide_gains[k]) for k in range(3)]
    sw = [wide_half(wide_shifts[k]) for k in range(3)]

    z_one = swap_add(mm(masked_rows, w_r1), 1)
    t, q = sums_of(col_sums(z_one, valid_in))
    st_one = stats(t, q, count_in)
    act_one = (gelu(xhat_of(z_one, st_one) * gm[0] + sm[0]) * valid_in).astype(BF16)

    planes = act_one.reshape(pair, 4, cells_out, mid_h)
    shifts_down = {
        (dr, dc): shift_matrix(dr, dc).astype(BF16) for dr in (-1, 0, 1) for dc in (-1, 0, 1)
    }
    windows = []
    for p in range(3):
        for r in range(3):
            plane = planes[:, 2 * int(p != 1) + int(r != 1)]
            key = (-int(p == 0), -int(r == 0))
            windows.append(plane if key == (0, 0) else selected(shifts_down[key], plane))
    win_one = jnp.concatenate(windows, -1).reshape(pair * cells_out, 9 * mid_h)
    z_two = swap_add(mm_nt(win_one, w_t1), 1)
    t, q = sums_of(col_sums(z_two, valid_out))
    st_two = stats(t, q, count_out)
    act_two_h = (gelu(xhat_of(z_two, st_two) * gm[1] + sm[1]) * valid_out).astype(BF16)
    act_two = swap_full(act_two_h, 1)
    z_three = mm(act_two, w_e1)
    z_short = mm(strided, w_s)
    t, q, ts, qs = sums_of(col_sums(z_three, valid_out) + col_sums(z_short, valid_out))
    st_three, st_short = stats(t, q, count_out), stats(ts, qs, count_out)
    joined_one = (xhat_of(z_three, st_three) * gw[0] + sw[0]) + (
        xhat_of(z_short, st_short) * gw[1] + sw[1]
    )
    hidden = gelu(joined_one) * valid_out
    hidden_low = hidden.astype(BF16)
    z_four = swap_add(mm(hidden_low, w_r2), 1)
    t, q = sums_of(col_sums(z_four, valid_out))
    st_four = stats(t, q, count_out)
    act_four = (gelu(xhat_of(z_four, st_four) * gm[2] + sm[2]) * valid_out).astype(BF16)
    plane = act_four.reshape(pair, cells_out, mid_h)
    windows = []
    for p in range(3):
        for r in range(3):
            key = (p - 1, r - 1)
            windows.append(plane if key == (0, 0) else selected(shifts_down[key], plane))
    win_two = jnp.concatenate(windows, -1).reshape(pair * cells_out, 9 * mid_h)
    z_five = swap_add(mm_nt(win_two, w_t2), 1)
    t, q = sums_of(col_sums(z_five, valid_out))
    st_five = stats(t, q, count_out)
    act_five_h = (gelu(xhat_of(z_five, st_five) * gm[3] + sm[3]) * valid_out).astype(BF16)
    act_five = swap_full(act_five_h, 1)
    z_six = mm(act_five, w_e2)
    t, q = sums_of(col_sums(z_six, valid_out))
    st_six = stats(t, q, count_out)
    xhat_six = xhat_of(z_six, st_six)
    joined_two = xhat_six * gw[2] + sw[2] + hidden

    cot = both_images(
        to_images(cotangent.reshape(img_dev, cells_out, out_part)).reshape(
            no, m, cells_out, out_part
        ),
        out_h,
    ).reshape(pair * cells_out, wide_h)
    value, slope = gelu_both(joined_two)
    out_pair = (value * valid_out).astype(BF16).reshape(pair, cells_out, wide_h)
    block_output = to_images(
        own_images(out_pair, out_h).reshape(img_dev, cells_out, out_part)
    ).reshape(img_dev, ho, wo, out_part)
    dy_six = cot.astype(F32) * valid_out * slope

    def back(dy, xhat, gain, st, valid, shift_sum, gain_sum, count):
        return (gain * st[1] * (dy - valid * ((shift_sum + xhat * gain_sum) / count))).astype(BF16)

    def dy_sums(dy, *xhats):
        return [jnp.sum(dy, 0)] + [jnp.sum(dy * x, 0) for x in xhats]

    def to_bf16(x):
        return x.astype(BF16)

    s6, g6 = sums_of(dy_sums(dy_six, xhat_six))
    dz_six = back(dy_six, xhat_six, gw[2], st_six, valid_out, s6, g6, count_out)
    grad_e2 = scatter_blocks(
        inner_blocks(to_bf16(mm_tn(act_five, dz_six)), second_expand.shape[0], out_h)
    )
    da_five = swap_add(mm_nt(dz_six, w_e2), 1)

    xhat_five = xhat_of(z_five, st_five)
    dy_five = da_five * valid_out * gelu_slope(xhat_five * gm[3] + sm[3])
    s5, g5 = sums_of(dy_sums(dy_five, xhat_five))
    dz_five = swap_full(
        back(dy_five, xhat_five, gm[3], st_five, valid_out, s5, g5, count_out), 1
    )
    grad_t2 = scatter_blocks(
        to_bf16(mm_tn(dz_five, win_two)).reshape(ni, no, mid // (ni * no), 9 * mid_h)
    )
    dz_cells = dz_five.reshape(pair, cells_out, mid)
    da_four = 0.0
    for p in range(3):
        for r in range(3):
            key = (1 - p, 1 - r)
            moved = dz_cells if key == (0, 0) else selected(shifts_down[key], dz_cells)
            tap = 3 * p + r
            da_four = da_four + mm(
                moved.reshape(pair * cells_out, mid), w_t2[:, tap * mid_h : (tap + 1) * mid_h]
            )
    xhat_four = xhat_of(z_four, st_four)
    dy_four = da_four * valid_out * gelu_slope(xhat_four * gm[2] + sm[2])
    s4, g4 = sums_of(dy_sums(dy_four, xhat_four))
    dz_four = swap_full(
        back(dy_four, xhat_four, gm[2], st_four, valid_out, s4, g4, count_out), 1
    )
    grad_r2 = scatter_blocks(
        outer_blocks(to_bf16(mm_tn(hidden_low, dz_four)), out_h, second_reduce.shape[1])
    )
    grad_hidden = dy_six + mm_nt(dz_four, w_r2)
    dy_joined = grad_hidden * valid_out * gelu_slope(joined_one)
    xhat_three, xhat_short = xhat_of(z_three, st_three), xhat_of(z_short, st_short)
    s3, g3, gs = sums_of(dy_sums(dy_joined, xhat_three, xhat_short))
    dz_three = back(dy_joined, xhat_three, gw[0], st_three, valid_out, s3, g3, count_out)
    dz_short = back(dy_joined, xhat_short, gw[1], st_short, valid_out, s3, gs, count_out)
    grad_es = scatter_blocks(
        jnp.concatenate(
            [
                inner_blocks(to_bf16(mm_tn(act_two, dz_three)), rows_e, out_h),
                outer_blocks(to_bf16(mm_tn(strided, dz_short)), in_part, out_h),
            ],
            2,
        )
    )
    da_two = swap_add(mm_nt(dz_three, w_e1), 1)
    d_short = mm_nt(dz_short, w_s).reshape(pair * cells_out, no, in_part)
    d_short = swap_add(d_short, 2).reshape(pair, cells_out, kin_h)

    xhat_two = xhat_of(z_two, st_two)
    dy_two = da_two * valid_out * gelu_slope(xhat_two * gm[1] + sm[1])
    s2, g2 = sums_of(dy_sums(dy_two, xhat_two))
    dz_two = swap_full(back(dy_two, xhat_two, gm[1], st_two, valid_out, s2, g2, count_out), 1)
    grad_t1 = scatter_blocks(
        to_bf16(mm_tn(dz_two, win_one)).reshape(ni, no, mid // (ni * no), 9 * mid_h)
    )
    dz_cells = dz_two.reshape(pair, cells_out, mid)
    moved = {}
    for dr in (0, 1):
        for dc in (0, 1):
            y = dz_cells if (dr, dc) == (0, 0) else selected(shifts_down[(dr, dc)], dz_cells)
            moved[(dr, dc)] = y.reshape(pair * cells_out, mid)
    plane_grads = []
    for pr in range(2):
        for pc in range(2):
            total = 0.0
            for p in (1,) if pr == 0 else (0, 2):
                for r in (1,) if pc == 0 else (0, 2):
                    tap = 3 * p + r
                    total = total + mm(
                        moved[(int(p == 0), int(r == 0))],
                        w_t1[:, tap * mid_h : (tap + 1) * mid_h],
                    )
            plane_grads.append(total.reshape(pair, cells_out, mid_h))
    da_one = jnp.concatenate(plane_grads, 1).reshape(pair * cells_in, mid_h)
    xhat_one = xhat_of(z_one, st_one)
    dy_one = da_one * valid_in * gelu_slope(xhat_one * gm[0] + sm[0])
    s1, g1 = sums_of(dy_sums(dy_one, xhat_one))
    dz_one = swap_full(back(dy_one, xhat_one, gm[0], st_one, valid_in, s1, g1, count_in), 1)
    grad_r1 = scatter_blocks(
        outer_blocks(to_bf16(mm_tn(masked_rows, dz_one)), in_h, first_reduce.shape[1])
    )
    d_in = mm_nt(dz_one, w_r1).reshape(pair, cells_in, kin_h)
    d_in = jnp.concatenate([d_in[:, :cells_out] + d_short, d_in[:, cells_out:]], 1)
    d_raw = jnp.einsum(
        "mps,mpk->msk", order, d_in.astype(BF16), preferred_element_type=F32
    ).astype(BF16)
    grad_images = (
        to_images(own_images(d_raw, in_h).reshape(img_dev, cells_in, in_part))
        .astype(F32)
        .reshape(images.shape)
    )

    def taps_out(half):
        rows = half.reshape(-1, 9, mid_h).transpose(1, 0, 2)
        both = swap_full(rows, 2)
        return both.transpose(0, 2, 1).reshape(first_taps.shape)

    grad_e1_s = swap_full(grad_es, 1)
    mids = jnp.concatenate([g1, g2, g4, g5, s1, s2, s4, s5]).reshape(8, mid_h)
    mids = swap_full(mids, 1)
    wides = jnp.concatenate([g3, gs, g6, s3, s6]).reshape(5, no, out_h)
    wides = swap_full(wides, 2).reshape(5, no * out_part)
    return (
        block_output,
        grad_images,
        swap_full(grad_r1, 0),
        taps_out(grad_t1),
        grad_e1_s[:rows_e],
        grad_e1_s[rows_e:],
        swap_full(grad_r2, 0),
        taps_out(grad_t2),
        swap_full(grad_e2, 1),
        mids[:4],
        mids[4:],
        wides[:3],
        jnp.stack([wides[3], wides[3], wides[4]]),
    )


def solution(mesh):
    wide = P(("batch", "inner"), None, None, "outer")
    down = P("outer", "inner")
    up = P("inner", "outer")
    taps = P(None, None, None, ("inner", "outer"))
    whole = P()
    return jax.shard_map(
        shards,
        mesh=mesh,
        in_specs=(wide, whole, down, taps, up, down, down, taps, up)
        + (whole, whole, whole, whole, wide),
        out_specs=(wide, wide, down, taps, up, down, down, taps, up, whole, whole, whole, whole),
        check_vma=False,
    )
```

```python
import math

import jax
import jax.numpy as jnp
from jax import lax
from jax.experimental import pallas as pl
from jax.experimental.pallas import tpu as pltpu
from jax.sharding import PartitionSpec as P

EPS = 1e-05
ROOT = math.sqrt(2.0 / math.pi)
CUBE = 0.044715
F32 = jnp.float32
BF16 = jnp.bfloat16
XS = [(k, k ^ 1) for k in range(4)]
YS = [(k, k ^ 2) for k in range(4)]
FAR = 3
GEO = 3
TAPS = [(p, r) for p in range(3) for r in range(3)]


def mm(left, right):
    return lax.dot_general(left, right, (((1,), (0,)), ((), ())), preferred_element_type=F32)


def mm_nt(left, right):
    return lax.dot_general(left, right, (((1,), (1,)), ((), ())), preferred_element_type=F32)


def mm_tn(left, right):
    return lax.dot_general(left, right, (((0,), (0,)), ((), ())), preferred_element_type=F32)


def gelu(v):
    return 0.5 * v * (1.0 + jnp.tanh(ROOT * (v + CUBE * v * v * v)))


def gelu_both(v):
    t = jnp.tanh(ROOT * (v + CUBE * v * v * v))
    half = 0.5 * (1.0 + t)
    return v * half, half + 0.5 * v * (1.0 - t * t) * (ROOT * (1.0 + 3.0 * CUBE * v * v))


def gelu_slope(v):
    return gelu_both(v)[1]


def halves(x, k):
    if k & (k - 1) == 0:
        s = k.bit_length() - 1
        return lax.shift_right_logical(x, jnp.int32(s)), lax.bitwise_and(x, jnp.int32(k - 1))
    return lax.div(x, jnp.int32(k)), lax.rem(x, jnp.int32(k))


def at(unit, index, size=None):
    return pl.ds(pl.multiple_of(index * unit, unit), unit if size is None else size)


def run(kernel, outs, smem, *arrays, scratch=(), flops=0, limit=40 << 20):
    shapes = [jax.ShapeDtypeStruct(s, d) for s, d in outs]
    moved = sum(a.size * a.dtype.itemsize for a in arrays)
    moved += sum(math.prod(s) * jnp.dtype(d).itemsize for s, d in outs)
    return pl.pallas_call(
        kernel,
        out_shape=shapes,
        in_specs=[pl.BlockSpec(memory_space=pltpu.SMEM)] * len(smem)
        + [pl.BlockSpec(memory_space=pltpu.VMEM)] * len(arrays),
        out_specs=[pl.BlockSpec(memory_space=pltpu.VMEM)] * len(outs),
        scratch_shapes=list(scratch),
        compiler_params=pltpu.CompilerParams(vmem_limit_bytes=limit),
        cost_estimate=pl.CostEstimate(flops=flops, bytes_accessed=moved, transcendentals=0),
    )(*smem, *arrays)


def shards(
    images,
    extents,
    first_reduce,
    first_taps,
    first_expand,
    first_shortcut,
    second_reduce,
    second_taps,
    second_expand,
    mid_gains,
    mid_shifts,
    wide_gains,
    wide_shifts,
    cotangent,
):
    nb = lax.axis_size("batch")
    ni = lax.axis_size("inner")
    no = lax.axis_size("outer")
    b = lax.axis_index("batch")
    i = lax.axis_index("inner")
    o = lax.axis_index("outer")
    c = b % 2
    img_dev, hi, wi, in_part = images.shape
    ho, wo = hi // 2, wi // 2
    out_part = cotangent.shape[3]
    m = img_dev // no
    pair = 2 * m
    cin, cout = hi * wi, ho * wo
    rin, rout = pair * cin, pair * cout
    mid = mid_gains.shape[1]
    mh = mid // 2
    in_h = in_part // 2
    out_h = out_part // 2
    kin = no * in_h
    wide = no * out_h
    mid_i = mid // ni
    mid_io = mid // (ni * no)
    peers = ni * no
    lanes = out_h

    def core_swap(x):
        return lax.ppermute(x, "batch", [(k, k ^ 1) for k in range(nb)])

    def pick(low, high):
        return jnp.where(c == 0, low, high)

    def mine(x, axis):
        h = x.shape[axis] // 2
        return pick(lax.slice_in_dim(x, 0, h, axis=axis), lax.slice_in_dim(x, h, 2 * h, axis=axis))

    def other(x, axis):
        h = x.shape[axis] // 2
        return pick(lax.slice_in_dim(x, h, 2 * h, axis=axis), lax.slice_in_dim(x, 0, h, axis=axis))

    def swap_full(x, axis):
        recv = core_swap(x)
        return pick(jnp.concatenate([x, recv], axis), jnp.concatenate([recv, x], axis))

    def over_batch(x):
        total = x
        for k in range(1, nb // 2):
            total = total + lax.ppermute(x, "batch", [(j, (j + 2 * k) % nb) for j in range(nb)])
        return total

    def sync(copies):
        got = lax.all_to_all(copies, ("inner", "outer"), split_axis=0, concat_axis=0, tiled=True)
        return got if nb == 2 else over_batch(jnp.sum(got, 0, keepdims=True))

    def to_images(x):
        return lax.all_to_all(x, "outer", split_axis=0, concat_axis=0, tiled=True)

    def taps_entries(first, w):
        def entry(tap):
            place = lambda pi, po: (pi * no + po, mid_io, 0, tap, mh)
            return (first + tap * mid_io, mid_io, 0, mh, w, place)

        return [entry(tap) for tap in range(9)], 9 * mid_io

    def up_entries(first, w):
        place = lambda pi, po: (pi, mid_i, 0, po, out_h)
        return [(first, mid_i, 0, out_h, w, place)], mid_i

    def short_entries(first, w):
        place = lambda pi, po: (po, in_part, 0, pi, out_h)
        return [(first, in_part, 0, out_h, w, place)], in_part

    def down_entries(rows):
        def make(first, w):
            half = rows // 2

            def entry(side):
                place = lambda pi, po: (po, rows, side * half, pi, mid_i)
                return (first, half, side * mid_i, mid_i, w, place)

            return [entry(0), entry(1)], half

        return make

    def table(makers):
        entries, first = [], 0
        for w, make in enumerate(makers):
            got, used = make(first, w)
            entries += got
            first += used
        return entries, first

    def cuts(entries, lo, hi_row):
        for first, count, lane, width, w, place in entries:
            a, z = max(lo, first), min(hi_row, first + count)
            if a < z:
                yield a, z, a - first, lane, width, w, place

    def spans(rows):
        h = rows // 2
        return [(0, 0, rows), (1, 0, rows), (2, 0, rows), (FAR, 0, h), (FAR, h, rows)]

    def region(place, pi, po, offset, count, width):
        row, row_unit, plus, col, col_unit = place(pi, po)
        return (
            pl.ds(pl.multiple_of(row * row_unit, row_unit) + (plus + offset), count),
            pl.ds(pl.multiple_of(col * col_unit, col_unit), width),
        )

    place_io = jnp.stack([i, o]).astype(jnp.int32)

    def gather(shard, makers, shapes):
        entries, rows = table(makers)
        ring = [(k, (k + 1) % no) for k in range(no)]
        pieces = [shard]
        for _ in range(1, no):
            pieces.append(lax.ppermute(pieces[-1], "outer", ring))
        whole = jnp.stack(pieces)
        h = rows // 2
        by_x = lax.ppermute(whole, "inner", XS)
        by_y = lax.ppermute(whole, "inner", YS)
        low = lax.ppermute(by_x[:, :h], "inner", YS)
        high = lax.ppermute(by_y[:, h:], "inner", XS)

        def kernel(where, *refs):
            sources, targets = refs[:5], refs[5:]
            for src, (far, lo, hi_row) in enumerate(spans(rows)):
                for d in range(no):
                    pi, po = where[0] ^ far, lax.rem(where[1] + (no - d), no)
                    for a, z, offset, lane, width, w, place in cuts(entries, lo, hi_row):
                        targets[w][region(place, pi, po, offset, z - a, width)] = sources[src][
                            d, a - lo : z - lo, lane : lane + width
                        ]

        return run(
            kernel, [(s, BF16) for s in shapes], [place_io], whole, by_x, by_y, low, high
        )

    def blocks_of(products, makers, operands):
        entries, rows = table(makers)
        h = rows // 2
        shapes = [prod[0] for prod in products]

        def kernel(where, *refs):
            ins, outs = refs[: len(operands)], refs[len(operands) : len(operands) + 5]
            grads = refs[len(operands) + 5 :]
            for grad, (shape, left, right) in zip(grads, products, strict=True):
                grad[...] = mm_tn(ins[left][...], ins[right][...]).astype(BF16)
            for dst, (far, lo, hi_row) in enumerate(spans(rows)):
                for po in range(no):
                    pi = where[0] ^ far
                    for a, z, offset, lane, width, w, place in cuts(entries, lo, hi_row):
                        outs[dst][po, a - lo : z - lo, lane : lane + width] = grads[w][
                            region(place, pi, po, offset, z - a, width)
                        ]

        sizes = [rows, rows, rows, h, rows - h]
        return run(
            kernel,
            [((no, r, lanes), BF16) for r in sizes],
            [place_io],
            *operands,
            scratch=[pltpu.VMEM(s, BF16) for s in shapes],
        )

    def scatter(own, to_x, to_y, low, high):
        h = low.shape[1]
        got_low = lax.ppermute(low, "inner", XS)
        got_high = lax.ppermute(high, "inner", YS)

        def first(x, y, a, z, out_x, out_y):
            out_x[:, :h] = x[:, :h]
            out_x[:, h:] = (x[:, h:].astype(F32) + z[...].astype(F32)).astype(BF16)
            out_y[:, :h] = (y[:, :h].astype(F32) + a[...].astype(F32)).astype(BF16)
            out_y[:, h:] = y[:, h:]

        to_x, to_y = run(first, [(own.shape, BF16)] * 2, [], to_x, to_y, got_low, got_high)
        by_x = lax.ppermute(to_x, "inner", XS)
        by_y = lax.ppermute(to_y, "inner", YS)

        def second(x, y, z, out):
            out[...] = (
                x[...].astype(F32) + y[...].astype(F32) + z[...].astype(F32)
            ).astype(BF16)

        (summed,) = run(second, [(own.shape, BF16)], [], own, by_x, by_y)
        parts = to_images(summed)
        return over_batch(jnp.sum(parts.astype(F32), axis=0))

    first_img = ((b - c) * ni + i) * img_dev + o * m
    ext = jnp.concatenate(
        [
            lax.dynamic_slice_in_dim(extents, first_img, m, 0),
            lax.dynamic_slice_in_dim(extents, first_img + ni * img_dev, m, 0),
        ],
        0,
    )
    geo = jnp.concatenate([jnp.stack([i, o, c]), ext[:, 0], ext[:, 1]]).astype(jnp.int32)
    area = jnp.sum(extents[:, 0] * extents[:, 1]).astype(F32)
    counts = jnp.stack([4.0 * area, area])

    def iota(shape, axis):
        return lax.broadcasted_iota(jnp.int32, shape, axis)

    def out_mask(geo):
        row, col = halves(iota((cout, 1), 0), wo)
        return jnp.concatenate(
            [
                ((row < geo[GEO + k]) & (col < geo[GEO + pair + k])).astype(F32)
                for k in range(pair)
            ],
            0,
        )

    def phase_cells(shape, axis):
        phase, cell = halves(iota(shape, axis), cout)
        row, col = halves(cell, wo)
        up, left = halves(phase, 2)
        return 2 * row + up, 2 * col + left

    def in_mask(geo):
        row, col = phase_cells((cin, 1), 0)
        return jnp.concatenate(
            [
                ((row < 2 * geo[GEO + k]) & (col < 2 * geo[GEO + pair + k])).astype(F32)
                for k in range(pair)
            ],
            0,
        )

    def order(geo, k, axis):
        shape = (cin, 1) if axis == 0 else (1, cin)
        row, col = phase_cells(shape, axis)
        inside = (row < 2 * geo[GEO + k]) & (col < 2 * geo[GEO + pair + k])
        source = jnp.where(inside, row * wi + col, -1)
        return (source == iota((cin, cin), 1 - axis)).astype(F32).astype(BF16)

    def shift(dr, dc):
        row, col = halves(iota((cout, 1), 0), wo)
        row, col = row + dr, col + dc
        inside = (row >= 0) & (row < ho) & (col >= 0) & (col < wo)
        source = jnp.where(inside, row * wo + col, -1)
        return (source == iota((cout, cout), 1)).astype(F32).astype(BF16)

    def taps_shard(w):
        return mine(w, 2).transpose(0, 1, 3, 2).reshape(9 * mid_io, mh)

    def side_by_side(w):
        h = w.shape[0] // 2
        return jnp.concatenate([w[:h], w[h:]], 1)

    got_in = to_images(images.reshape(img_dev, cin, in_part)).reshape(no, m, cin, in_part)
    make_r1, make_r2 = down_entries(in_h), down_entries(out_h)
    shape_t = (mid, 9 * mh)
    (w_r1,) = gather(side_by_side(mine(first_reduce, 0)), [make_r1], [(kin, mid)])
    (w_t1,) = gather(taps_shard(first_taps), [taps_entries], [shape_t])
    w_e1, w_s = gather(
        jnp.concatenate([mine(first_expand, 1), mine(first_shortcut, 1)], 0),
        [up_entries, short_entries],
        [(mid, wide), (no * in_part, wide)],
    )
    w_r2, w_t2, w_e2 = gather(
        jnp.concatenate(
            [
                side_by_side(mine(second_reduce, 0)),
                taps_shard(second_taps),
                mine(second_expand, 1),
            ],
            0,
        ),
        [make_r2, taps_entries, up_entries],
        [(wide, mid), shape_t, (mid, wide)],
    )

    pm = mine(jnp.concatenate([mid_gains, mid_shifts], 0), 1)
    pw = mine(
        jnp.concatenate([wide_gains, wide_shifts], 0).reshape(6, no, out_part), 2
    ).reshape(6, wide)

    def moments(got, counts, which, row=0):
        total = jnp.sum(got[...], 0)
        mean = total[row : row + 1] / counts[which]
        square = total[row + 1 : row + 2] / counts[which]
        return mean, lax.rsqrt(square - mean * mean + EPS)

    def send_all(copies, rows):
        value = jnp.concatenate(rows, 0)
        for k in range(peers):
            copies[k] = value

    def sums(z, valid=None):
        zv = z if valid is None else z * valid
        return [jnp.sum(zv, 0, keepdims=True), jnp.sum(zv * z, 0, keepdims=True)]

    def copies_shape(rows, width):
        return ((peers, rows, width), F32)

    mid_f = ((rout, mh), F32)
    wide_f = ((rout, wide), F32)
    wide_b = ((rout, wide), BF16)
    mid_b = ((rout, mh), BF16)

    swap_in = core_swap(other(got_in, 3))

    def one_kernel(geo, got, recv, w, masked, own, oth, raw):
        me = geo[2]
        for k in range(m):
            for j in range(no):
                at_lane = slice(j * in_h, (j + 1) * in_h)
                raw[me * m + k, :, at_lane] = got[j, k, :, at(in_h, me)]
                raw[(1 - me) * m + k, :, at_lane] = recv[j, k]
        for k in range(pair):
            rows = slice(k * cin, (k + 1) * cin)
            masked[rows, :] = mm(order(geo, k, 0), raw[k]).astype(BF16)
        own[...] = mm(masked[...], w[:, at(mh, me)])
        oth[...] = mm(masked[...], w[:, at(mh, 1 - me)])

    masked, z_own, z_oth = run(
        one_kernel,
        [((rin, kin), BF16), ((rin, mh), F32), ((rin, mh), F32)],
        [geo],
        got_in,
        swap_in,
        w_r1,
        scratch=[pltpu.VMEM((pair, cin, kin), BF16)],
    )

    def one_sums(x, y, z, copies):
        z[...] = x[...] + y[...]
        send_all(copies, sums(z[...]))

    z_one, copies = run(
        one_sums, [((rin, mh), F32), copies_shape(2, mh)], [], z_own, core_swap(z_oth)
    )
    got_one = sync(copies)

    def mid_sums(geo, x, y, z, copies):
        z[...] = x[...] + y[...]
        send_all(copies, sums(z[...], out_mask(geo)))

    def mid_partial(kernel, z, got, w):
        win, own, oth = run(
            kernel,
            [((rout, 9 * mh), BF16), mid_f, mid_f],
            [geo, counts],
            z,
            got,
            pm,
            w,
            scratch=[pltpu.VMEM(z.shape, BF16)],
        )
        z_next, copies = run(
            mid_sums, [mid_f, copies_shape(2, mh)], [geo], own, core_swap(oth)
        )
        return win, z_next, sync(copies)

    def normed(z, st, gains, g, s):
        return (z - st[0]) * st[1] * gains[g : g + 1] + gains[s : s + 1]

    def two_kernel(geo, counts, z, got, pm, w, win, own, oth, act):
        st = moments(got, counts, 0)
        act[...] = (gelu(normed(z[...], st, pm, 0, 4)) * in_mask(geo)).astype(BF16)
        moves = {}
        for tap, (p, r) in enumerate(TAPS):
            key = (-int(p == 0), -int(r == 0))
            plane = 2 * int(p != 1) + int(r != 1)
            if key != (0, 0) and key not in moves:
                moves[key] = shift(*key)
            for k in range(pair):
                x = act[k * cin + plane * cout : k * cin + (plane + 1) * cout, :]
                if key != (0, 0):
                    x = mm(moves[key], x).astype(BF16)
                win[k * cout : (k + 1) * cout, tap * mh : (tap + 1) * mh] = x
        own[...] = mm_nt(win[...], w[at(mh, geo[2]), :])
        oth[...] = mm_nt(win[...], w[at(mh, 1 - geo[2]), :])

    win_one, z_two, got_two = mid_partial(two_kernel, z_one, got_one, w_t1)

    strided_h = masked.reshape(pair, cin, kin)[:, :cout].reshape(rout, kin)
    strided_r = core_swap(strided_h)

    def short_kernel(geo, x, y, w, full, z):
        me = geo[2]
        for j in range(no):
            part = slice(j * in_h, (j + 1) * in_h)
            full[:, pl.ds(pl.multiple_of(j * in_part + me * in_h, in_h), in_h)] = x[:, part]
            full[:, pl.ds(pl.multiple_of(j * in_part + (1 - me) * in_h, in_h), in_h)] = y[:, part]
        z[...] = mm(full[...], w[...])

    strided, z_short = run(
        short_kernel, [((rout, no * in_part), BF16), wide_f], [geo], strided_h, strided_r, w_s
    )

    def act_of(row, z, got):
        def kernel(geo, counts, z, got, pm, act):
            st = moments(got, counts, 1)
            act[...] = (gelu(normed(z[...], st, pm, row, row + 4)) * out_mask(geo)).astype(BF16)

        (act,) = run(kernel, [mid_b], [geo, counts], z, got, pm)
        return act, core_swap(act)

    def join_to(full, geo, x, y):
        full[:, at(mh, geo[2])] = x[...]
        full[:, at(mh, 1 - geo[2])] = y[...]

    def three_kernel(geo, x, y, w, zs, full, z, copies):
        join_to(full, geo, x, y)
        z[...] = mm(full[...], w[...])
        send_all(copies, sums(z[...]) + sums(zs[...]))

    act_own, act_recv = act_of(1, z_two, got_two)
    act_two, z_three, copies = run(
        three_kernel,
        [((rout, mid), BF16), wide_f, copies_shape(4, wide)],
        [geo],
        act_own,
        act_recv,
        w_e1,
        z_short,
    )
    got_three = sync(copies)

    def four_kernel(geo, counts, z3, zs, got, pw, w, hidden, slope, low, own, oth):
        st3, sts = moments(got, counts, 1), moments(got, counts, 1, 2)
        joined = normed(z3[...], st3, pw, 0, 3) + normed(zs[...], sts, pw, 1, 4)
        value, rise = gelu_both(joined)
        valid = out_mask(geo)
        hidden[...] = value * valid
        slope[...] = rise * valid
        low[...] = hidden[...].astype(BF16)
        own[...] = mm(low[...], w[:, at(mh, geo[2])])
        oth[...] = mm(low[...], w[:, at(mh, 1 - geo[2])])

    hidden, slope_one, hidden_low, z_own, z_oth = run(
        four_kernel,
        [wide_f, wide_f, wide_b, mid_f, mid_f],
        [geo, counts],
        z_three,
        z_short,
        got_three,
        pw,
        w_r2,
    )
    z_four, copies = run(
        mid_sums, [mid_f, copies_shape(2, mh)], [geo], z_own, core_swap(z_oth)
    )
    got_four = sync(copies)

    def five_kernel(geo, counts, z, got, pm, w, win, own, oth, act):
        st = moments(got, counts, 1)
        act[...] = (gelu(normed(z[...], st, pm, 2, 6)) * out_mask(geo)).astype(BF16)
        for tap, (p, r) in enumerate(TAPS):
            key = (p - 1, r - 1)
            move = None if key == (0, 0) else shift(*key)
            for k in range(pair):
                x = act[k * cout : (k + 1) * cout, :]
                if move is not None:
                    x = mm(move, x).astype(BF16)
                win[k * cout : (k + 1) * cout, tap * mh : (tap + 1) * mh] = x
        own[...] = mm_nt(win[...], w[at(mh, geo[2]), :])
        oth[...] = mm_nt(win[...], w[at(mh, 1 - geo[2]), :])

    win_two, z_five, got_five = mid_partial(five_kernel, z_four, got_four, w_t2)
    act_own, act_recv = act_of(3, z_five, got_five)

    def six_kernel(geo, x, y, w, full, z, copies):
        join_to(full, geo, x, y)
        z[...] = mm(full[...], w[...])
        send_all(copies, sums(z[...]))

    act_five, z_six, copies = run(
        six_kernel,
        [((rout, mid), BF16), wide_f, copies_shape(2, wide)],
        [geo],
        act_own,
        act_recv,
        w_e2,
    )
    got_six = sync(copies)

    got_cot = to_images(cotangent.reshape(img_dev, cout, out_part)).reshape(
        no, m, cout, out_part
    )
    swap_cot = core_swap(other(got_cot, 3))

    def loss_kernel(geo, counts, z, got, pw, hidden, cot, recv, own, oth, dy, copies, value):
        me = geo[2]
        st = moments(got, counts, 1)
        xhat = (z[...] - st[0]) * st[1]
        out, rise = gelu_both(xhat * pw[2:3] + pw[5:6] + hidden[...])
        valid = out_mask(geo)
        value[...] = (out * valid).astype(BF16)
        own[...] = value[at(m * cout, me), :]
        oth[...] = value[at(m * cout, 1 - me), :]
        for k in range(m):
            for j in range(no):
                part = slice(j * out_h, (j + 1) * out_h)
                dy[at(cout, me * m + k), part] = cot[j, k, :, at(out_h, me)].astype(F32)
                dy[at(cout, (1 - me) * m + k), part] = recv[j, k].astype(F32)
        dy[...] = dy[...] * (rise * valid)
        send_all(copies, dy_sums(dy[...], xhat))

    def dy_sums(dy, *xhats):
        return [jnp.sum(dy, 0, keepdims=True)] + [
            jnp.sum(dy * x, 0, keepdims=True) for x in xhats
        ]

    out_own, out_oth, dy_six, copies = run(
        loss_kernel,
        [((m * cout, wide), BF16), ((m * cout, wide), BF16), wide_f, copies_shape(2, wide)],
        [geo, counts],
        z_six,
        got_six,
        pw,
        hidden,
        got_cot,
        swap_cot,
        scratch=[pltpu.VMEM((rout, wide), BF16)],
    )
    got_g6 = sync(copies)

    def home(own, recv, cells, part_h):
        def kernel(geo, x, y, out):
            for k in range(m):
                rows = slice(k * cells, (k + 1) * cells)
                for j in range(no):
                    part = slice(j * part_h, (j + 1) * part_h)
                    out[j, k, :, at(part_h, geo[2])] = x[rows, part]
                    out[j, k, :, at(part_h, 1 - geo[2])] = y[rows, part]

        (full,) = run(kernel, [((no, m, cells, 2 * part_h), BF16)], [geo], own, recv)
        return to_images(full.reshape(img_dev, cells, 2 * part_h))

    block_output = home(out_own, core_swap(out_oth), cout, out_h).reshape(
        img_dev, ho, wo, out_part
    )

    def back(dy, xhat, gain, st, valid, total, row, shift_row, count):
        shift_sum, gain_sum = total[shift_row : shift_row + 1], total[row : row + 1]
        return (
            gain * st[1] * (dy - valid * ((shift_sum + xhat * gain_sum) / count))
        ).astype(BF16)

    def back_six(geo, counts, dy, z, got, grads, pw, w, dz, own, oth, total):
        st = moments(got, counts, 1)
        total[...] = jnp.sum(grads[...], 0)
        xhat = (z[...] - st[0]) * st[1]
        dz[...] = back(dy[...], xhat, pw[2:3], st, out_mask(geo), total, 1, 0, counts[1])
        own[...] = mm_nt(dz[...], w[at(mh, geo[2]), :])
        oth[...] = mm_nt(dz[...], w[at(mh, 1 - geo[2]), :])

    dz_six, da_own, da_oth, sum_six = run(
        back_six,
        [wide_b, mid_f, mid_f, ((2, wide), F32)],
        [geo, counts],
        dy_six,
        z_six,
        got_six,
        got_g6,
        pw,
        w_e2,
    )

    def mid_dy(row, own, recv, z, got):
        def kernel(geo, counts, x, y, z, got, pm, dy, copies):
            st = moments(got, counts, 1)
            xhat = (z[...] - st[0]) * st[1]
            rise = gelu_slope(xhat * pm[row : row + 1] + pm[row + 4 : row + 5])
            dy[...] = (x[...] + y[...]) * (out_mask(geo) * rise)
            send_all(copies, dy_sums(dy[...], xhat))

        dy, copies = run(
            kernel, [mid_f, copies_shape(2, mh)], [geo, counts], own, recv, z, got, pm
        )
        return dy, sync(copies)

    def mid_dz(row, dy, z, got, grads):
        which = 0 if row == 0 else 1

        def kernel(geo, counts, dy, z, got, grads, pm, dz, total):
            st = moments(got, counts, which)
            total[...] = jnp.sum(grads[...], 0)
            xhat = (z[...] - st[0]) * st[1]
            valid = in_mask(geo) if row == 0 else out_mask(geo)
            dz[...] = back(
                dy[...], xhat, pm[row : row + 1], st, valid, total, 1, 0, counts[which]
            )

        dz, total = run(
            kernel, [(z.shape, BF16), ((2, mh), F32)], [geo, counts], dy, z, got, grads, pm
        )
        return dz, core_swap(dz), total

    dy_five, got_g5 = mid_dy(3, da_own, core_swap(da_oth), z_five, got_five)
    dz_own, dz_recv, sum_five = mid_dz(3, dy_five, z_five, got_five, got_g5)

    def four_dy(geo, counts, x, y, z, got, pm, w, full, dy, copies, moved):
        join_to(full, geo, x, y)
        total = None
        for tap, (p, r) in enumerate(TAPS):
            key = (1 - p, 1 - r)
            if key == (0, 0):
                left = full[...]
            else:
                move = shift(*key)
                for k in range(pair):
                    rows = slice(k * cout, (k + 1) * cout)
                    moved[rows, :] = mm(move, full[rows, :]).astype(BF16)
                left = moved[...]
            term = mm(left, w[:, tap * mh : (tap + 1) * mh])
            total = term if total is None else total + term
        st = moments(got, counts, 1)
        xhat = (z[...] - st[0]) * st[1]
        dy[...] = total * (out_mask(geo) * gelu_slope(xhat * pm[2:3] + pm[6:7]))
        send_all(copies, dy_sums(dy[...], xhat))

    dz_five, dy_four, copies = run(
        four_dy,
        [((rout, mid), BF16), mid_f, copies_shape(2, mh)],
        [geo, counts],
        dz_own,
        dz_recv,
        z_four,
        got_four,
        pm,
        w_t2,
        scratch=[pltpu.VMEM((rout, mid), BF16)],
    )
    got_g4 = sync(copies)
    dz_own, dz_recv, sum_four = mid_dz(2, dy_four, z_four, got_four, got_g4)

    def joined_dy(geo, counts, x, y, w, dy6, slope, z3, zs, got, full, dy, copies):
        join_to(full, geo, x, y)
        dy[...] = (dy6[...] + mm_nt(full[...], w[...])) * slope[...]
        st3, sts = moments(got, counts, 1), moments(got, counts, 1, 2)
        send_all(
            copies,
            dy_sums(dy[...], (z3[...] - st3[0]) * st3[1], (zs[...] - sts[0]) * sts[1]),
        )

    dz_four, dy_joined, copies = run(
        joined_dy,
        [((rout, mid), BF16), wide_f, copies_shape(3, wide)],
        [geo, counts],
        dz_own,
        dz_recv,
        w_r2,
        dy_six,
        slope_one,
        z_three,
        z_short,
        got_three,
    )
    got_g3 = sync(copies)
    grads_second = scatter(
        *blocks_of(
            [((wide, mid), 0, 1), (shape_t, 2, 3), ((mid, wide), 4, 5)],
            [make_r2, taps_entries, up_entries],
            [hidden_low, dz_four, dz_five, win_two, act_five, dz_six],
        )
    )

    def back_three(geo, counts, dy, z3, zs, got, grads, pw, w, dz3, dzs, own, oth, total):
        st3, sts = moments(got, counts, 1), moments(got, counts, 1, 2)
        total[...] = jnp.sum(grads[...], 0)
        valid = out_mask(geo)
        x3, xs = (z3[...] - st3[0]) * st3[1], (zs[...] - sts[0]) * sts[1]
        dz3[...] = back(dy[...], x3, pw[0:1], st3, valid, total, 1, 0, counts[1])
        dzs[...] = back(dy[...], xs, pw[1:2], sts, valid, total, 2, 0, counts[1])
        own[...] = mm_nt(dz3[...], w[at(mh, geo[2]), :])
        oth[...] = mm_nt(dz3[...], w[at(mh, 1 - geo[2]), :])

    dz_three, dz_short, da_own, da_oth, sum_three = run(
        back_three,
        [wide_b, wide_b, mid_f, mid_f, ((3, wide), F32)],
        [geo, counts],
        dy_joined,
        z_three,
        z_short,
        got_three,
        got_g3,
        pw,
        w_e1,
    )
    dy_two, got_g2 = mid_dy(1, da_own, core_swap(da_oth), z_two, got_two)
    grads_es = scatter(
        *blocks_of(
            [((mid, wide), 0, 1), ((no * in_part, wide), 2, 3)],
            [up_entries, short_entries],
            [act_two, dz_three, strided, dz_short],
        )
    )

    def short_back(geo, dz, w, own, oth):
        me = geo[2]
        for j in range(no):
            part = slice(j * in_h, (j + 1) * in_h)
            rows = pl.ds(pl.multiple_of(j * in_part + me * in_h, in_h), in_h)
            own[:, part] = mm_nt(dz[...], w[rows, :])
            rows = pl.ds(pl.multiple_of(j * in_part + (1 - me) * in_h, in_h), in_h)
            oth[:, part] = mm_nt(dz[...], w[rows, :])

    ds_own, ds_oth = run(short_back, [((rout, kin), F32)] * 2, [geo], dz_short, w_s)
    ds_recv = core_swap(ds_oth)
    dz_own, dz_recv, sum_two = mid_dz(1, dy_two, z_two, got_two, got_g2)

    def one_dy(geo, counts, x, y, z, got, pm, w, full, dy, copies, moved):
        join_to(full, geo, x, y)
        for n, key in enumerate([(0, 1), (1, 0), (1, 1)]):
            move = shift(*key)
            for k in range(pair):
                rows = slice(k * cout, (k + 1) * cout)
                moved[n, rows, :] = mm(move, full[rows, :]).astype(BF16)
        for plane in range(4):
            total = None
            for p in (1,) if plane < 2 else (0, 2):
                for r in (1,) if plane % 2 == 0 else (0, 2):
                    n = 2 * int(p == 0) + int(r == 0)
                    left = full[...] if n == 0 else moved[n - 1]
                    tap = 3 * p + r
                    term = mm(left, w[:, tap * mh : (tap + 1) * mh])
                    total = term if total is None else total + term
            for k in range(pair):
                dy[k * cin + plane * cout : k * cin + (plane + 1) * cout, :] = total[
                    k * cout : (k + 1) * cout
                ]
        st = moments(got, counts, 0)
        xhat = (z[...] - st[0]) * st[1]
        dy[...] = dy[...] * (in_mask(geo) * gelu_slope(xhat * pm[0:1] + pm[4:5]))
        send_all(copies, dy_sums(dy[...], xhat))

    dz_two, dy_one, copies = run(
        one_dy,
        [((rout, mid), BF16), ((rin, mh), F32), copies_shape(2, mh)],
        [geo, counts],
        dz_own,
        dz_recv,
        z_one,
        got_one,
        pm,
        w_t1,
        scratch=[pltpu.VMEM((3, rout, mid), BF16)],
    )
    got_g1 = sync(copies)
    grads_t1 = scatter(*blocks_of([(shape_t, 0, 1)], [taps_entries], [dz_two, win_one]))
    dz_own, dz_recv, sum_one = mid_dz(0, dy_one, z_one, got_one, got_g1)

    def images_kernel(geo, x, y, w, ds, dr, full, own, oth, rows_in):
        join_to(full, geo, x, y)
        me = geo[2]
        for k in range(pair):
            rows = slice(k * cin, (k + 1) * cin)
            first = slice(k * cin, k * cin + cout)
            rest = slice(k * cin + cout, (k + 1) * cin)
            outs = slice(k * cout, (k + 1) * cout)
            rows_in[first, :] = (
                mm_nt(full[first, :], w[...]) + (ds[outs, :] + dr[outs, :])
            ).astype(BF16)
            rows_in[rest, :] = mm_nt(full[rest, :], w[...]).astype(BF16)
        for k in range(m):
            rows = slice(k * cin, (k + 1) * cin)
            for ref, img in ((oth, (1 - me) * m + k), (own, me * m + k)):
                ref[rows, :] = mm(order(geo, img, 1), rows_in[at(cin, img), :]).astype(BF16)

    dz_one, d_own, d_oth = run(
        images_kernel,
        [((rin, mid), BF16), ((m * cin, kin), BF16), ((m * cin, kin), BF16)],
        [geo],
        dz_own,
        dz_recv,
        w_r1,
        ds_own,
        ds_recv,
        scratch=[pltpu.VMEM((rin, kin), BF16)],
    )
    grad_images = home(d_own, core_swap(d_oth), cin, in_h).astype(F32).reshape(images.shape)
    grads_r1 = scatter(*blocks_of([((kin, mid), 0, 1)], [make_r1], [masked, dz_one]))

    def stacked(x):
        w = x.shape[1] // 2
        return jnp.concatenate([x[:, :w], x[:, w:]], 0)

    def taps_out(rows):
        both = swap_full(rows.reshape(9, mid_io, mh), 2)
        return both.transpose(0, 2, 1).reshape(first_taps.shape)

    rows_r2, rows_t = out_h // 2, 9 * mid_io
    grad_e1_s = swap_full(grads_es, 1)
    mids = jnp.stack([sum_one, sum_two, sum_four, sum_five], 1)
    mids = swap_full(mids, 2)
    wides = jnp.concatenate([sum_three, sum_six], 0).reshape(5, no, out_h)
    wides = swap_full(wides, 2).reshape(5, no * out_part)
    return (
        block_output,
        grad_images,
        swap_full(stacked(grads_r1), 0),
        taps_out(grads_t1),
        grad_e1_s[:mid_i],
        grad_e1_s[mid_i:],
        swap_full(stacked(grads_second[:rows_r2]), 0),
        taps_out(grads_second[rows_r2 : rows_r2 + rows_t]),
        swap_full(grads_second[rows_r2 + rows_t :], 1),
        mids[1],
        mids[0],
        jnp.stack([wides[1], wides[2], wides[4]]),
        jnp.stack([wides[0], wides[0], wides[3]]),
    )


def solution(mesh):
    wide = P(("batch", "inner"), None, None, "outer")
    down = P("outer", "inner")
    up = P("inner", "outer")
    taps = P(None, None, None, ("inner", "outer"))
    whole = P()
    return jax.shard_map(
        shards,
        mesh=mesh,
        in_specs=(wide, whole, down, taps, up, down, down, taps, up)
        + (whole, whole, whole, whole, wide),
        out_specs=(wide, wide, down, taps, up, down, down, taps, up, whole, whole, whole, whole),
        check_vma=False,
    )
```

```python
import math

import jax
import jax.numpy as jnp
from jax import lax
from jax.experimental import pallas as pl
from jax.experimental.pallas import tpu as pltpu
from jax.sharding import PartitionSpec as P

EPS = 1e-05
ROOT = math.sqrt(2.0 / math.pi)
CUBE = 0.044715
F32 = jnp.float32
BF16 = jnp.bfloat16
XS = [(k, k ^ 1) for k in range(4)]
YS = [(k, k ^ 2) for k in range(4)]
DS = [(k, k ^ 3) for k in range(4)]
FAR = 3
GEO = 3
TAPS = [(p, r) for p in range(3) for r in range(3)]


def mm(left, right):
    return lax.dot_general(left, right, (((1,), (0,)), ((), ())), preferred_element_type=F32)


def mm_nt(left, right):
    return lax.dot_general(left, right, (((1,), (1,)), ((), ())), preferred_element_type=F32)


def mm_tn(left, right):
    return lax.dot_general(left, right, (((0,), (0,)), ((), ())), preferred_element_type=F32)


def gelu(v):
    return 0.5 * v * (1.0 + jnp.tanh(ROOT * (v + CUBE * v * v * v)))


def gelu_both(v):
    t = jnp.tanh(ROOT * (v + CUBE * v * v * v))
    half = 0.5 * (1.0 + t)
    return v * half, half + 0.5 * v * (1.0 - t * t) * (ROOT * (1.0 + 3.0 * CUBE * v * v))


def gelu_slope(v):
    return gelu_both(v)[1]


def halves(x, k):
    if k & (k - 1) == 0:
        s = k.bit_length() - 1
        return lax.shift_right_logical(x, jnp.int32(s)), lax.bitwise_and(x, jnp.int32(k - 1))
    return lax.div(x, jnp.int32(k)), lax.rem(x, jnp.int32(k))


def at(unit, index, size=None):
    return pl.ds(pl.multiple_of(index * unit, unit), unit if size is None else size)


def after(x, *done):
    return lax.optimization_barrier((x, done))[0]


def together(*groups):
    flat = [x for g in groups for x in g]
    flat = list(lax.optimization_barrier(tuple(flat)))
    out = []
    for g in groups:
        out.append(flat[: len(g)])
        flat = flat[len(g) :]
    return out


def run(kernel, outs, smem, *arrays, scratch=(), flops=0, limit=20 << 20):
    shapes = [jax.ShapeDtypeStruct(s, d) for s, d in outs]
    moved = sum(a.size * a.dtype.itemsize for a in arrays)
    moved += sum(math.prod(s) * jnp.dtype(d).itemsize for s, d in outs)
    return pl.pallas_call(
        kernel,
        out_shape=shapes,
        in_specs=[pl.BlockSpec(memory_space=pltpu.SMEM)] * len(smem)
        + [pl.BlockSpec(memory_space=pltpu.VMEM)] * len(arrays),
        out_specs=[pl.BlockSpec(memory_space=pltpu.VMEM)] * len(outs),
        scratch_shapes=list(scratch),
        compiler_params=pltpu.CompilerParams(vmem_limit_bytes=limit),
        cost_estimate=pl.CostEstimate(flops=flops, bytes_accessed=moved, transcendentals=0),
    )(*smem, *arrays)


def shards(
    images,
    extents,
    first_reduce,
    first_taps,
    first_expand,
    first_shortcut,
    second_reduce,
    second_taps,
    second_expand,
    mid_gains,
    mid_shifts,
    wide_gains,
    wide_shifts,
    cotangent,
):
    nb = lax.axis_size("batch")
    ni = lax.axis_size("inner")
    no = lax.axis_size("outer")
    b = lax.axis_index("batch")
    i = lax.axis_index("inner")
    o = lax.axis_index("outer")
    c = b % 2
    img_dev, hi, wi, in_part = images.shape
    ho, wo = hi // 2, wi // 2
    out_part = cotangent.shape[3]
    m = img_dev // no
    pair = 2 * m
    cin, cout = hi * wi, ho * wo
    rin, rout = pair * cin, pair * cout
    mid = mid_gains.shape[1]
    mh = mid // 2
    in_h = in_part // 2
    out_h = out_part // 2
    kin = no * in_h
    wide = no * out_h
    mid_i = mid // ni
    mid_io = mid // (ni * no)
    peers = ni * no
    lanes = out_h

    def core_swap(x):
        return lax.ppermute(x, "batch", [(k, k ^ 1) for k in range(nb)])

    def pick(low, high):
        return jnp.where(c == 0, low, high)

    def mine(x, axis):
        h = x.shape[axis] // 2
        return pick(lax.slice_in_dim(x, 0, h, axis=axis), lax.slice_in_dim(x, h, 2 * h, axis=axis))

    def other(x, axis):
        h = x.shape[axis] // 2
        return pick(lax.slice_in_dim(x, h, 2 * h, axis=axis), lax.slice_in_dim(x, 0, h, axis=axis))

    def swap_full(x, axis):
        recv = core_swap(x)
        return pick(jnp.concatenate([x, recv], axis), jnp.concatenate([recv, x], axis))

    def over_batch(x):
        total = x
        for k in range(1, nb // 2):
            total = total + lax.ppermute(x, "batch", [(j, (j + 2 * k) % nb) for j in range(nb)])
        return total

    def sync(copies):
        got = lax.all_to_all(copies, ("inner", "outer"), split_axis=0, concat_axis=0, tiled=True)
        return got if nb == 2 else over_batch(jnp.sum(got, 0, keepdims=True))

    def to_images(x):
        return lax.all_to_all(x, "outer", split_axis=0, concat_axis=0, tiled=True)

    def taps_entries(first, w):
        def entry(tap):
            place = lambda pi, po: (pi * no + po, mid_io, 0, tap, mh)
            return (first + tap * mid_io, mid_io, 0, mh, w, place)

        return [entry(tap) for tap in range(9)], 9 * mid_io

    def up_entries(first, w):
        place = lambda pi, po: (pi, mid_i, 0, po, out_h)
        return [(first, mid_i, 0, out_h, w, place)], mid_i

    def short_entries(first, w):
        quarter = in_part // 4

        def entry(k):
            place = lambda pi, po: (po, in_part, k * quarter, pi, out_h)
            return (first + k * quarter, quarter, 0, out_h, w, place)

        return [entry(k) for k in range(4)], in_part

    def down_entries(rows):
        def make(first, w):
            half = rows // 2

            def entry(side):
                place = lambda pi, po: (po, rows, side * half, pi, mid_i)
                return (first, half, side * mid_i, mid_i, w, place)

            return [entry(0), entry(1)], half

        return make

    def table(makers):
        entries, first = [], 0
        for w, make in enumerate(makers):
            got, used = make(first, w)
            entries += got
            first += used
        return entries, first

    def middle(makers):
        entries, rows = table(makers)
        return min(first + count for first, count, *_ in entries if 2 * (first + count) >= rows)

    def region(place, pi, po, count, width):
        row, row_unit, plus, col, col_unit = place(pi, po)
        return (
            pl.ds(pl.multiple_of(row * row_unit, row_unit) + plus, count),
            pl.ds(pl.multiple_of(col * col_unit, col_unit), width),
        )

    place_io = jnp.stack([i, o]).astype(jnp.int32)

    def shifted(x, k):
        return lax.ppermute(x, "outer", [(j, (j + k) % no) for j in range(no)])

    def along_outer(shard):
        return [shard] + [shifted(shard, k) for k in range(1, no)]

    def along_inner(pieces):
        whole = jnp.stack(pieces)
        return [whole] + [lax.ppermute(whole, "inner", perm) for perm in (XS, YS, DS)]

    def along_near(pieces):
        whole = jnp.stack(pieces)
        return whole, lax.ppermute(whole, "inner", XS), lax.ppermute(whole, "inner", YS)

    def along_far(whole, by_x, by_y, h):
        low = lax.ppermute(by_x[:, :h], "inner", YS)
        high = lax.ppermute(by_y[:, h:], "inner", XS)
        return whole, by_x, by_y, low, high

    def assembled(parts, makers, shapes):
        entries, _ = table(makers)
        h = middle(makers)

        def kernel(where, *refs):
            sources, targets = refs[: len(parts)], refs[len(parts) :]
            for far in range(ni):
                for d in range(no):
                    pi, po = where[0] ^ far, lax.rem(where[1] + (no - d), no)
                    for first, count, lane, width, w, place in entries:
                        source, start = sources[far], first
                        if len(parts) > ni and far == FAR and first >= h:
                            source, start = sources[ni], first - h
                        targets[w][region(place, pi, po, count, width)] = source[
                            d, start : start + count, lane : lane + width
                        ]

        return run(kernel, [(s, BF16) for s in shapes], [place_io], *parts)

    def blocks_of(products, makers, operands, split=True):
        entries, rows = table(makers)
        h = middle(makers)
        sizes = [rows, rows, rows] + ([h, rows - h] if split else [rows])
        n = len(operands)

        def kernel(where, *refs):
            ins, outs, grads = refs[:n], refs[n : n + len(sizes)], refs[n + len(sizes) :]
            for grad, (_, left, right) in zip(grads, products, strict=True):
                grad[...] = mm_tn(ins[left][...], ins[right][...]).astype(BF16)
            for far in range(ni):
                for po in range(no):
                    pi = where[0] ^ far
                    for first, count, lane, width, w, place in entries:
                        out, start = outs[far], first
                        if split and far == FAR and first >= h:
                            out, start = outs[ni], first - h
                        out[po, start : start + count, lane : lane + width] = grads[w][
                            region(place, pi, po, count, width)
                        ]

        return run(
            kernel,
            [((no, r, lanes), BF16) for r in sizes],
            [place_io],
            *operands,
            scratch=[pltpu.VMEM(prod[0], BF16) for prod in products],
        )

    def scatter_far(own, to_x, to_y, low, high):
        return own, to_x, to_y, lax.ppermute(low, "inner", XS), lax.ppermute(high, "inner", YS)

    def scatter_add(own, to_x, to_y, low, high):
        h = low.shape[1]

        def kernel(x, y, a, z, out_x, out_y):
            out_x[:, :h] = x[:, :h]
            out_x[:, h:] = (x[:, h:].astype(F32) + z[...].astype(F32)).astype(BF16)
            out_y[:, :h] = (y[:, :h].astype(F32) + a[...].astype(F32)).astype(BF16)
            out_y[:, h:] = y[:, h:]

        return [own] + list(run(kernel, [(own.shape, BF16)] * 2, [], to_x, to_y, low, high))

    def scatter_near(own, to_x, to_y):
        return [own, lax.ppermute(to_x, "inner", XS), lax.ppermute(to_y, "inner", YS)]

    def scatter_inner(own, *sends):
        return [own] + [
            lax.ppermute(x, "inner", perm) for x, perm in zip(sends, (XS, YS, DS), strict=True)
        ]

    def scatter_sum(*got):
        def kernel(*refs):
            total = refs[0][...].astype(F32)
            for ref in refs[1:-1]:
                total = total + ref[...].astype(F32)
            refs[-1][...] = total.astype(BF16)

        return run(kernel, [(got[0].shape, BF16)], [], *got)[0]

    def scatter_sends(own, by_x, by_y):
        shape = own.shape[1:]

        def kernel(where, x, y, z, *outs):
            for k, out in enumerate(outs):
                j = lax.rem(where[1] + k, no)
                total = x[j].astype(F32) + y[j].astype(F32) + z[j].astype(F32)
                out[...] = total.astype(BF16)

        sends = run(kernel, [(shape, BF16)] * no, [place_io], own, by_x, by_y)
        return [sends[0]] + [shifted(sends[k], k) for k in range(1, no)]

    def scatter_last(parts):
        return over_batch(jnp.sum(parts.astype(F32), axis=0))

    first_img = ((b - c) * ni + i) * img_dev + o * m
    ext = jnp.concatenate(
        [
            lax.dynamic_slice_in_dim(extents, first_img, m, 0),
            lax.dynamic_slice_in_dim(extents, first_img + ni * img_dev, m, 0),
        ],
        0,
    )
    geo = jnp.concatenate([jnp.stack([i, o, c]), ext[:, 0], ext[:, 1]]).astype(jnp.int32)
    area = jnp.sum(extents[:, 0] * extents[:, 1]).astype(F32)
    counts = jnp.stack([4.0 * area, area])

    def iota(shape, axis):
        return lax.broadcasted_iota(jnp.int32, shape, axis)

    def out_mask(geo):
        row, col = halves(iota((cout, 1), 0), wo)
        return jnp.concatenate(
            [
                ((row < geo[GEO + k]) & (col < geo[GEO + pair + k])).astype(F32)
                for k in range(pair)
            ],
            0,
        )

    def phase_cells(shape, axis):
        phase, cell = halves(iota(shape, axis), cout)
        row, col = halves(cell, wo)
        up, left = halves(phase, 2)
        return 2 * row + up, 2 * col + left

    def in_mask(geo):
        row, col = phase_cells((cin, 1), 0)
        return jnp.concatenate(
            [
                ((row < 2 * geo[GEO + k]) & (col < 2 * geo[GEO + pair + k])).astype(F32)
                for k in range(pair)
            ],
            0,
        )

    def order(geo, k, axis):
        shape = (cin, 1) if axis == 0 else (1, cin)
        row, col = phase_cells(shape, axis)
        inside = (row < 2 * geo[GEO + k]) & (col < 2 * geo[GEO + pair + k])
        source = jnp.where(inside, row * wi + col, -1)
        return (source == iota((cin, cin), 1 - axis)).astype(F32).astype(BF16)

    def shift(dr, dc):
        row, col = halves(iota((cout, 1), 0), wo)
        row, col = row + dr, col + dc
        inside = (row >= 0) & (row < ho) & (col >= 0) & (col < wo)
        source = jnp.where(inside, row * wo + col, -1)
        return (source == iota((cout, cout), 1)).astype(F32).astype(BF16)

    def taps_shard(w):
        return mine(w, 2).transpose(0, 1, 3, 2).reshape(9 * mid_io, mh)

    def side_by_side(w):
        h = w.shape[0] // 2
        return jnp.concatenate([w[:h], w[h:]], 1)

    make_r1, make_r2 = down_entries(in_h), down_entries(out_h)
    shape_t = (mid, 9 * mh)
    makers_1 = [make_r1, taps_entries, make_r2]
    makers_2 = [up_entries, short_entries]
    makers_3 = [taps_entries, up_entries]
    shard_1 = jnp.concatenate(
        [
            side_by_side(mine(first_reduce, 0)),
            taps_shard(first_taps),
            side_by_side(mine(second_reduce, 0)),
        ],
        0,
    )
    shard_2 = jnp.concatenate([mine(first_expand, 1), mine(first_shortcut, 1)], 0)
    shard_3 = jnp.concatenate([taps_shard(second_taps), mine(second_expand, 1)], 0)
    def half_rows(take):
        cot_half = take(cotangent.reshape(img_dev, cout, out_part), 2)
        return jnp.concatenate(
            [take(images.reshape(img_dev, cin, in_part), 2)]
            + [cot_half[:, :, q * in_h : (q + 1) * in_h] for q in range(cot_parts)],
            1,
        )

    cot_parts = out_h // in_h
    own_rows = half_rows(mine)
    recv_rows = core_swap(half_rows(other))
    both_rows = jnp.stack([pick(own_rows, recv_rows), pick(recv_rows, own_rows)], 1)
    pieces_1, (shard_2, shard_3), (both_rows,) = together(
        along_outer(shard_1), [shard_2, shard_3], [both_rows]
    )
    parts_1, pieces_2, (both_rows,) = together(
        along_near(pieces_1), along_outer(shard_2), [both_rows]
    )
    parts_1 = along_far(*parts_1, middle(makers_1))
    got_rows = to_images(both_rows)
    parts_1, pieces_2 = together(parts_1, pieces_2)
    (got_rows,), parts_2 = together([got_rows], along_near(pieces_2))
    pieces_3 = along_outer(after(shard_3, got_rows))
    parts_2 = along_far(*parts_2, middle(makers_2))
    w_r1, w_t1, w_r2 = assembled(parts_1, makers_1, [(kin, mid), shape_t, (wide, mid)])

    pm = mine(jnp.concatenate([mid_gains, mid_shifts], 0), 1)
    pw = mine(
        jnp.concatenate([wide_gains, wide_shifts], 0).reshape(6, no, out_part), 2
    ).reshape(6, wide)

    def moments(got, counts, which, row=0):
        total = jnp.sum(got[...], 0)
        mean = total[row : row + 1] / counts[which]
        square = total[row + 1 : row + 2] / counts[which]
        return mean, lax.rsqrt(square - mean * mean + EPS)

    def send_all(copies, rows):
        value = jnp.concatenate(rows, 0)
        for k in range(peers):
            copies[k] = value

    def sums(z, valid=None):
        zv = z if valid is None else z * valid
        return [jnp.sum(zv, 0, keepdims=True), jnp.sum(zv * z, 0, keepdims=True)]

    def copies_shape(rows, width):
        return ((peers, rows, width), F32)

    mid_f = ((rout, mh), F32)
    wide_f = ((rout, wide), F32)
    wide_b = ((rout, wide), BF16)
    mid_b = ((rout, mh), BF16)

    def one_kernel(geo, got, w, masked, own, oth, raw):
        me = geo[2]
        for k in range(m):
            for j in range(no):
                for p in range(2):
                    raw[p * m + k, :, j * in_h : (j + 1) * in_h] = got[j * m + k, p, :cin, :]
        for k in range(pair):
            rows = slice(k * cin, (k + 1) * cin)
            masked[rows, :] = mm(order(geo, k, 0), raw[k]).astype(BF16)
        own[...] = mm(masked[...], w[:, at(mh, me)])
        oth[...] = mm(masked[...], w[:, at(mh, 1 - me)])

    masked, z_own, z_oth = run(
        one_kernel,
        [((rin, kin), BF16), ((rin, mh), F32), ((rin, mh), F32)],
        [geo],
        got_rows,
        w_r1,
        scratch=[pltpu.VMEM((pair, cin, kin), BF16)],
    )

    def one_sums(x, y, z, copies):
        z[...] = x[...] + y[...]
        send_all(copies, sums(z[...]))

    z_one, copies = run(
        one_sums, [((rin, mh), F32), copies_shape(2, mh)], [], z_own, core_swap(z_oth)
    )
    (got_one,), parts_2, pieces_3 = together([sync(copies)], parts_2, pieces_3)
    parts_3 = along_near(pieces_3)
    got_cot = got_rows[:, :, cin:]

    def mid_sums(geo, x, y, z, copies):
        z[...] = x[...] + y[...]
        send_all(copies, sums(z[...], out_mask(geo)))

    def mid_partial(kernel, z, got, w):
        win, own, oth = run(
            kernel,
            [((rout, 9 * mh), BF16), mid_f, mid_f],
            [geo, counts],
            z,
            got,
            pm,
            w,
            scratch=[pltpu.VMEM(z.shape, BF16)],
        )
        z_next, copies = run(
            mid_sums, [mid_f, copies_shape(2, mh)], [geo], own, core_swap(oth)
        )
        return win, z_next, copies

    def normed(z, st, gains, g, s):
        return (z - st[0]) * st[1] * gains[g : g + 1] + gains[s : s + 1]

    def two_kernel(geo, counts, z, got, pm, w, win, own, oth, act):
        st = moments(got, counts, 0)
        act[...] = (gelu(normed(z[...], st, pm, 0, 4)) * in_mask(geo)).astype(BF16)
        moves = {}
        for tap, (p, r) in enumerate(TAPS):
            key = (-int(p == 0), -int(r == 0))
            plane = 2 * int(p != 1) + int(r != 1)
            if key != (0, 0) and key not in moves:
                moves[key] = shift(*key)
            for k in range(pair):
                x = act[k * cin + plane * cout : k * cin + (plane + 1) * cout, :]
                if key != (0, 0):
                    x = mm(moves[key], x).astype(BF16)
                win[k * cout : (k + 1) * cout, tap * mh : (tap + 1) * mh] = x
        own[...] = mm_nt(win[...], w[at(mh, geo[2]), :])
        oth[...] = mm_nt(win[...], w[at(mh, 1 - geo[2]), :])

    win_one, z_two, copies = mid_partial(two_kernel, z_one, got_one, w_t1)
    (got_two,), parts_3 = together([sync(copies)], parts_3)
    parts_3 = along_far(*parts_3, middle(makers_3))
    w_e1, w_s = assembled(parts_2, makers_2, [(mid, wide), (no * in_part, wide)])

    strided_h = masked.reshape(pair, cin, kin)[:, :cout].reshape(rout, kin)
    strided_r = core_swap(strided_h)

    def short_kernel(geo, x, y, w, full, z):
        me = geo[2]
        for j in range(no):
            part = slice(j * in_h, (j + 1) * in_h)
            full[:, pl.ds(pl.multiple_of(j * in_part + me * in_h, in_h), in_h)] = x[:, part]
            full[:, pl.ds(pl.multiple_of(j * in_part + (1 - me) * in_h, in_h), in_h)] = y[:, part]
        z[...] = mm(full[...], w[...])

    strided, z_short = run(
        short_kernel, [((rout, no * in_part), BF16), wide_f], [geo], strided_h, strided_r, w_s
    )

    def act_of(row, z, got):
        def kernel(geo, counts, z, got, pm, act):
            st = moments(got, counts, 1)
            act[...] = (gelu(normed(z[...], st, pm, row, row + 4)) * out_mask(geo)).astype(BF16)

        (act,) = run(kernel, [mid_b], [geo, counts], z, got, pm)
        return act, core_swap(act)

    def join_to(full, geo, x, y):
        full[:, at(mh, geo[2])] = x[...]
        full[:, at(mh, 1 - geo[2])] = y[...]

    def three_kernel(geo, x, y, w, zs, full, z, copies):
        join_to(full, geo, x, y)
        z[...] = mm(full[...], w[...])
        send_all(copies, sums(z[...]) + sums(zs[...]))

    act_own, act_recv = act_of(1, z_two, got_two)
    act_two, z_three, copies = run(
        three_kernel,
        [((rout, mid), BF16), wide_f, copies_shape(4, wide)],
        [geo],
        act_own,
        act_recv,
        w_e1,
        z_short,
    )
    got_three = sync(copies)

    def four_kernel(geo, counts, z3, zs, got, pw, w, hidden, slope, low, own, oth):
        st3, sts = moments(got, counts, 1), moments(got, counts, 1, 2)
        joined = normed(z3[...], st3, pw, 0, 3) + normed(zs[...], sts, pw, 1, 4)
        value, rise = gelu_both(joined)
        valid = out_mask(geo)
        hidden[...] = value * valid
        slope[...] = rise * valid
        low[...] = hidden[...].astype(BF16)
        own[...] = mm(low[...], w[:, at(mh, geo[2])])
        oth[...] = mm(low[...], w[:, at(mh, 1 - geo[2])])

    hidden, slope_one, hidden_low, z_own, z_oth = run(
        four_kernel,
        [wide_f, wide_f, wide_b, mid_f, mid_f],
        [geo, counts],
        z_three,
        z_short,
        got_three,
        pw,
        w_r2,
    )
    z_four, copies = run(
        mid_sums, [mid_f, copies_shape(2, mh)], [geo], z_own, core_swap(z_oth)
    )
    (got_four,), parts_3, (got_cot,) = together([sync(copies)], parts_3, [got_cot])
    w_t2, w_e2 = assembled(parts_3, makers_3, [shape_t, (mid, wide)])

    def five_kernel(geo, counts, z, got, pm, w, win, own, oth, act):
        st = moments(got, counts, 1)
        act[...] = (gelu(normed(z[...], st, pm, 2, 6)) * out_mask(geo)).astype(BF16)
        for tap, (p, r) in enumerate(TAPS):
            key = (p - 1, r - 1)
            move = None if key == (0, 0) else shift(*key)
            for k in range(pair):
                x = act[k * cout : (k + 1) * cout, :]
                if move is not None:
                    x = mm(move, x).astype(BF16)
                win[k * cout : (k + 1) * cout, tap * mh : (tap + 1) * mh] = x
        own[...] = mm_nt(win[...], w[at(mh, geo[2]), :])
        oth[...] = mm_nt(win[...], w[at(mh, 1 - geo[2]), :])

    win_two, z_five, copies = mid_partial(five_kernel, z_four, got_four, w_t2)
    got_five = sync(copies)
    act_own, act_recv = act_of(3, z_five, got_five)

    def six_kernel(geo, x, y, w, full, z, copies):
        join_to(full, geo, x, y)
        z[...] = mm(full[...], w[...])
        send_all(copies, sums(z[...]))

    act_five, z_six, copies = run(
        six_kernel,
        [((rout, mid), BF16), wide_f, copies_shape(2, wide)],
        [geo],
        act_own,
        act_recv,
        w_e2,
    )
    got_six = sync(copies)

    def loss_kernel(geo, counts, z, got, pw, hidden, cot, own, oth, dy, copies, value):
        me = geo[2]
        st = moments(got, counts, 1)
        xhat = (z[...] - st[0]) * st[1]
        out, rise = gelu_both(xhat * pw[2:3] + pw[5:6] + hidden[...])
        valid = out_mask(geo)
        value[...] = (out * valid).astype(BF16)
        own[...] = value[at(m * cout, me), :]
        oth[...] = value[at(m * cout, 1 - me), :]
        for k in range(m):
            for j in range(no):
                for p in range(2):
                    for q in range(cot_parts):
                        part = slice(j * out_h + q * in_h, j * out_h + (q + 1) * in_h)
                        rows = slice((p * m + k) * cout, (p * m + k + 1) * cout)
                        dy[rows, part] = cot[
                            j * m + k, p, q * cout : (q + 1) * cout, :
                        ].astype(F32)
        dy[...] = dy[...] * (rise * valid)
        send_all(copies, dy_sums(dy[...], xhat))

    def dy_sums(dy, *xhats):
        return [jnp.sum(dy, 0, keepdims=True)] + [
            jnp.sum(dy * x, 0, keepdims=True) for x in xhats
        ]

    out_own, out_oth, dy_six, copies = run(
        loss_kernel,
        [((m * cout, wide), BF16), ((m * cout, wide), BF16), wide_f, copies_shape(2, wide)],
        [geo, counts],
        z_six,
        got_six,
        pw,
        hidden,
        got_cot,
        scratch=[pltpu.VMEM((rout, wide), BF16)],
    )
    got_g6 = sync(copies)

    def home(own, recv, cells, part_h):
        def kernel(geo, x, y, out):
            for k in range(m):
                rows = slice(k * cells, (k + 1) * cells)
                for j in range(no):
                    part = slice(j * part_h, (j + 1) * part_h)
                    out[j * m + k, :, at(part_h, geo[2])] = x[rows, part]
                    out[j * m + k, :, at(part_h, 1 - geo[2])] = y[rows, part]

        return run(kernel, [((img_dev, cells, 2 * part_h), BF16)], [geo], own, recv)[0]

    def home_sides(own, recv):
        def kernel(geo, x, y, out):
            for k in range(m):
                rows = slice(k * cout, (k + 1) * cout)
                for j in range(no):
                    part = slice(j * out_h, (j + 1) * out_h)
                    out[j * m + k, at(cout, geo[2]), :] = x[rows, part]
                    out[j * m + k, at(cout, 1 - geo[2]), :] = y[rows, part]

        return run(kernel, [((img_dev, 2 * cout, out_h), BF16)], [geo], own, recv)[0]

    out_rows = home_sides(out_own, core_swap(out_oth))

    def back(dy, xhat, gain, st, valid, total, row, shift_row, count):
        shift_sum, gain_sum = total[shift_row : shift_row + 1], total[row : row + 1]
        return (
            gain * st[1] * (dy - valid * ((shift_sum + xhat * gain_sum) / count))
        ).astype(BF16)

    def back_six(geo, counts, dy, z, got, grads, pw, w, dz, own, oth, total):
        st = moments(got, counts, 1)
        total[...] = jnp.sum(grads[...], 0)
        xhat = (z[...] - st[0]) * st[1]
        dz[...] = back(dy[...], xhat, pw[2:3], st, out_mask(geo), total, 1, 0, counts[1])
        own[...] = mm_nt(dz[...], w[at(mh, geo[2]), :])
        oth[...] = mm_nt(dz[...], w[at(mh, 1 - geo[2]), :])

    dz_six, da_own, da_oth, sum_six = run(
        back_six,
        [wide_b, mid_f, mid_f, ((2, wide), F32)],
        [geo, counts],
        dy_six,
        z_six,
        got_six,
        got_g6,
        pw,
        w_e2,
    )

    def mid_dy(row, own, recv, z, got):
        def kernel(geo, counts, x, y, z, got, pm, dy, copies):
            st = moments(got, counts, 1)
            xhat = (z[...] - st[0]) * st[1]
            rise = gelu_slope(xhat * pm[row : row + 1] + pm[row + 4 : row + 5])
            dy[...] = (x[...] + y[...]) * (out_mask(geo) * rise)
            send_all(copies, dy_sums(dy[...], xhat))

        dy, copies = run(
            kernel, [mid_f, copies_shape(2, mh)], [geo, counts], own, recv, z, got, pm
        )
        return dy, sync(copies)

    def mid_dz(row, dy, z, got, grads):
        which = 0 if row == 0 else 1

        def kernel(geo, counts, dy, z, got, grads, pm, dz, total):
            st = moments(got, counts, which)
            total[...] = jnp.sum(grads[...], 0)
            xhat = (z[...] - st[0]) * st[1]
            valid = in_mask(geo) if row == 0 else out_mask(geo)
            dz[...] = back(
                dy[...], xhat, pm[row : row + 1], st, valid, total, 1, 0, counts[which]
            )

        dz, total = run(
            kernel, [(z.shape, BF16), ((2, mh), F32)], [geo, counts], dy, z, got, grads, pm
        )
        return dz, core_swap(dz), total

    dy_five, got_g5 = mid_dy(3, da_own, core_swap(da_oth), z_five, got_five)
    dz_own, dz_recv, sum_five = mid_dz(3, dy_five, z_five, got_five, got_g5)

    def four_dy(geo, counts, x, y, z, got, pm, w, full, dy, copies, moved):
        join_to(full, geo, x, y)
        total = None
        for tap, (p, r) in enumerate(TAPS):
            key = (1 - p, 1 - r)
            if key == (0, 0):
                left = full[...]
            else:
                move = shift(*key)
                for k in range(pair):
                    rows = slice(k * cout, (k + 1) * cout)
                    moved[rows, :] = mm(move, full[rows, :]).astype(BF16)
                left = moved[...]
            term = mm(left, w[:, tap * mh : (tap + 1) * mh])
            total = term if total is None else total + term
        st = moments(got, counts, 1)
        xhat = (z[...] - st[0]) * st[1]
        dy[...] = total * (out_mask(geo) * gelu_slope(xhat * pm[2:3] + pm[6:7]))
        send_all(copies, dy_sums(dy[...], xhat))

    dz_five, dy_four, copies = run(
        four_dy,
        [((rout, mid), BF16), mid_f, copies_shape(2, mh)],
        [geo, counts],
        dz_own,
        dz_recv,
        z_four,
        got_four,
        pm,
        w_t2,
        scratch=[pltpu.VMEM((rout, mid), BF16)],
    )
    group_te = blocks_of(
        [(shape_t, 0, 1), ((mid, wide), 2, 3)],
        makers_3,
        [dz_five, win_two, act_five, dz_six],
    )
    (got_g4,), group_te = together([sync(copies)], group_te)
    group_te = scatter_far(*group_te)
    dz_own, dz_recv, sum_four = mid_dz(2, dy_four, z_four, got_four, got_g4)

    def joined_dy(geo, counts, x, y, w, dy6, slope, z3, zs, got, full, dy, copies):
        join_to(full, geo, x, y)
        dy[...] = (dy6[...] + mm_nt(full[...], w[...])) * slope[...]
        st3, sts = moments(got, counts, 1), moments(got, counts, 1, 2)
        send_all(
            copies,
            dy_sums(dy[...], (z3[...] - st3[0]) * st3[1], (zs[...] - sts[0]) * sts[1]),
        )

    dz_four, dy_joined, copies = run(
        joined_dy,
        [((rout, mid), BF16), wide_f, copies_shape(3, wide)],
        [geo, counts],
        dz_own,
        dz_recv,
        w_r2,
        dy_six,
        slope_one,
        z_three,
        z_short,
        got_three,
    )
    (copies,), group_te = together([copies], group_te)
    (got_g3,), group_te = together([sync(copies)], scatter_add(*group_te))
    group_te = scatter_near(*group_te)

    def back_three(geo, counts, dy, z3, zs, got, grads, pw, w, dz3, dzs, own, oth, total):
        st3, sts = moments(got, counts, 1), moments(got, counts, 1, 2)
        total[...] = jnp.sum(grads[...], 0)
        valid = out_mask(geo)
        x3, xs = (z3[...] - st3[0]) * st3[1], (zs[...] - sts[0]) * sts[1]
        dz3[...] = back(dy[...], x3, pw[0:1], st3, valid, total, 1, 0, counts[1])
        dzs[...] = back(dy[...], xs, pw[1:2], sts, valid, total, 2, 0, counts[1])
        own[...] = mm_nt(dz3[...], w[at(mh, geo[2]), :])
        oth[...] = mm_nt(dz3[...], w[at(mh, 1 - geo[2]), :])

    dz_three, dz_short, da_own, da_oth, sum_three = run(
        back_three,
        [wide_b, wide_b, mid_f, mid_f, ((3, wide), F32)],
        [geo, counts],
        dy_joined,
        z_three,
        z_short,
        got_three,
        got_g3,
        pw,
        w_e1,
    )
    group_es = blocks_of(
        [((wide, mid), 0, 1), ((mid, wide), 2, 3), ((no * in_part, wide), 4, 5)],
        [make_r2] + makers_2,
        [hidden_low, dz_four, act_two, dz_three, strided, dz_short],
    )
    dy_two, got_g2 = mid_dy(1, da_own, core_swap(da_oth), z_two, got_two)
    (got_g2,), group_es, group_te = together([got_g2], group_es, group_te)
    group_te = scatter_sends(*group_te)
    group_es = scatter_far(*group_es)

    def short_back(geo, dz, w, own, oth):
        me = geo[2]
        for j in range(no):
            part = slice(j * in_h, (j + 1) * in_h)
            rows = pl.ds(pl.multiple_of(j * in_part + me * in_h, in_h), in_h)
            own[:, part] = mm_nt(dz[...], w[rows, :])
            rows = pl.ds(pl.multiple_of(j * in_part + (1 - me) * in_h, in_h), in_h)
            oth[:, part] = mm_nt(dz[...], w[rows, :])

    ds_own, ds_oth = run(short_back, [((rout, kin), F32)] * 2, [geo], dz_short, w_s)
    ds_recv = core_swap(ds_oth)
    dz_own, dz_recv, sum_two = mid_dz(1, dy_two, z_two, got_two, got_g2)

    def one_dy(geo, counts, x, y, z, got, pm, w, full, dy, copies, moved):
        join_to(full, geo, x, y)
        for n, key in enumerate([(0, 1), (1, 0), (1, 1)]):
            move = shift(*key)
            for k in range(pair):
                rows = slice(k * cout, (k + 1) * cout)
                moved[n, rows, :] = mm(move, full[rows, :]).astype(BF16)
        for plane in range(4):
            total = None
            for p in (1,) if plane < 2 else (0, 2):
                for r in (1,) if plane % 2 == 0 else (0, 2):
                    n = 2 * int(p == 0) + int(r == 0)
                    left = full[...] if n == 0 else moved[n - 1]
                    tap = 3 * p + r
                    term = mm(left, w[:, tap * mh : (tap + 1) * mh])
                    total = term if total is None else total + term
            for k in range(pair):
                dy[k * cin + plane * cout : k * cin + (plane + 1) * cout, :] = total[
                    k * cout : (k + 1) * cout
                ]
        st = moments(got, counts, 0)
        xhat = (z[...] - st[0]) * st[1]
        dy[...] = dy[...] * (in_mask(geo) * gelu_slope(xhat * pm[0:1] + pm[4:5]))
        send_all(copies, dy_sums(dy[...], xhat))

    dz_two, dy_one, copies = run(
        one_dy,
        [((rout, mid), BF16), ((rin, mh), F32), copies_shape(2, mh)],
        [geo, counts],
        dz_own,
        dz_recv,
        z_one,
        got_one,
        pm,
        w_t1,
        scratch=[pltpu.VMEM((3, rout, mid), BF16)],
    )
    group_t1 = blocks_of([(shape_t, 0, 1)], [taps_entries], [dz_two, win_one])
    (copies,), group_es = together([copies], group_es)
    (got_g1,), group_es, group_t1, group_te = together(
        [sync(copies)], scatter_add(*group_es), group_t1, group_te
    )
    group_t1 = scatter_far(*group_t1)
    group_es = scatter_near(*group_es)
    dz_own, dz_recv, sum_one = mid_dz(0, dy_one, z_one, got_one, got_g1)

    def images_kernel(geo, x, y, w, ds, dr, full, own, oth, rows_in):
        join_to(full, geo, x, y)
        me = geo[2]
        for k in range(pair):
            rows = slice(k * cin, (k + 1) * cin)
            first = slice(k * cin, k * cin + cout)
            rest = slice(k * cin + cout, (k + 1) * cin)
            outs = slice(k * cout, (k + 1) * cout)
            rows_in[first, :] = (
                mm_nt(full[first, :], w[...]) + (ds[outs, :] + dr[outs, :])
            ).astype(BF16)
            rows_in[rest, :] = mm_nt(full[rest, :], w[...]).astype(BF16)
        for k in range(m):
            rows = slice(k * cin, (k + 1) * cin)
            for ref, img in ((oth, (1 - me) * m + k), (own, me * m + k)):
                ref[rows, :] = mm(order(geo, img, 1), rows_in[at(cin, img), :]).astype(BF16)

    dz_one, d_own, d_oth = run(
        images_kernel,
        [((rin, mid), BF16), ((m * cin, kin), BF16), ((m * cin, kin), BF16)],
        [geo],
        dz_own,
        dz_recv,
        w_r1,
        ds_own,
        ds_recv,
        scratch=[pltpu.VMEM((rin, kin), BF16)],
    )
    d_rows = home(d_own, core_swap(d_oth), cin, in_h)
    group_t1 = scatter_near(*scatter_add(*group_t1))
    group_r1 = scatter_inner(
        *blocks_of([((kin, mid), 0, 1)], [make_r1], [masked, dz_one], split=False)
    )

    rows_es = group_es[0].shape[1]
    rows_t = 9 * mid_io
    (d_rows,), group_es = together([d_rows], group_es)
    near = to_images(jnp.concatenate([d_rows, out_rows], 1))
    last = jnp.concatenate(
        [scatter_sum(*group_es), scatter_sum(*group_t1), scatter_sum(*group_r1)], 1
    )
    (near,), (last,) = together([near], [last])
    last = to_images(last)
    grad_images = near[:, :cin].astype(F32).reshape(images.shape)
    block_output = jnp.concatenate(
        [near[:, cin : cin + cout], near[:, cin + cout :]], 2
    ).reshape(img_dev, ho, wo, out_part)
    grads_es = scatter_last(last[:, :rows_es])
    grads_t1 = scatter_last(last[:, rows_es : rows_es + rows_t])
    grads_r1 = scatter_last(last[:, rows_es + rows_t :])
    grads_te = scatter_last(jnp.stack(group_te))

    def stacked(x):
        w = x.shape[1] // 2
        return jnp.concatenate([x[:, :w], x[:, w:]], 0)

    rows_r2 = out_h // 2

    def taps_out(rows):
        both = swap_full(rows.reshape(9, mid_io, mh), 2)
        return both.transpose(0, 2, 1).reshape(first_taps.shape)

    grad_e1_s = swap_full(grads_es[rows_r2:], 1)
    mids = jnp.stack([sum_one, sum_two, sum_four, sum_five], 1)
    mids = swap_full(mids, 2)
    wides = jnp.concatenate([sum_three, sum_six], 0).reshape(5, no, out_h)
    wides = swap_full(wides, 2).reshape(5, no * out_part)
    return (
        block_output,
        grad_images,
        swap_full(stacked(grads_r1), 0),
        taps_out(grads_t1),
        grad_e1_s[:mid_i],
        grad_e1_s[mid_i:],
        swap_full(stacked(grads_es[:rows_r2]), 0),
        taps_out(grads_te[:rows_t]),
        swap_full(grads_te[rows_t:], 1),
        mids[1],
        mids[0],
        jnp.stack([wides[1], wides[2], wides[4]]),
        jnp.stack([wides[0], wides[0], wides[3]]),
    )


def solution(mesh):
    wide = P(("batch", "inner"), None, None, "outer")
    down = P("outer", "inner")
    up = P("inner", "outer")
    taps = P(None, None, None, ("inner", "outer"))
    whole = P()
    return jax.shard_map(
        shards,
        mesh=mesh,
        in_specs=(wide, whole, down, taps, up, down, down, taps, up)
        + (whole, whole, whole, whole, wide),
        out_specs=(wide, wide, down, taps, up, down, down, taps, up, whole, whole, whole, whole),
        check_vma=False,
    )
```

```python
import math

import jax
import jax.numpy as jnp
from jax import lax
from jax.experimental import pallas as pl
from jax.experimental.pallas import tpu as pltpu
from jax.sharding import PartitionSpec as P

EPS = 1e-05
ROOT = math.sqrt(2.0 / math.pi)
CUBE = 0.044715
F32 = jnp.float32
BF16 = jnp.bfloat16
XS = [(k, k ^ 1) for k in range(4)]
YS = [(k, k ^ 2) for k in range(4)]
DS = [(k, k ^ 3) for k in range(4)]
FAR = 3
GEO = 3
TAPS = [(p, r) for p in range(3) for r in range(3)]


def mm(left, right):
    return lax.dot_general(left, right, (((1,), (0,)), ((), ())), preferred_element_type=F32)


def mm_nt(left, right):
    return lax.dot_general(left, right, (((1,), (1,)), ((), ())), preferred_element_type=F32)


def mm_tn(left, right):
    return lax.dot_general(left, right, (((0,), (0,)), ((), ())), preferred_element_type=F32)


def gelu(v):
    return 0.5 * v * (1.0 + jnp.tanh(ROOT * (v + CUBE * v * v * v)))


def gelu_both(v):
    t = jnp.tanh(ROOT * (v + CUBE * v * v * v))
    half = 0.5 * (1.0 + t)
    return v * half, half + 0.5 * v * (1.0 - t * t) * (ROOT * (1.0 + 3.0 * CUBE * v * v))


def gelu_slope(v):
    return gelu_both(v)[1]


def halves(x, k):
    if k & (k - 1) == 0:
        s = k.bit_length() - 1
        return lax.shift_right_logical(x, jnp.int32(s)), lax.bitwise_and(x, jnp.int32(k - 1))
    return lax.div(x, jnp.int32(k)), lax.rem(x, jnp.int32(k))


def at(unit, index, size=None):
    return pl.ds(pl.multiple_of(index * unit, unit), unit if size is None else size)


def after(x, *done):
    return lax.optimization_barrier((x, done))[0]


def together(*groups):
    flat = [x for g in groups for x in g]
    flat = list(lax.optimization_barrier(tuple(flat)))
    out = []
    for g in groups:
        out.append(flat[: len(g)])
        flat = flat[len(g) :]
    return out


def run(kernel, outs, smem, *arrays, scratch=(), flops=0, limit=20 << 20):
    shapes = [jax.ShapeDtypeStruct(s, d) for s, d in outs]
    moved = sum(a.size * a.dtype.itemsize for a in arrays)
    moved += sum(math.prod(s) * jnp.dtype(d).itemsize for s, d in outs)
    return pl.pallas_call(
        kernel,
        out_shape=shapes,
        in_specs=[pl.BlockSpec(memory_space=pltpu.SMEM)] * len(smem)
        + [pl.BlockSpec(memory_space=pltpu.VMEM)] * len(arrays),
        out_specs=[pl.BlockSpec(memory_space=pltpu.VMEM)] * len(outs),
        scratch_shapes=list(scratch),
        compiler_params=pltpu.CompilerParams(vmem_limit_bytes=limit),
        cost_estimate=pl.CostEstimate(flops=flops, bytes_accessed=moved, transcendentals=0),
    )(*smem, *arrays)


def shards(
    images,
    extents,
    first_reduce,
    first_taps,
    first_expand,
    first_shortcut,
    second_reduce,
    second_taps,
    second_expand,
    mid_gains,
    mid_shifts,
    wide_gains,
    wide_shifts,
    cotangent,
):
    nb = lax.axis_size("batch")
    ni = lax.axis_size("inner")
    no = lax.axis_size("outer")
    b = lax.axis_index("batch")
    i = lax.axis_index("inner")
    o = lax.axis_index("outer")
    c = b % 2
    img_dev, hi, wi, in_part = images.shape
    ho, wo = hi // 2, wi // 2
    out_part = cotangent.shape[3]
    m = img_dev // no
    pair = 2 * m
    cin, cout = hi * wi, ho * wo
    rin, rout = pair * cin, pair * cout
    mid = mid_gains.shape[1]
    mh = mid // 2
    in_h = in_part // 2
    out_h = out_part // 2
    kin = no * in_h
    wide = no * out_h
    mid_i = mid // ni
    mid_io = mid // (ni * no)
    peers = ni * no
    lanes = out_h

    def core_swap(x):
        return lax.ppermute(x, "batch", [(k, k ^ 1) for k in range(nb)])

    def pick(low, high):
        return jnp.where(c == 0, low, high)

    def mine(x, axis):
        h = x.shape[axis] // 2
        return pick(lax.slice_in_dim(x, 0, h, axis=axis), lax.slice_in_dim(x, h, 2 * h, axis=axis))

    def other(x, axis):
        h = x.shape[axis] // 2
        return pick(lax.slice_in_dim(x, h, 2 * h, axis=axis), lax.slice_in_dim(x, 0, h, axis=axis))

    def swap_full(x, axis):
        recv = core_swap(x)
        return pick(jnp.concatenate([x, recv], axis), jnp.concatenate([recv, x], axis))

    def over_batch(x):
        total = x
        for k in range(1, nb // 2):
            total = total + lax.ppermute(x, "batch", [(j, (j + 2 * k) % nb) for j in range(nb)])
        return total

    def sync(copies):
        got = lax.all_to_all(copies, ("inner", "outer"), split_axis=0, concat_axis=0, tiled=True)
        return got if nb == 2 else over_batch(jnp.sum(got, 0, keepdims=True))

    def to_images(x):
        return lax.all_to_all(x, "outer", split_axis=0, concat_axis=0, tiled=True)

    def taps_entries(first, w):
        def entry(tap):
            place = lambda pi, po: (pi * no + po, mid_io, 0, tap, mh)
            return (first + tap * mid_io, mid_io, 0, mh, w, place)

        return [entry(tap) for tap in range(9)], 9 * mid_io

    def up_entries(first, w):
        place = lambda pi, po: (pi, mid_i, 0, po, out_h)
        return [(first, mid_i, 0, out_h, w, place)], mid_i

    def short_entries(first, w):
        quarter = in_part // 4

        def entry(k):
            place = lambda pi, po: (po, in_part, k * quarter, pi, out_h)
            return (first + k * quarter, quarter, 0, out_h, w, place)

        return [entry(k) for k in range(4)], in_part

    def down_entries(rows):
        def make(first, w):
            half = rows // 2

            def entry(side):
                place = lambda pi, po: (po, rows, side * half, pi, mid_i)
                return (first, half, side * mid_i, mid_i, w, place)

            return [entry(0), entry(1)], half

        return make

    def table(makers):
        entries, first = [], 0
        for w, make in enumerate(makers):
            got, used = make(first, w)
            entries += got
            first += used
        return entries, first

    def middle(makers):
        entries, rows = table(makers)
        return min(first + count for first, count, *_ in entries if 2 * (first + count) >= rows)

    def region(place, pi, po, count, width):
        row, row_unit, plus, col, col_unit = place(pi, po)
        return (
            pl.ds(pl.multiple_of(row * row_unit, row_unit) + plus, count),
            pl.ds(pl.multiple_of(col * col_unit, col_unit), width),
        )

    place_io = jnp.stack([i, o]).astype(jnp.int32)

    def shifted(x, k):
        return lax.ppermute(x, "outer", [(j, (j + k) % no) for j in range(no)])

    def along_outer(shard):
        return [shard] + [shifted(shard, k) for k in range(1, no)]

    def along_inner(pieces):
        whole = jnp.stack(pieces)
        return [whole] + [lax.ppermute(whole, "inner", perm) for perm in (XS, YS, DS)]

    def along_near(pieces):
        def kernel(*refs):
            for k in range(no):
                refs[no][k] = refs[k][...]

        (whole,) = run(kernel, [((no,) + pieces[0].shape, BF16)], [], *pieces)
        return whole, lax.ppermute(whole, "inner", XS), lax.ppermute(whole, "inner", YS)

    def along_far(whole, by_x, by_y, h):
        def kernel(x, y, low, high):
            low[...] = x[:, :h]
            high[...] = y[:, h:]

        rows, cols = whole.shape[1:]
        low, high = run(
            kernel, [((no, h, cols), BF16), ((no, rows - h, cols), BF16)], [], by_x, by_y
        )
        low, high = lax.ppermute(low, "inner", YS), lax.ppermute(high, "inner", XS)
        return whole, by_x, by_y, low, high

    def assembled(parts, makers, shapes):
        entries, _ = table(makers)
        h = middle(makers)

        def kernel(where, *refs):
            sources, targets = refs[: len(parts)], refs[len(parts) :]
            for far in range(ni):
                for d in range(no):
                    pi, po = where[0] ^ far, lax.rem(where[1] + (no - d), no)
                    for first, count, lane, width, w, place in entries:
                        source, start = sources[far], first
                        if len(parts) > ni and far == FAR and first >= h:
                            source, start = sources[ni], first - h
                        targets[w][region(place, pi, po, count, width)] = source[
                            d, start : start + count, lane : lane + width
                        ]

        return run(kernel, [(s, BF16) for s in shapes], [place_io], *parts)

    def blocks_of(products, makers, operands, split=True):
        entries, rows = table(makers)
        h = middle(makers)
        sizes = [rows, rows, rows] + ([h, rows - h] if split else [rows])
        n = len(operands)

        def kernel(where, *refs):
            ins, outs, grads = refs[:n], refs[n : n + len(sizes)], refs[n + len(sizes) :]
            for grad, (_, left, right) in zip(grads, products, strict=True):
                grad[...] = mm_tn(ins[left][...], ins[right][...]).astype(BF16)
            for far in range(ni):
                for po in range(no):
                    pi = where[0] ^ far
                    for first, count, lane, width, w, place in entries:
                        out, start = outs[far], first
                        if split and far == FAR and first >= h:
                            out, start = outs[ni], first - h
                        out[po, start : start + count, lane : lane + width] = grads[w][
                            region(place, pi, po, count, width)
                        ]

        return run(
            kernel,
            [((no, r, lanes), BF16) for r in sizes],
            [place_io],
            *operands,
            scratch=[pltpu.VMEM(prod[0], BF16) for prod in products],
        )

    def scatter_far(own, to_x, to_y, low, high):
        return own, to_x, to_y, lax.ppermute(low, "inner", XS), lax.ppermute(high, "inner", YS)

    def scatter_add(own, to_x, to_y, low, high):
        h = low.shape[1]

        def kernel(x, y, a, z, out_x, out_y):
            out_x[:, :h] = x[:, :h]
            out_x[:, h:] = (x[:, h:].astype(F32) + z[...].astype(F32)).astype(BF16)
            out_y[:, :h] = (y[:, :h].astype(F32) + a[...].astype(F32)).astype(BF16)
            out_y[:, h:] = y[:, h:]

        return [own] + list(run(kernel, [(own.shape, BF16)] * 2, [], to_x, to_y, low, high))

    def scatter_near(own, to_x, to_y):
        return [own, lax.ppermute(to_x, "inner", XS), lax.ppermute(to_y, "inner", YS)]

    def scatter_inner(own, *sends):
        return [own] + [
            lax.ppermute(x, "inner", perm) for x, perm in zip(sends, (XS, YS, DS), strict=True)
        ]

    def scatter_sum(*groups):
        rows = [g[0].shape[1] for g in groups]

        def kernel(*refs):
            row, refs, out = 0, list(refs[:-1]), refs[-1]
            for g, count in zip(groups, rows, strict=True):
                mine, refs = refs[: len(g)], refs[len(g) :]
                total = mine[0][...].astype(F32)
                for ref in mine[1:]:
                    total = total + ref[...].astype(F32)
                out[:, row : row + count, :] = total.astype(BF16)
                row += count

        flat = [x for g in groups for x in g]
        return run(kernel, [((no, sum(rows), lanes), BF16)], [], *flat)[0]

    def scatter_last(*parts):
        def kernel(*refs):
            total = refs[0][...].astype(F32)
            for ref in refs[1:-1]:
                total = total + ref[...].astype(F32)
            refs[-1][...] = total

        half = over_batch(run(kernel, [(parts[0].shape, F32)], [], *parts)[0])
        return half, core_swap(half)

    first_img = ((b - c) * ni + i) * img_dev + o * m
    ext = jnp.concatenate(
        [
            lax.dynamic_slice_in_dim(extents, first_img, m, 0),
            lax.dynamic_slice_in_dim(extents, first_img + ni * img_dev, m, 0),
        ],
        0,
    )
    geo = jnp.concatenate([jnp.stack([i, o, c]), ext[:, 0], ext[:, 1]]).astype(jnp.int32)
    area = jnp.sum(extents[:, 0] * extents[:, 1]).astype(F32)
    counts = jnp.stack([4.0 * area, area])

    def iota(shape, axis):
        return lax.broadcasted_iota(jnp.int32, shape, axis)

    def out_mask(geo):
        row, col = halves(iota((cout, 1), 0), wo)
        return jnp.concatenate(
            [
                ((row < geo[GEO + k]) & (col < geo[GEO + pair + k])).astype(F32)
                for k in range(pair)
            ],
            0,
        )

    def phase_cells(shape, axis):
        phase, cell = halves(iota(shape, axis), cout)
        row, col = halves(cell, wo)
        up, left = halves(phase, 2)
        return 2 * row + up, 2 * col + left

    def in_mask(geo):
        row, col = phase_cells((cin, 1), 0)
        return jnp.concatenate(
            [
                ((row < 2 * geo[GEO + k]) & (col < 2 * geo[GEO + pair + k])).astype(F32)
                for k in range(pair)
            ],
            0,
        )

    def order(geo, k, axis):
        shape = (cin, 1) if axis == 0 else (1, cin)
        row, col = phase_cells(shape, axis)
        inside = (row < 2 * geo[GEO + k]) & (col < 2 * geo[GEO + pair + k])
        source = jnp.where(inside, row * wi + col, -1)
        return (source == iota((cin, cin), 1 - axis)).astype(F32).astype(BF16)

    def shift(dr, dc):
        row, col = halves(iota((cout, 1), 0), wo)
        row, col = row + dr, col + dc
        inside = (row >= 0) & (row < ho) & (col >= 0) & (col < wo)
        source = jnp.where(inside, row * wo + col, -1)
        return (source == iota((cout, cout), 1)).astype(F32).astype(BF16)

    def taps_shard(w):
        return mine(w, 2).transpose(0, 1, 3, 2).reshape(9 * mid_io, mh)

    def side_by_side(w):
        h = w.shape[0] // 2
        return jnp.concatenate([w[:h], w[h:]], 1)

    make_r1, make_r2 = down_entries(in_h), down_entries(out_h)
    shape_t = (mid, 9 * mh)
    makers_1 = [make_r1, taps_entries, make_r2]
    makers_2 = [up_entries, short_entries]
    makers_3 = [taps_entries, up_entries]
    shard_1 = jnp.concatenate(
        [
            side_by_side(mine(first_reduce, 0)),
            taps_shard(first_taps),
            side_by_side(mine(second_reduce, 0)),
        ],
        0,
    )
    shard_2 = jnp.concatenate([mine(first_expand, 1), mine(first_shortcut, 1)], 0)
    shard_3 = jnp.concatenate([taps_shard(second_taps), mine(second_expand, 1)], 0)
    def both_cores(x):
        own, recv = mine(x, 2), core_swap(other(x, 2))
        return jnp.stack([pick(own, recv), pick(recv, own)], 1)

    both_rows = both_cores(images.reshape(img_dev, cin, in_part))
    cot_rows = both_cores(cotangent.reshape(img_dev, cout, out_part)).reshape(
        no, m, 2, cout, out_h
    )
    cots = [
        lax.dynamic_index_in_dim(cot_rows, (o + k) % no, 0, keepdims=False).reshape(
            pair * cout, out_h
        )
        for k in range(no)
    ]
    pieces_1, (shard_2, shard_3), (both_rows,), cots = together(
        along_outer(shard_1), [shard_2, shard_3], [both_rows], cots
    )
    parts_1, pieces_2, (both_rows,) = together(
        along_near(pieces_1), along_outer(shard_2), [both_rows]
    )
    parts_1 = along_far(*parts_1, middle(makers_1))
    got_rows = to_images(both_rows)
    parts_1, pieces_2 = together(parts_1, pieces_2)
    (got_rows,), parts_2 = together([got_rows], along_near(pieces_2))
    pieces_3 = along_outer(after(shard_3, got_rows))
    parts_2 = along_far(*parts_2, middle(makers_2))
    w_r1, w_t1, w_r2 = assembled(parts_1, makers_1, [(kin, mid), shape_t, (wide, mid)])

    pm = mine(jnp.concatenate([mid_gains, mid_shifts], 0), 1)
    pw = mine(
        jnp.concatenate([wide_gains, wide_shifts], 0).reshape(6, no, out_part), 2
    ).reshape(6, wide)
    (got_rows,), (pm, pw) = together([got_rows], [pm, pw])

    def moments(got, counts, which, row=0):
        total = jnp.sum(got[...], 0)
        mean = total[row : row + 1] / counts[which]
        square = total[row + 1 : row + 2] / counts[which]
        return mean, lax.rsqrt(square - mean * mean + EPS)

    def send_all(copies, rows):
        value = jnp.concatenate(rows, 0)
        for k in range(peers):
            copies[k] = value

    def sums(z, valid=None):
        zv = z if valid is None else z * valid
        return [jnp.sum(zv, 0, keepdims=True), jnp.sum(zv * z, 0, keepdims=True)]

    def copies_shape(rows, width):
        return ((peers, rows, width), F32)

    mid_f = ((rout, mh), F32)
    wide_f = ((rout, wide), F32)
    wide_b = ((rout, wide), BF16)
    mid_b = ((rout, mh), BF16)

    def one_kernel(geo, got, w, masked, own, oth, raw):
        me = geo[2]
        for k in range(m):
            for j in range(no):
                for p in range(2):
                    raw[p * m + k, :, j * in_h : (j + 1) * in_h] = got[j * m + k, p, :cin, :]
        for k in range(pair):
            rows = slice(k * cin, (k + 1) * cin)
            masked[rows, :] = mm(order(geo, k, 0), raw[k]).astype(BF16)
        own[...] = mm(masked[...], w[:, at(mh, me)])
        oth[...] = mm(masked[...], w[:, at(mh, 1 - me)])

    masked, z_own, z_oth = run(
        one_kernel,
        [((rin, kin), BF16), ((rin, mh), F32), ((rin, mh), F32)],
        [geo],
        got_rows,
        w_r1,
        scratch=[pltpu.VMEM((pair, cin, kin), BF16)],
    )

    def one_sums(x, y, z, copies):
        z[...] = x[...] + y[...]
        send_all(copies, sums(z[...]))

    z_one, copies = run(
        one_sums, [((rin, mh), F32), copies_shape(2, mh)], [], z_own, core_swap(z_oth)
    )
    (got_one,), parts_2, pieces_3 = together([sync(copies)], parts_2, pieces_3)
    parts_3 = along_near(pieces_3)

    def mid_sums(geo, x, y, z, copies):
        z[...] = x[...] + y[...]
        send_all(copies, sums(z[...], out_mask(geo)))

    def mid_partial(kernel, z, got, w):
        win, own, oth = run(
            kernel,
            [((rout, 9 * mh), BF16), mid_f, mid_f],
            [geo, counts],
            z,
            got,
            pm,
            w,
            scratch=[pltpu.VMEM(z.shape, BF16)],
        )
        z_next, copies = run(
            mid_sums, [mid_f, copies_shape(2, mh)], [geo], own, core_swap(oth)
        )
        return win, z_next, copies

    def normed(z, st, gains, g, s):
        return (z - st[0]) * st[1] * gains[g : g + 1] + gains[s : s + 1]

    def two_kernel(geo, counts, z, got, pm, w, win, own, oth, act):
        st = moments(got, counts, 0)
        act[...] = (gelu(normed(z[...], st, pm, 0, 4)) * in_mask(geo)).astype(BF16)
        moves = {}
        for tap, (p, r) in enumerate(TAPS):
            key = (-int(p == 0), -int(r == 0))
            plane = 2 * int(p != 1) + int(r != 1)
            if key != (0, 0) and key not in moves:
                moves[key] = shift(*key)
            for k in range(pair):
                x = act[k * cin + plane * cout : k * cin + (plane + 1) * cout, :]
                if key != (0, 0):
                    x = mm(moves[key], x).astype(BF16)
                win[k * cout : (k + 1) * cout, tap * mh : (tap + 1) * mh] = x
        own[...] = mm_nt(win[...], w[at(mh, geo[2]), :])
        oth[...] = mm_nt(win[...], w[at(mh, 1 - geo[2]), :])

    win_one, z_two, copies = mid_partial(two_kernel, z_one, got_one, w_t1)
    (got_two,), parts_3 = together([sync(copies)], parts_3)
    parts_3 = along_far(*parts_3, middle(makers_3))
    w_e1, w_s = assembled(parts_2, makers_2, [(mid, wide), (no * in_part, wide)])

    strided_h = masked.reshape(pair, cin, kin)[:, :cout].reshape(rout, kin)
    strided_r = core_swap(strided_h)

    def short_kernel(geo, x, y, w, full, z):
        me = geo[2]
        for j in range(no):
            part = slice(j * in_h, (j + 1) * in_h)
            full[:, pl.ds(pl.multiple_of(j * in_part + me * in_h, in_h), in_h)] = x[:, part]
            full[:, pl.ds(pl.multiple_of(j * in_part + (1 - me) * in_h, in_h), in_h)] = y[:, part]
        z[...] = mm(full[...], w[...])

    strided, z_short = run(
        short_kernel, [((rout, no * in_part), BF16), wide_f], [geo], strided_h, strided_r, w_s
    )

    def act_of(row, z, got):
        def kernel(geo, counts, z, got, pm, act):
            st = moments(got, counts, 1)
            act[...] = (gelu(normed(z[...], st, pm, row, row + 4)) * out_mask(geo)).astype(BF16)

        (act,) = run(kernel, [mid_b], [geo, counts], z, got, pm)
        return act, core_swap(act)

    def join_to(full, geo, x, y):
        full[:, at(mh, geo[2])] = x[...]
        full[:, at(mh, 1 - geo[2])] = y[...]

    def three_kernel(geo, x, y, w, zs, full, z, copies):
        join_to(full, geo, x, y)
        z[...] = mm(full[...], w[...])
        send_all(copies, sums(z[...]) + sums(zs[...]))

    act_own, act_recv = act_of(1, z_two, got_two)
    act_two, z_three, copies = run(
        three_kernel,
        [((rout, mid), BF16), wide_f, copies_shape(4, wide)],
        [geo],
        act_own,
        act_recv,
        w_e1,
        z_short,
    )
    (copies,), parts_3 = together([copies], parts_3)
    (got_three,), cots = together([sync(copies)], cots)
    cots = cots[:1] + [shifted(x, k) for k, x in enumerate(cots) if k]

    def four_kernel(geo, counts, z3, zs, got, pw, w, hidden, slope, low, own, oth):
        st3, sts = moments(got, counts, 1), moments(got, counts, 1, 2)
        joined = normed(z3[...], st3, pw, 0, 3) + normed(zs[...], sts, pw, 1, 4)
        value, rise = gelu_both(joined)
        valid = out_mask(geo)
        hidden[...] = value * valid
        slope[...] = rise * valid
        low[...] = hidden[...].astype(BF16)
        own[...] = mm(low[...], w[:, at(mh, geo[2])])
        oth[...] = mm(low[...], w[:, at(mh, 1 - geo[2])])

    hidden, slope_one, hidden_low, z_own, z_oth = run(
        four_kernel,
        [wide_f, wide_f, wide_b, mid_f, mid_f],
        [geo, counts],
        z_three,
        z_short,
        got_three,
        pw,
        w_r2,
    )
    z_four, copies = run(
        mid_sums, [mid_f, copies_shape(2, mh)], [geo], z_own, core_swap(z_oth)
    )
    (got_four,), parts_3 = together([sync(copies)], parts_3)
    w_t2, w_e2 = assembled(parts_3, makers_3, [shape_t, (mid, wide)])

    def five_kernel(geo, counts, z, got, pm, w, win, own, oth, act):
        st = moments(got, counts, 1)
        act[...] = (gelu(normed(z[...], st, pm, 2, 6)) * out_mask(geo)).astype(BF16)
        for tap, (p, r) in enumerate(TAPS):
            key = (p - 1, r - 1)
            move = None if key == (0, 0) else shift(*key)
            for k in range(pair):
                x = act[k * cout : (k + 1) * cout, :]
                if move is not None:
                    x = mm(move, x).astype(BF16)
                win[k * cout : (k + 1) * cout, tap * mh : (tap + 1) * mh] = x
        own[...] = mm_nt(win[...], w[at(mh, geo[2]), :])
        oth[...] = mm_nt(win[...], w[at(mh, 1 - geo[2]), :])

    win_two, z_five, copies = mid_partial(five_kernel, z_four, got_four, w_t2)
    got_five = sync(copies)
    act_own, act_recv = act_of(3, z_five, got_five)

    def six_kernel(geo, x, y, w, full, z, copies):
        join_to(full, geo, x, y)
        z[...] = mm(full[...], w[...])
        send_all(copies, sums(z[...]))

    act_five, z_six, copies = run(
        six_kernel,
        [((rout, mid), BF16), wide_f, copies_shape(2, wide)],
        [geo],
        act_own,
        act_recv,
        w_e2,
    )
    (copies,), cots = together([copies], cots)
    got_six = sync(copies)

    def loss_kernel(geo, counts, z, got, pw, hidden, *refs):
        cots, (own, oth, dy, copies, value) = refs[:no], refs[no:]
        me = geo[2]
        st = moments(got, counts, 1)
        xhat = (z[...] - st[0]) * st[1]
        out, rise = gelu_both(xhat * pw[2:3] + pw[5:6] + hidden[...])
        valid = out_mask(geo)
        value[...] = (out * valid).astype(BF16)
        own[...] = value[at(m * cout, me), :]
        oth[...] = value[at(m * cout, 1 - me), :]
        for d in range(no):
            part = at(out_h, lax.rem(geo[1] + (no - d), no))
            for k in range(m):
                for p in range(2):
                    rows = slice((p * m + k) * cout, (p * m + k + 1) * cout)
                    source = slice((k * 2 + p) * cout, (k * 2 + p + 1) * cout)
                    dy[rows, part] = cots[d][source, :].astype(F32)
        dy[...] = dy[...] * (rise * valid)
        send_all(copies, dy_sums(dy[...], xhat))

    def dy_sums(dy, *xhats):
        return [jnp.sum(dy, 0, keepdims=True)] + [
            jnp.sum(dy * x, 0, keepdims=True) for x in xhats
        ]

    out_own, out_oth, dy_six, copies = run(
        loss_kernel,
        [((m * cout, wide), BF16), ((m * cout, wide), BF16), wide_f, copies_shape(2, wide)],
        [geo, counts],
        z_six,
        got_six,
        pw,
        hidden,
        *cots,
        scratch=[pltpu.VMEM((rout, wide), BF16)],
    )
    (got_g6,), (out_own, out_oth) = together([sync(copies)], [out_own, out_oth])

    def home(own, recv, others, cells, part_h):
        mores = [z.shape[1] // m for z in others]
        more = sum(mores)

        def kernel(geo, x, y, *refs):
            out, row = refs[-1], cells
            for z, count in zip(refs[:-1], mores, strict=True):
                for j in range(img_dev):
                    out[j, row : row + count, :] = z[j // m, (j % m) * count : (j % m + 1) * count]
                row += count
            for k in range(m):
                rows = slice(k * cells, (k + 1) * cells)
                for j in range(no):
                    part = slice(j * part_h, (j + 1) * part_h)
                    out[j * m + k, :cells, at(part_h, geo[2])] = x[rows, part]
                    out[j * m + k, :cells, at(part_h, 1 - geo[2])] = y[rows, part]

        shape = (img_dev, cells + more, 2 * part_h)
        return run(kernel, [(shape, BF16)], [geo], own, recv, *others)[0]

    def home_sides(own, recv):
        def kernel(geo, x, y, out):
            for j in range(no):
                part = slice(j * out_h, (j + 1) * out_h)
                for k in range(m):
                    rows = slice(k * cout, (k + 1) * cout)
                    out[j, at(cout, 2 * k + geo[2]), :] = x[rows, part]
                    out[j, at(cout, 2 * k + 1 - geo[2]), :] = y[rows, part]

        return run(kernel, [((no, pair * cout, out_h), BF16)], [geo], own, recv)[0]

    def back(dy, xhat, gain, st, valid, total, row, shift_row, count):
        shift_sum, gain_sum = total[shift_row : shift_row + 1], total[row : row + 1]
        return (
            gain * st[1] * (dy - valid * ((shift_sum + xhat * gain_sum) / count))
        ).astype(BF16)

    def back_six(geo, counts, dy, z, got, grads, pw, w, dz, own, oth, total):
        st = moments(got, counts, 1)
        total[...] = jnp.sum(grads[...], 0)
        xhat = (z[...] - st[0]) * st[1]
        dz[...] = back(dy[...], xhat, pw[2:3], st, out_mask(geo), total, 1, 0, counts[1])
        own[...] = mm_nt(dz[...], w[at(mh, geo[2]), :])
        oth[...] = mm_nt(dz[...], w[at(mh, 1 - geo[2]), :])

    dz_six, da_own, da_oth, sum_six = run(
        back_six,
        [wide_b, mid_f, mid_f, ((2, wide), F32)],
        [geo, counts],
        dy_six,
        z_six,
        got_six,
        got_g6,
        pw,
        w_e2,
    )

    def mid_dy(row, own, recv, z, got):
        def kernel(geo, counts, x, y, z, got, pm, dy, copies):
            st = moments(got, counts, 1)
            xhat = (z[...] - st[0]) * st[1]
            rise = gelu_slope(xhat * pm[row : row + 1] + pm[row + 4 : row + 5])
            dy[...] = (x[...] + y[...]) * (out_mask(geo) * rise)
            send_all(copies, dy_sums(dy[...], xhat))

        dy, copies = run(
            kernel, [mid_f, copies_shape(2, mh)], [geo, counts], own, recv, z, got, pm
        )
        return dy, copies

    def mid_dz(row, dy, z, got, grads):
        which = 0 if row == 0 else 1

        def kernel(geo, counts, dy, z, got, grads, pm, dz, total):
            st = moments(got, counts, which)
            total[...] = jnp.sum(grads[...], 0)
            xhat = (z[...] - st[0]) * st[1]
            valid = in_mask(geo) if row == 0 else out_mask(geo)
            dz[...] = back(
                dy[...], xhat, pm[row : row + 1], st, valid, total, 1, 0, counts[which]
            )

        dz, total = run(
            kernel, [(z.shape, BF16), ((2, mh), F32)], [geo, counts], dy, z, got, grads, pm
        )
        return dz, core_swap(dz), total

    dy_five, copies = mid_dy(3, da_own, core_swap(da_oth), z_five, got_five)
    got_g5 = sync(copies)
    dz_own, dz_recv, sum_five = mid_dz(3, dy_five, z_five, got_five, got_g5)

    def four_dy(geo, counts, x, y, z, got, pm, w, full, dy, copies, moved):
        join_to(full, geo, x, y)
        total = None
        for tap, (p, r) in enumerate(TAPS):
            key = (1 - p, 1 - r)
            if key == (0, 0):
                left = full[...]
            else:
                move = shift(*key)
                for k in range(pair):
                    rows = slice(k * cout, (k + 1) * cout)
                    moved[rows, :] = mm(move, full[rows, :]).astype(BF16)
                left = moved[...]
            term = mm(left, w[:, tap * mh : (tap + 1) * mh])
            total = term if total is None else total + term
        st = moments(got, counts, 1)
        xhat = (z[...] - st[0]) * st[1]
        dy[...] = total * (out_mask(geo) * gelu_slope(xhat * pm[2:3] + pm[6:7]))
        send_all(copies, dy_sums(dy[...], xhat))

    dz_five, dy_four, copies = run(
        four_dy,
        [((rout, mid), BF16), mid_f, copies_shape(2, mh)],
        [geo, counts],
        dz_own,
        dz_recv,
        z_four,
        got_four,
        pm,
        w_t2,
        scratch=[pltpu.VMEM((rout, mid), BF16)],
    )
    (got_g4,), ops_te = together([sync(copies)], [dz_five, win_two, act_five, dz_six])
    group_te = scatter_far(
        *blocks_of([(shape_t, 0, 1), ((mid, wide), 2, 3)], makers_3, ops_te)
    )
    dz_own, dz_recv, sum_four = mid_dz(2, dy_four, z_four, got_four, got_g4)

    def joined_dy(geo, counts, x, y, w, dy6, slope, z3, zs, got, full, dy, copies):
        join_to(full, geo, x, y)
        dy[...] = (dy6[...] + mm_nt(full[...], w[...])) * slope[...]
        st3, sts = moments(got, counts, 1), moments(got, counts, 1, 2)
        send_all(
            copies,
            dy_sums(dy[...], (z3[...] - st3[0]) * st3[1], (zs[...] - sts[0]) * sts[1]),
        )

    dz_four, dy_joined, copies = run(
        joined_dy,
        [((rout, mid), BF16), wide_f, copies_shape(3, wide)],
        [geo, counts],
        dz_own,
        dz_recv,
        w_r2,
        dy_six,
        slope_one,
        z_three,
        z_short,
        got_three,
    )
    (copies,), group_te = together([copies], group_te)
    (got_g3,), group_te = together([sync(copies)], group_te)
    group_te = scatter_near(*scatter_add(*group_te))

    def back_three(geo, counts, dy, z3, zs, got, grads, pw, w, dz3, dzs, own, oth, total):
        st3, sts = moments(got, counts, 1), moments(got, counts, 1, 2)
        total[...] = jnp.sum(grads[...], 0)
        valid = out_mask(geo)
        x3, xs = (z3[...] - st3[0]) * st3[1], (zs[...] - sts[0]) * sts[1]
        dz3[...] = back(dy[...], x3, pw[0:1], st3, valid, total, 1, 0, counts[1])
        dzs[...] = back(dy[...], xs, pw[1:2], sts, valid, total, 2, 0, counts[1])
        own[...] = mm_nt(dz3[...], w[at(mh, geo[2]), :])
        oth[...] = mm_nt(dz3[...], w[at(mh, 1 - geo[2]), :])

    dz_three, dz_short, da_own, da_oth, sum_three = run(
        back_three,
        [wide_b, wide_b, mid_f, mid_f, ((3, wide), F32)],
        [geo, counts],
        dy_joined,
        z_three,
        z_short,
        got_three,
        got_g3,
        pw,
        w_e1,
    )
    dy_two, copies = mid_dy(1, da_own, core_swap(da_oth), z_two, got_two)
    got_g2 = sync(copies)

    def short_back(geo, dz, w, own, oth):
        me = geo[2]
        for j in range(no):
            part = slice(j * in_h, (j + 1) * in_h)
            rows = pl.ds(pl.multiple_of(j * in_part + me * in_h, in_h), in_h)
            own[:, part] = mm_nt(dz[...], w[rows, :])
            rows = pl.ds(pl.multiple_of(j * in_part + (1 - me) * in_h, in_h), in_h)
            oth[:, part] = mm_nt(dz[...], w[rows, :])

    dz_own, dz_recv, sum_two = mid_dz(1, dy_two, z_two, got_two, got_g2)
    (dz_own,), group_te = together([dz_own], group_te)

    def one_dy(geo, counts, x, y, z, got, pm, w, full, dy, copies, moved):
        join_to(full, geo, x, y)
        for n, key in enumerate([(0, 1), (1, 0), (1, 1)]):
            move = shift(*key)
            for k in range(pair):
                rows = slice(k * cout, (k + 1) * cout)
                moved[n, rows, :] = mm(move, full[rows, :]).astype(BF16)
        for plane in range(4):
            total = None
            for p in (1,) if plane < 2 else (0, 2):
                for r in (1,) if plane % 2 == 0 else (0, 2):
                    n = 2 * int(p == 0) + int(r == 0)
                    left = full[...] if n == 0 else moved[n - 1]
                    tap = 3 * p + r
                    term = mm(left, w[:, tap * mh : (tap + 1) * mh])
                    total = term if total is None else total + term
            for k in range(pair):
                dy[k * cin + plane * cout : k * cin + (plane + 1) * cout, :] = total[
                    k * cout : (k + 1) * cout
                ]
        st = moments(got, counts, 0)
        xhat = (z[...] - st[0]) * st[1]
        dy[...] = dy[...] * (in_mask(geo) * gelu_slope(xhat * pm[0:1] + pm[4:5]))
        send_all(copies, dy_sums(dy[...], xhat))

    dz_two, dy_one, copies = run(
        one_dy,
        [((rout, mid), BF16), ((rin, mh), F32), copies_shape(2, mh)],
        [geo, counts],
        dz_own,
        dz_recv,
        z_one,
        got_one,
        pm,
        w_t1,
        scratch=[pltpu.VMEM((3, rout, mid), BF16)],
    )
    (got_g1,), ops = together(
        [sync(copies)],
        [dz_short, hidden_low, dz_four, act_two, dz_three, strided, dz_two, win_one],
    )
    dz_short = ops[0]
    ops_es, ops_t1 = ops[1:6] + ops[:1], ops[6:]
    ds_own, ds_oth = run(short_back, [((rout, kin), F32)] * 2, [geo], dz_short, w_s)
    ds_recv = core_swap(ds_oth)
    dz_own, dz_recv, sum_one = mid_dz(0, dy_one, z_one, got_one, got_g1)
    group_es = blocks_of(
        [((wide, mid), 0, 1), ((mid, wide), 2, 3), ((no * in_part, wide), 4, 5)],
        [make_r2] + makers_2,
        ops_es,
    )
    (dz_own,), group_es, group_te, outs = together(
        [dz_own], group_es, group_te, [out_own, out_oth]
    )
    group_es = scatter_far(*group_es)
    below = home_sides(outs[0], core_swap(outs[1]))

    def images_kernel(geo, x, y, w, ds, dr, full, own, oth, rows_in):
        join_to(full, geo, x, y)
        me = geo[2]
        for k in range(pair):
            rows = slice(k * cin, (k + 1) * cin)
            first = slice(k * cin, k * cin + cout)
            rest = slice(k * cin + cout, (k + 1) * cin)
            outs = slice(k * cout, (k + 1) * cout)
            rows_in[first, :] = (
                mm_nt(full[first, :], w[...]) + (ds[outs, :] + dr[outs, :])
            ).astype(BF16)
            rows_in[rest, :] = mm_nt(full[rest, :], w[...]).astype(BF16)
        for k in range(m):
            rows = slice(k * cin, (k + 1) * cin)
            for ref, img in ((oth, (1 - me) * m + k), (own, me * m + k)):
                ref[rows, :] = mm(order(geo, img, 1), rows_in[at(cin, img), :]).astype(BF16)

    dz_one, d_own, d_oth = run(
        images_kernel,
        [((rin, mid), BF16), ((m * cin, kin), BF16), ((m * cin, kin), BF16)],
        [geo],
        dz_own,
        dz_recv,
        w_r1,
        ds_own,
        ds_recv,
        scratch=[pltpu.VMEM((rin, kin), BF16)],
    )
    d_rows = home(d_own, core_swap(d_oth), [below, scatter_sum(group_te)], cin, in_h)
    (d_rows,), group_es, ops = together([d_rows], group_es, [masked, dz_one] + ops_t1)
    near = to_images(d_rows)
    group_es = scatter_near(*scatter_add(*group_es))
    group_t1 = scatter_far(*blocks_of([(shape_t, 0, 1)], [taps_entries], ops[2:]))
    group_r1 = blocks_of([((kin, mid), 0, 1)], [make_r1], ops[:2], split=False)
    group_t1 = scatter_near(*scatter_add(*group_t1))
    group_r1 = scatter_inner(*group_r1)

    rows_t = 9 * mid_io
    last = scatter_sum(group_es, group_t1, group_r1)
    (near,), (last,), totals = together(
        [near], [last], [sum_one, sum_two, sum_four, sum_five, sum_three, sum_six]
    )
    sum_one, sum_two, sum_four, sum_five, sum_three, sum_six = totals
    last = to_images(last)
    grad_images = near[:, :cin].astype(F32).reshape(images.shape)
    block_output = jnp.concatenate(
        [near[:, cin : cin + cout], near[:, cin + cout : cin + 2 * cout]], 2
    ).reshape(img_dev, ho, wo, out_part)
    parts_te = near[:, cin + 2 * cout :].reshape(no, -1, lanes)
    rows_es = group_es[0].shape[1]
    half_te = scatter_last(*[parts_te[k] for k in range(no)])
    half_rest = scatter_last(*[last[k] for k in range(no)])

    def both(half, first, count, axis):
        own, recv = half[0][first : first + count], half[1][first : first + count]
        return pick(jnp.concatenate([own, recv], axis), jnp.concatenate([recv, own], axis))

    def stacked(half, first, count):
        w = lanes // 2
        own, recv = half[0][first : first + count], half[1][first : first + count]
        own = jnp.concatenate([own[:, :w], own[:, w:]], 0)
        recv = jnp.concatenate([recv[:, :w], recv[:, w:]], 0)
        return pick(jnp.concatenate([own, recv], 0), jnp.concatenate([recv, own], 0))

    def taps_out(half, first):
        rows = both(half, first, rows_t, 1).reshape(9, mid_io, mid)
        return rows.transpose(0, 2, 1).reshape(first_taps.shape)

    rows_r1, rows_r2 = in_h // 2, out_h // 2
    mids = jnp.stack([sum_one, sum_two, sum_four, sum_five], 1)
    mids = swap_full(mids, 2)
    wides = jnp.concatenate([sum_three, sum_six], 0).reshape(5, no, out_h)
    wides = swap_full(wides, 2).reshape(5, no * out_part)
    return (
        block_output,
        grad_images,
        stacked(half_rest, rows_es + rows_t, rows_r1),
        taps_out(half_rest, rows_es),
        both(half_rest, rows_r2, mid_i, 1),
        both(half_rest, rows_r2 + mid_i, in_part, 1),
        stacked(half_rest, 0, rows_r2),
        taps_out(half_te, 0),
        both(half_te, rows_t, mid_i, 1),
        mids[1],
        mids[0],
        jnp.stack([wides[1], wides[2], wides[4]]),
        jnp.stack([wides[0], wides[0], wides[3]]),
    )


def solution(mesh):
    wide = P(("batch", "inner"), None, None, "outer")
    down = P("outer", "inner")
    up = P("inner", "outer")
    taps = P(None, None, None, ("inner", "outer"))
    whole = P()
    return jax.shard_map(
        shards,
        mesh=mesh,
        in_specs=(wide, whole, down, taps, up, down, down, taps, up)
        + (whole, whole, whole, whole, wide),
        out_specs=(wide, wide, down, taps, up, down, down, taps, up, whole, whole, whole, whole),
        check_vma=False,
    )
```

```python
import math

import jax
import jax.numpy as jnp
from jax import lax
from jax.experimental import pallas as pl
from jax.experimental.pallas import tpu as pltpu
from jax.sharding import PartitionSpec as P

EPS = 1e-05
ROOT = math.sqrt(2.0 / math.pi)
CUBE = 0.044715
F32 = jnp.float32
BF16 = jnp.bfloat16
XS = [(k, k ^ 1) for k in range(4)]
YS = [(k, k ^ 2) for k in range(4)]
DS = [(k, k ^ 3) for k in range(4)]
FAR = 3
GEO = 3
TAPS = [(p, r) for p in range(3) for r in range(3)]


def mm(left, right):
    return lax.dot_general(left, right, (((1,), (0,)), ((), ())), preferred_element_type=F32)


def mm_nt(left, right):
    return lax.dot_general(left, right, (((1,), (1,)), ((), ())), preferred_element_type=F32)


def mm_tn(left, right):
    return lax.dot_general(left, right, (((0,), (0,)), ((), ())), preferred_element_type=F32)


def gelu(v):
    return 0.5 * v * (1.0 + jnp.tanh(ROOT * (v + CUBE * v * v * v)))


def gelu_both(v):
    t = jnp.tanh(ROOT * (v + CUBE * v * v * v))
    half = 0.5 * (1.0 + t)
    return v * half, half + 0.5 * v * (1.0 - t * t) * (ROOT * (1.0 + 3.0 * CUBE * v * v))


def gelu_slope(v):
    return gelu_both(v)[1]


def halves(x, k):
    if k & (k - 1) == 0:
        s = k.bit_length() - 1
        return lax.shift_right_logical(x, jnp.int32(s)), lax.bitwise_and(x, jnp.int32(k - 1))
    return lax.div(x, jnp.int32(k)), lax.rem(x, jnp.int32(k))


def at(unit, index, size=None):
    return pl.ds(pl.multiple_of(index * unit, unit), unit if size is None else size)


def after(x, *done):
    return lax.optimization_barrier((x, done))[0]


def together(*groups):
    flat = [x for g in groups for x in g]
    flat = list(lax.optimization_barrier(tuple(flat)))
    out = []
    for g in groups:
        out.append(flat[: len(g)])
        flat = flat[len(g) :]
    return out


def run(kernel, outs, smem, *arrays, scratch=(), flops=0, limit=20 << 20):
    shapes = [jax.ShapeDtypeStruct(s, d) for s, d in outs]
    moved = sum(a.size * a.dtype.itemsize for a in arrays)
    moved += sum(math.prod(s) * jnp.dtype(d).itemsize for s, d in outs)
    return pl.pallas_call(
        kernel,
        out_shape=shapes,
        in_specs=[pl.BlockSpec(memory_space=pltpu.SMEM)] * len(smem)
        + [pl.BlockSpec(memory_space=pltpu.VMEM)] * len(arrays),
        out_specs=[pl.BlockSpec(memory_space=pltpu.VMEM)] * len(outs),
        scratch_shapes=list(scratch),
        compiler_params=pltpu.CompilerParams(vmem_limit_bytes=limit),
        cost_estimate=pl.CostEstimate(flops=flops, bytes_accessed=moved, transcendentals=0),
    )(*smem, *arrays)


def shards(
    images,
    extents,
    first_reduce,
    first_taps,
    first_expand,
    first_shortcut,
    second_reduce,
    second_taps,
    second_expand,
    mid_gains,
    mid_shifts,
    wide_gains,
    wide_shifts,
    cotangent,
):
    nb = lax.axis_size("batch")
    ni = lax.axis_size("inner")
    no = lax.axis_size("outer")
    b = lax.axis_index("batch")
    i = lax.axis_index("inner")
    o = lax.axis_index("outer")
    c = b % 2
    img_dev, hi, wi, in_part = images.shape
    ho, wo = hi // 2, wi // 2
    out_part = cotangent.shape[3]
    m = img_dev // no
    pair = 2 * m
    cin, cout = hi * wi, ho * wo
    rin, rout = pair * cin, pair * cout
    mid = mid_gains.shape[1]
    mh = mid // 2
    in_h = in_part // 2
    out_h = out_part // 2
    kin = no * in_h
    wide = no * out_h
    mid_i = mid // ni
    mid_io = mid // (ni * no)
    peers = ni * no
    lanes = out_h

    def core_swap(x):
        return lax.ppermute(x, "batch", [(k, k ^ 1) for k in range(nb)])

    def pick(low, high):
        return jnp.where(c == 0, low, high)

    def mine(x, axis):
        h = x.shape[axis] // 2
        return pick(lax.slice_in_dim(x, 0, h, axis=axis), lax.slice_in_dim(x, h, 2 * h, axis=axis))

    def other(x, axis):
        h = x.shape[axis] // 2
        return pick(lax.slice_in_dim(x, h, 2 * h, axis=axis), lax.slice_in_dim(x, 0, h, axis=axis))

    def swap_full(x, axis):
        recv = core_swap(x)
        return pick(jnp.concatenate([x, recv], axis), jnp.concatenate([recv, x], axis))

    def over_batch(x):
        total = x
        for k in range(1, nb // 2):
            total = total + lax.ppermute(x, "batch", [(j, (j + 2 * k) % nb) for j in range(nb)])
        return total

    def sync(copies):
        got = lax.all_to_all(copies, ("inner", "outer"), split_axis=0, concat_axis=0, tiled=True)
        return got if nb == 2 else over_batch(jnp.sum(got, 0, keepdims=True))

    def to_images(x):
        return lax.all_to_all(x, "outer", split_axis=0, concat_axis=0, tiled=True)

    def taps_entries(first, w):
        def entry(tap):
            place = lambda pi, po: (pi * no + po, mid_io, 0, tap, mh)
            return (first + tap * mid_io, mid_io, 0, mh, w, place)

        return [entry(tap) for tap in range(9)], 9 * mid_io

    def up_entries(first, w):
        place = lambda pi, po: (pi, mid_i, 0, po, out_h)
        return [(first, mid_i, 0, out_h, w, place)], mid_i

    def short_entries(first, w):
        quarter = in_part // 4

        def entry(k):
            place = lambda pi, po: (po, in_part, k * quarter, pi, out_h)
            return (first + k * quarter, quarter, 0, out_h, w, place)

        return [entry(k) for k in range(4)], in_part

    def down_entries(rows):
        def make(first, w):
            half = rows // 2

            def entry(side):
                place = lambda pi, po: (po, rows, side * half, pi, mid_i)
                return (first, half, side * mid_i, mid_i, w, place)

            return [entry(0), entry(1)], half

        return make

    def table(makers):
        entries, first = [], 0
        for w, make in enumerate(makers):
            got, used = make(first, w)
            entries += got
            first += used
        return entries, first

    def middle(makers):
        entries, rows = table(makers)
        return min(first + count for first, count, *_ in entries if 2 * (first + count) >= rows)

    def region(place, pi, po, count, width):
        row, row_unit, plus, col, col_unit = place(pi, po)
        return (
            pl.ds(pl.multiple_of(row * row_unit, row_unit) + plus, count),
            pl.ds(pl.multiple_of(col * col_unit, col_unit), width),
        )

    place_io = jnp.stack([i, o]).astype(jnp.int32)

    def shifted(x, k):
        return lax.ppermute(x, "outer", [(j, (j + k) % no) for j in range(no)])

    def along_outer(shard):
        return [shard] + [shifted(shard, k) for k in range(1, no)]

    def along_inner(pieces):
        whole = jnp.stack(pieces)
        return [whole] + [lax.ppermute(whole, "inner", perm) for perm in (XS, YS, DS)]

    def along_near(pieces):
        def kernel(*refs):
            for k in range(no):
                refs[no][k] = refs[k][...]

        (whole,) = run(kernel, [((no,) + pieces[0].shape, BF16)], [], *pieces)
        return whole, lax.ppermute(whole, "inner", XS), lax.ppermute(whole, "inner", YS)

    def along_far(whole, by_x, by_y, h):
        def kernel(x, y, low, high):
            low[...] = x[:, :h]
            high[...] = y[:, h:]

        rows, cols = whole.shape[1:]
        low, high = run(
            kernel, [((no, h, cols), BF16), ((no, rows - h, cols), BF16)], [], by_x, by_y
        )
        low, high = lax.ppermute(low, "inner", YS), lax.ppermute(high, "inner", XS)
        return whole, by_x, by_y, low, high

    def assembled(parts, makers, shapes):
        entries, _ = table(makers)
        h = middle(makers)

        def kernel(where, *refs):
            sources, targets = refs[: len(parts)], refs[len(parts) :]
            for far in range(ni):
                for d in range(no):
                    pi, po = where[0] ^ far, lax.rem(where[1] + (no - d), no)
                    for first, count, lane, width, w, place in entries:
                        source, start = sources[far], first
                        if len(parts) > ni and far == FAR and first >= h:
                            source, start = sources[ni], first - h
                        targets[w][region(place, pi, po, count, width)] = source[
                            d, start : start + count, lane : lane + width
                        ]

        return run(kernel, [(s, BF16) for s in shapes], [place_io], *parts)

    def blocks_of(products, makers, operands, split=True):
        entries, rows = table(makers)
        h = middle(makers)
        sizes = [rows, rows, rows] + ([h, rows - h] if split else [rows])
        n = len(operands)

        def kernel(where, *refs):
            ins, outs, grads = refs[:n], refs[n : n + len(sizes)], refs[n + len(sizes) :]
            for grad, (_, left, right) in zip(grads, products, strict=True):
                grad[...] = mm_tn(ins[left][...], ins[right][...]).astype(BF16)
            for far in range(ni):
                for po in range(no):
                    pi = where[0] ^ far
                    for first, count, lane, width, w, place in entries:
                        out, start = outs[far], first
                        if split and far == FAR and first >= h:
                            out, start = outs[ni], first - h
                        out[po, start : start + count, lane : lane + width] = grads[w][
                            region(place, pi, po, count, width)
                        ]

        return run(
            kernel,
            [((no, r, lanes), BF16) for r in sizes],
            [place_io],
            *operands,
            scratch=[pltpu.VMEM(prod[0], BF16) for prod in products],
        )

    def scatter_far(own, to_x, to_y, low, high):
        return own, to_x, to_y, lax.ppermute(low, "inner", XS), lax.ppermute(high, "inner", YS)

    def scatter_add(own, to_x, to_y, low, high):
        h = low.shape[1]

        def kernel(x, y, a, z, out_x, out_y):
            out_x[:, :h] = x[:, :h]
            out_x[:, h:] = (x[:, h:].astype(F32) + z[...].astype(F32)).astype(BF16)
            out_y[:, :h] = (y[:, :h].astype(F32) + a[...].astype(F32)).astype(BF16)
            out_y[:, h:] = y[:, h:]

        return [own] + list(run(kernel, [(own.shape, BF16)] * 2, [], to_x, to_y, low, high))

    def scatter_near(own, to_x, to_y):
        return [own, lax.ppermute(to_x, "inner", XS), lax.ppermute(to_y, "inner", YS)]

    def scatter_inner(own, *sends):
        return [own] + [
            lax.ppermute(x, "inner", perm) for x, perm in zip(sends, (XS, YS, DS), strict=True)
        ]

    def scatter_sum(*groups):
        rows = [g[0].shape[1] for g in groups]

        def kernel(*refs):
            row, refs, out = 0, list(refs[:-1]), refs[-1]
            for g, count in zip(groups, rows, strict=True):
                mine, refs = refs[: len(g)], refs[len(g) :]
                total = mine[0][...].astype(F32)
                for ref in mine[1:]:
                    total = total + ref[...].astype(F32)
                out[:, row : row + count, :] = total.astype(BF16)
                row += count

        flat = [x for g in groups for x in g]
        return run(kernel, [((no, sum(rows), lanes), BF16)], [], *flat)[0]

    def scatter_last(*parts):
        def kernel(*refs):
            total = refs[0][...].astype(F32)
            for ref in refs[1:-1]:
                total = total + ref[...].astype(F32)
            refs[-1][...] = total

        half = over_batch(run(kernel, [(parts[0].shape, F32)], [], *parts)[0])
        return half, core_swap(half)

    first_img = ((b - c) * ni + i) * img_dev + o * m
    ext = jnp.concatenate(
        [
            lax.dynamic_slice_in_dim(extents, first_img, m, 0),
            lax.dynamic_slice_in_dim(extents, first_img + ni * img_dev, m, 0),
        ],
        0,
    )
    geo = jnp.concatenate([jnp.stack([i, o, c]), ext[:, 0], ext[:, 1]]).astype(jnp.int32)
    area = jnp.sum(extents[:, 0] * extents[:, 1]).astype(F32)
    counts = jnp.stack([4.0 * area, area])

    def iota(shape, axis):
        return lax.broadcasted_iota(jnp.int32, shape, axis)

    def out_mask(geo):
        row, col = halves(iota((cout, 1), 0), wo)
        return jnp.concatenate(
            [
                ((row < geo[GEO + k]) & (col < geo[GEO + pair + k])).astype(F32)
                for k in range(pair)
            ],
            0,
        )

    def phase_cells(shape, axis):
        phase, cell = halves(iota(shape, axis), cout)
        row, col = halves(cell, wo)
        up, left = halves(phase, 2)
        return 2 * row + up, 2 * col + left

    def in_mask(geo):
        row, col = phase_cells((cin, 1), 0)
        return jnp.concatenate(
            [
                ((row < 2 * geo[GEO + k]) & (col < 2 * geo[GEO + pair + k])).astype(F32)
                for k in range(pair)
            ],
            0,
        )

    def order(geo, k, axis):
        shape = (cin, 1) if axis == 0 else (1, cin)
        row, col = phase_cells(shape, axis)
        inside = (row < 2 * geo[GEO + k]) & (col < 2 * geo[GEO + pair + k])
        source = jnp.where(inside, row * wi + col, -1)
        return (source == iota((cin, cin), 1 - axis)).astype(F32).astype(BF16)

    def shift(dr, dc):
        row, col = halves(iota((cout, 1), 0), wo)
        row, col = row + dr, col + dc
        inside = (row >= 0) & (row < ho) & (col >= 0) & (col < wo)
        source = jnp.where(inside, row * wo + col, -1)
        return (source == iota((cout, cout), 1)).astype(F32).astype(BF16)

    def taps_shard(w):
        return mine(w, 2).transpose(0, 1, 3, 2).reshape(9 * mid_io, mh)

    def side_by_side(w):
        h = w.shape[0] // 2
        return jnp.concatenate([w[:h], w[h:]], 1)

    make_r1, make_r2 = down_entries(in_h), down_entries(out_h)
    shape_t = (mid, 9 * mh)
    makers_1 = [make_r1, taps_entries, make_r2]
    makers_2 = [up_entries, short_entries]
    makers_3 = [taps_entries, up_entries]
    shard_1 = jnp.concatenate(
        [
            side_by_side(mine(first_reduce, 0)),
            taps_shard(first_taps),
            side_by_side(mine(second_reduce, 0)),
        ],
        0,
    )
    shard_2 = jnp.concatenate([mine(first_expand, 1), mine(first_shortcut, 1)], 0)
    shard_3 = jnp.concatenate([taps_shard(second_taps), mine(second_expand, 1)], 0)
    def both_cores(x):
        own, recv = mine(x, 2), core_swap(other(x, 2))
        return jnp.stack([pick(own, recv), pick(recv, own)], 1)

    both_rows = both_cores(images.reshape(img_dev, cin, in_part))
    cot_rows = both_cores(cotangent.reshape(img_dev, cout, out_part)).reshape(
        no, m, 2, cout, out_h
    )
    cots = [
        lax.dynamic_index_in_dim(cot_rows, (o + k) % no, 0, keepdims=False).reshape(
            pair * cout, out_h
        )
        for k in range(no)
    ]
    pieces_1, (shard_2, shard_3), (both_rows,), cots = together(
        along_outer(shard_1), [shard_2, shard_3], [both_rows], cots
    )
    parts_1, pieces_2, (both_rows,) = together(
        along_near(pieces_1), along_outer(shard_2), [both_rows]
    )
    parts_1 = along_far(*parts_1, middle(makers_1))
    got_rows = to_images(both_rows)
    parts_1, pieces_2 = together(parts_1, pieces_2)
    (got_rows,), parts_2 = together([got_rows], along_near(pieces_2))
    w_r1, w_t1, w_r2 = assembled(parts_1, makers_1, [(kin, mid), shape_t, (wide, mid)])

    pm = mine(jnp.concatenate([mid_gains, mid_shifts], 0), 1)
    pw = mine(
        jnp.concatenate([wide_gains, wide_shifts], 0).reshape(6, no, out_part), 2
    ).reshape(6, wide)
    (got_rows,), (pm, pw, counts, geo), cots = together([got_rows], [pm, pw, counts, geo], cots)
    cots = cots[:1] + [shifted(x, k) for k, x in enumerate(cots) if k]

    def moments(got, counts, which, row=0):
        total = jnp.sum(got[...], 0)
        mean = total[row : row + 1] / counts[which]
        square = total[row + 1 : row + 2] / counts[which]
        return mean, lax.rsqrt(square - mean * mean + EPS)

    def send_all(copies, rows):
        value = jnp.concatenate(rows, 0)
        for k in range(peers):
            copies[k] = value

    def sums(z, valid=None):
        zv = z if valid is None else z * valid
        return [jnp.sum(zv, 0, keepdims=True), jnp.sum(zv * z, 0, keepdims=True)]

    def copies_shape(rows, width):
        return ((peers, rows, width), F32)

    mid_f = ((rout, mh), F32)
    wide_f = ((rout, wide), F32)
    wide_b = ((rout, wide), BF16)
    mid_b = ((rout, mh), BF16)

    def one_kernel(geo, got, w, masked, strided, own, oth, raw):
        me = geo[2]
        for k in range(m):
            for j in range(no):
                for p in range(2):
                    raw[p * m + k, :, j * in_h : (j + 1) * in_h] = got[j * m + k, p, :cin, :]
        for k in range(pair):
            rows = slice(k * cin, (k + 1) * cin)
            masked[rows, :] = mm(order(geo, k, 0), raw[k]).astype(BF16)
            strided[k * cout : (k + 1) * cout, :] = masked[k * cin : k * cin + cout, :]
        own[...] = mm(masked[...], w[:, at(mh, me)])
        oth[...] = mm(masked[...], w[:, at(mh, 1 - me)])

    masked, strided_h, z_own, z_oth = run(
        one_kernel,
        [((rin, kin), BF16), ((rout, kin), BF16), ((rin, mh), F32), ((rin, mh), F32)],
        [geo],
        got_rows,
        w_r1,
        scratch=[pltpu.VMEM((pair, cin, kin), BF16)],
    )

    def one_sums(x, y, z, copies):
        z[...] = x[...] + y[...]
        send_all(copies, sums(z[...]))

    z_one, copies = run(
        one_sums, [((rin, mh), F32), copies_shape(2, mh)], [], z_own, core_swap(z_oth)
    )
    (copies,), parts_2, (shard_3,), cots = together([copies], parts_2, [shard_3], cots)
    (got_one,), parts_2, (shard_3,) = together([sync(copies)], parts_2, [shard_3])
    parts_2 = along_far(*parts_2, middle(makers_2))
    pieces_3 = along_outer(shard_3)

    def mid_sums(geo, x, y, z, copies):
        z[...] = x[...] + y[...]
        send_all(copies, sums(z[...], out_mask(geo)))

    def mid_partial(kernel, z, got, w):
        win, own, oth = run(
            kernel,
            [((rout, 9 * mh), BF16), mid_f, mid_f],
            [geo, counts],
            z,
            got,
            pm,
            w,
            scratch=[pltpu.VMEM(z.shape, BF16)],
        )
        z_next, copies = run(
            mid_sums, [mid_f, copies_shape(2, mh)], [geo], own, core_swap(oth)
        )
        return win, z_next, copies

    def normed(z, st, gains, g, s):
        return (z - st[0]) * st[1] * gains[g : g + 1] + gains[s : s + 1]

    def two_kernel(geo, counts, z, got, pm, w, win, own, oth, act):
        st = moments(got, counts, 0)
        act[...] = (gelu(normed(z[...], st, pm, 0, 4)) * in_mask(geo)).astype(BF16)
        moves = {}
        for tap, (p, r) in enumerate(TAPS):
            key = (-int(p == 0), -int(r == 0))
            plane = 2 * int(p != 1) + int(r != 1)
            if key != (0, 0) and key not in moves:
                moves[key] = shift(*key)
            for k in range(pair):
                x = act[k * cin + plane * cout : k * cin + (plane + 1) * cout, :]
                if key != (0, 0):
                    x = mm(moves[key], x).astype(BF16)
                win[k * cout : (k + 1) * cout, tap * mh : (tap + 1) * mh] = x
        own[...] = mm_nt(win[...], w[at(mh, geo[2]), :])
        oth[...] = mm_nt(win[...], w[at(mh, 1 - geo[2]), :])

    win_one, z_two, copies = mid_partial(two_kernel, z_one, got_one, w_t1)
    (got_two,), parts_2, pieces_3 = together([sync(copies)], parts_2, pieces_3)
    parts_3 = along_near(pieces_3)
    w_e1, w_s = assembled(parts_2, makers_2, [(mid, wide), (no * in_part, wide)])

    strided_r = core_swap(strided_h)

    def short_kernel(geo, x, y, w, full, z):
        me = geo[2]
        for j in range(no):
            part = slice(j * in_h, (j + 1) * in_h)
            full[:, pl.ds(pl.multiple_of(j * in_part + me * in_h, in_h), in_h)] = x[:, part]
            full[:, pl.ds(pl.multiple_of(j * in_part + (1 - me) * in_h, in_h), in_h)] = y[:, part]
        z[...] = mm(full[...], w[...])

    strided, z_short = run(
        short_kernel, [((rout, no * in_part), BF16), wide_f], [geo], strided_h, strided_r, w_s
    )

    def act_of(row, z, got):
        def kernel(geo, counts, z, got, pm, act):
            st = moments(got, counts, 1)
            act[...] = (gelu(normed(z[...], st, pm, row, row + 4)) * out_mask(geo)).astype(BF16)

        (act,) = run(kernel, [mid_b], [geo, counts], z, got, pm)
        return act, core_swap(act)

    def join_to(full, geo, x, y):
        full[:, at(mh, geo[2])] = x[...]
        full[:, at(mh, 1 - geo[2])] = y[...]

    def three_kernel(geo, x, y, w, zs, full, z, copies):
        join_to(full, geo, x, y)
        z[...] = mm(full[...], w[...])
        send_all(copies, sums(z[...]) + sums(zs[...]))

    act_own, act_recv = act_of(1, z_two, got_two)
    act_two, z_three, copies = run(
        three_kernel,
        [((rout, mid), BF16), wide_f, copies_shape(4, wide)],
        [geo],
        act_own,
        act_recv,
        w_e1,
        z_short,
    )
    (got_three,), parts_3 = together([sync(copies)], parts_3)
    parts_3 = along_far(*parts_3, middle(makers_3))

    def four_kernel(geo, counts, z3, zs, got, pw, w, hidden, slope, low, own, oth):
        st3, sts = moments(got, counts, 1), moments(got, counts, 1, 2)
        joined = normed(z3[...], st3, pw, 0, 3) + normed(zs[...], sts, pw, 1, 4)
        value, rise = gelu_both(joined)
        valid = out_mask(geo)
        hidden[...] = value * valid
        slope[...] = rise * valid
        low[...] = hidden[...].astype(BF16)
        own[...] = mm(low[...], w[:, at(mh, geo[2])])
        oth[...] = mm(low[...], w[:, at(mh, 1 - geo[2])])

    hidden, slope_one, hidden_low, z_own, z_oth = run(
        four_kernel,
        [wide_f, wide_f, wide_b, mid_f, mid_f],
        [geo, counts],
        z_three,
        z_short,
        got_three,
        pw,
        w_r2,
    )
    z_four, copies = run(
        mid_sums, [mid_f, copies_shape(2, mh)], [geo], z_own, core_swap(z_oth)
    )
    (got_four,), parts_3 = together([sync(copies)], parts_3)
    w_t2, w_e2 = assembled(parts_3, makers_3, [shape_t, (mid, wide)])

    def five_kernel(geo, counts, z, got, pm, w, win, own, oth, act):
        st = moments(got, counts, 1)
        act[...] = (gelu(normed(z[...], st, pm, 2, 6)) * out_mask(geo)).astype(BF16)
        for tap, (p, r) in enumerate(TAPS):
            key = (p - 1, r - 1)
            move = None if key == (0, 0) else shift(*key)
            for k in range(pair):
                x = act[k * cout : (k + 1) * cout, :]
                if move is not None:
                    x = mm(move, x).astype(BF16)
                win[k * cout : (k + 1) * cout, tap * mh : (tap + 1) * mh] = x
        own[...] = mm_nt(win[...], w[at(mh, geo[2]), :])
        oth[...] = mm_nt(win[...], w[at(mh, 1 - geo[2]), :])

    win_two, z_five, copies = mid_partial(five_kernel, z_four, got_four, w_t2)
    got_five = sync(copies)
    act_own, act_recv = act_of(3, z_five, got_five)

    def six_kernel(geo, x, y, w, full, z, copies):
        join_to(full, geo, x, y)
        z[...] = mm(full[...], w[...])
        send_all(copies, sums(z[...]))

    act_five, z_six, copies = run(
        six_kernel,
        [((rout, mid), BF16), wide_f, copies_shape(2, wide)],
        [geo],
        act_own,
        act_recv,
        w_e2,
    )
    (copies,), cots = together([copies], cots)
    got_six = sync(copies)

    def loss_kernel(geo, counts, z, got, pw, hidden, *refs):
        cots, (own, oth, dy, copies, value) = refs[:no], refs[no:]
        me = geo[2]
        st = moments(got, counts, 1)
        xhat = (z[...] - st[0]) * st[1]
        out, rise = gelu_both(xhat * pw[2:3] + pw[5:6] + hidden[...])
        valid = out_mask(geo)
        value[...] = (out * valid).astype(BF16)
        own[...] = value[at(m * cout, me), :]
        oth[...] = value[at(m * cout, 1 - me), :]
        for d in range(no):
            part = at(out_h, lax.rem(geo[1] + (no - d), no))
            for k in range(m):
                for p in range(2):
                    rows = slice((p * m + k) * cout, (p * m + k + 1) * cout)
                    source = slice((k * 2 + p) * cout, (k * 2 + p + 1) * cout)
                    dy[rows, part] = cots[d][source, :].astype(F32)
        dy[...] = dy[...] * (rise * valid)
        send_all(copies, dy_sums(dy[...], xhat))

    def dy_sums(dy, *xhats):
        return [jnp.sum(dy, 0, keepdims=True)] + [
            jnp.sum(dy * x, 0, keepdims=True) for x in xhats
        ]

    out_own, out_oth, dy_six, copies = run(
        loss_kernel,
        [((m * cout, wide), BF16), ((m * cout, wide), BF16), wide_f, copies_shape(2, wide)],
        [geo, counts],
        z_six,
        got_six,
        pw,
        hidden,
        *cots,
        scratch=[pltpu.VMEM((rout, wide), BF16)],
    )
    (got_g6,), (out_own, out_oth) = together([sync(copies)], [out_own, out_oth])

    def home(own, recv, others, cells, part_h):
        mores = [z.shape[1] // m for z in others]
        more = sum(mores)

        def kernel(geo, x, y, *refs):
            out, row = refs[-1], cells
            for z, count in zip(refs[:-1], mores, strict=True):
                for j in range(img_dev):
                    out[j, row : row + count, :] = z[j // m, (j % m) * count : (j % m + 1) * count]
                row += count
            for k in range(m):
                rows = slice(k * cells, (k + 1) * cells)
                for j in range(no):
                    part = slice(j * part_h, (j + 1) * part_h)
                    out[j * m + k, :cells, at(part_h, geo[2])] = x[rows, part]
                    out[j * m + k, :cells, at(part_h, 1 - geo[2])] = y[rows, part]

        shape = (img_dev, cells + more, 2 * part_h)
        return run(kernel, [(shape, BF16)], [geo], own, recv, *others)[0]

    def home_sides(own, recv):
        def kernel(geo, x, y, out):
            for j in range(no):
                part = slice(j * out_h, (j + 1) * out_h)
                for k in range(m):
                    rows = slice(k * cout, (k + 1) * cout)
                    out[j, at(cout, 2 * k + geo[2]), :] = x[rows, part]
                    out[j, at(cout, 2 * k + 1 - geo[2]), :] = y[rows, part]

        return run(kernel, [((no, pair * cout, out_h), BF16)], [geo], own, recv)[0]

    def back(dy, xhat, gain, st, valid, total, row, shift_row, count):
        shift_sum, gain_sum = total[shift_row : shift_row + 1], total[row : row + 1]
        return (
            gain * st[1] * (dy - valid * ((shift_sum + xhat * gain_sum) / count))
        ).astype(BF16)

    def back_six(geo, counts, dy, z, got, grads, pw, w, dz, own, oth, total):
        st = moments(got, counts, 1)
        total[...] = jnp.sum(grads[...], 0)
        xhat = (z[...] - st[0]) * st[1]
        dz[...] = back(dy[...], xhat, pw[2:3], st, out_mask(geo), total, 1, 0, counts[1])
        own[...] = mm_nt(dz[...], w[at(mh, geo[2]), :])
        oth[...] = mm_nt(dz[...], w[at(mh, 1 - geo[2]), :])

    dz_six, da_own, da_oth, sum_six = run(
        back_six,
        [wide_b, mid_f, mid_f, ((2, wide), F32)],
        [geo, counts],
        dy_six,
        z_six,
        got_six,
        got_g6,
        pw,
        w_e2,
    )

    def mid_dy(row, own, recv, z, got):
        def kernel(geo, counts, x, y, z, got, pm, dy, copies):
            st = moments(got, counts, 1)
            xhat = (z[...] - st[0]) * st[1]
            rise = gelu_slope(xhat * pm[row : row + 1] + pm[row + 4 : row + 5])
            dy[...] = (x[...] + y[...]) * (out_mask(geo) * rise)
            send_all(copies, dy_sums(dy[...], xhat))

        dy, copies = run(
            kernel, [mid_f, copies_shape(2, mh)], [geo, counts], own, recv, z, got, pm
        )
        return dy, copies

    def mid_dz(row, dy, z, got, grads):
        which = 0 if row == 0 else 1

        def kernel(geo, counts, dy, z, got, grads, pm, dz, total):
            st = moments(got, counts, which)
            total[...] = jnp.sum(grads[...], 0)
            xhat = (z[...] - st[0]) * st[1]
            valid = in_mask(geo) if row == 0 else out_mask(geo)
            dz[...] = back(
                dy[...], xhat, pm[row : row + 1], st, valid, total, 1, 0, counts[which]
            )

        dz, total = run(
            kernel, [(z.shape, BF16), ((2, mh), F32)], [geo, counts], dy, z, got, grads, pm
        )
        return dz, core_swap(dz), total

    dy_five, copies = mid_dy(3, da_own, core_swap(da_oth), z_five, got_five)
    got_g5 = sync(copies)
    dz_own, dz_recv, sum_five = mid_dz(3, dy_five, z_five, got_five, got_g5)

    def four_dy(geo, counts, x, y, z, got, pm, w, full, dy, copies, moved):
        join_to(full, geo, x, y)
        total = None
        for tap, (p, r) in enumerate(TAPS):
            key = (1 - p, 1 - r)
            if key == (0, 0):
                left = full[...]
            else:
                move = shift(*key)
                for k in range(pair):
                    rows = slice(k * cout, (k + 1) * cout)
                    moved[rows, :] = mm(move, full[rows, :]).astype(BF16)
                left = moved[...]
            term = mm(left, w[:, tap * mh : (tap + 1) * mh])
            total = term if total is None else total + term
        st = moments(got, counts, 1)
        xhat = (z[...] - st[0]) * st[1]
        dy[...] = total * (out_mask(geo) * gelu_slope(xhat * pm[2:3] + pm[6:7]))
        send_all(copies, dy_sums(dy[...], xhat))

    dz_five, dy_four, copies = run(
        four_dy,
        [((rout, mid), BF16), mid_f, copies_shape(2, mh)],
        [geo, counts],
        dz_own,
        dz_recv,
        z_four,
        got_four,
        pm,
        w_t2,
        scratch=[pltpu.VMEM((rout, mid), BF16)],
    )
    (got_g4,), ops_te = together([sync(copies)], [dz_five, win_two, act_five, dz_six])
    group_te = scatter_far(
        *blocks_of([(shape_t, 0, 1), ((mid, wide), 2, 3)], makers_3, ops_te)
    )
    dz_own, dz_recv, sum_four = mid_dz(2, dy_four, z_four, got_four, got_g4)

    def joined_dy(geo, counts, x, y, w, dy6, slope, z3, zs, got, full, dy, copies):
        join_to(full, geo, x, y)
        dy[...] = (dy6[...] + mm_nt(full[...], w[...])) * slope[...]
        st3, sts = moments(got, counts, 1), moments(got, counts, 1, 2)
        send_all(
            copies,
            dy_sums(dy[...], (z3[...] - st3[0]) * st3[1], (zs[...] - sts[0]) * sts[1]),
        )

    dz_four, dy_joined, copies = run(
        joined_dy,
        [((rout, mid), BF16), wide_f, copies_shape(3, wide)],
        [geo, counts],
        dz_own,
        dz_recv,
        w_r2,
        dy_six,
        slope_one,
        z_three,
        z_short,
        got_three,
    )
    (copies,), group_te = together([copies], group_te)
    (got_g3,), group_te = together([sync(copies)], group_te)
    group_te = scatter_near(*scatter_add(*group_te))

    def back_three(geo, counts, dy, z3, zs, got, grads, pw, w, dz3, dzs, own, oth, total):
        st3, sts = moments(got, counts, 1), moments(got, counts, 1, 2)
        total[...] = jnp.sum(grads[...], 0)
        valid = out_mask(geo)
        x3, xs = (z3[...] - st3[0]) * st3[1], (zs[...] - sts[0]) * sts[1]
        dz3[...] = back(dy[...], x3, pw[0:1], st3, valid, total, 1, 0, counts[1])
        dzs[...] = back(dy[...], xs, pw[1:2], sts, valid, total, 2, 0, counts[1])
        own[...] = mm_nt(dz3[...], w[at(mh, geo[2]), :])
        oth[...] = mm_nt(dz3[...], w[at(mh, 1 - geo[2]), :])

    dz_three, dz_short, da_own, da_oth, sum_three = run(
        back_three,
        [wide_b, wide_b, mid_f, mid_f, ((3, wide), F32)],
        [geo, counts],
        dy_joined,
        z_three,
        z_short,
        got_three,
        got_g3,
        pw,
        w_e1,
    )
    dy_two, copies = mid_dy(1, da_own, core_swap(da_oth), z_two, got_two)
    got_g2 = sync(copies)

    def short_back(geo, dz, w, own, oth):
        me = geo[2]
        for j in range(no):
            part = slice(j * in_h, (j + 1) * in_h)
            rows = pl.ds(pl.multiple_of(j * in_part + me * in_h, in_h), in_h)
            own[:, part] = mm_nt(dz[...], w[rows, :])
            rows = pl.ds(pl.multiple_of(j * in_part + (1 - me) * in_h, in_h), in_h)
            oth[:, part] = mm_nt(dz[...], w[rows, :])

    dz_own, dz_recv, sum_two = mid_dz(1, dy_two, z_two, got_two, got_g2)
    (dz_own,), group_te = together([dz_own], group_te)

    def one_dy(geo, counts, x, y, z, got, pm, w, full, dy, copies, moved):
        join_to(full, geo, x, y)
        for n, key in enumerate([(0, 1), (1, 0), (1, 1)]):
            move = shift(*key)
            for k in range(pair):
                rows = slice(k * cout, (k + 1) * cout)
                moved[n, rows, :] = mm(move, full[rows, :]).astype(BF16)
        for plane in range(4):
            total = None
            for p in (1,) if plane < 2 else (0, 2):
                for r in (1,) if plane % 2 == 0 else (0, 2):
                    n = 2 * int(p == 0) + int(r == 0)
                    left = full[...] if n == 0 else moved[n - 1]
                    tap = 3 * p + r
                    term = mm(left, w[:, tap * mh : (tap + 1) * mh])
                    total = term if total is None else total + term
            for k in range(pair):
                dy[k * cin + plane * cout : k * cin + (plane + 1) * cout, :] = total[
                    k * cout : (k + 1) * cout
                ]
        st = moments(got, counts, 0)
        xhat = (z[...] - st[0]) * st[1]
        dy[...] = dy[...] * (in_mask(geo) * gelu_slope(xhat * pm[0:1] + pm[4:5]))
        send_all(copies, dy_sums(dy[...], xhat))

    dz_two, dy_one, copies = run(
        one_dy,
        [((rout, mid), BF16), ((rin, mh), F32), copies_shape(2, mh)],
        [geo, counts],
        dz_own,
        dz_recv,
        z_one,
        got_one,
        pm,
        w_t1,
        scratch=[pltpu.VMEM((3, rout, mid), BF16)],
    )
    (got_g1,), ops = together(
        [sync(copies)],
        [dz_short, hidden_low, dz_four, act_two, dz_three, strided, dz_two, win_one],
    )
    dz_short = ops[0]
    ops_es, ops_t1 = ops[1:6] + ops[:1], ops[6:]
    ds_own, ds_oth = run(short_back, [((rout, kin), F32)] * 2, [geo], dz_short, w_s)
    ds_recv = core_swap(ds_oth)
    dz_own, dz_recv, sum_one = mid_dz(0, dy_one, z_one, got_one, got_g1)
    group_es = blocks_of(
        [((wide, mid), 0, 1), ((mid, wide), 2, 3), ((no * in_part, wide), 4, 5)],
        [make_r2] + makers_2,
        ops_es,
    )
    (dz_own,), group_es, group_te, outs = together(
        [dz_own], group_es, group_te, [out_own, out_oth]
    )
    group_es = scatter_far(*group_es)
    below = home_sides(outs[0], core_swap(outs[1]))

    def images_kernel(geo, x, y, w, ds, dr, full, own, oth, rows_in):
        join_to(full, geo, x, y)
        me = geo[2]
        for k in range(pair):
            rows = slice(k * cin, (k + 1) * cin)
            first = slice(k * cin, k * cin + cout)
            rest = slice(k * cin + cout, (k + 1) * cin)
            outs = slice(k * cout, (k + 1) * cout)
            rows_in[first, :] = (
                mm_nt(full[first, :], w[...]) + (ds[outs, :] + dr[outs, :])
            ).astype(BF16)
            rows_in[rest, :] = mm_nt(full[rest, :], w[...]).astype(BF16)
        for k in range(m):
            rows = slice(k * cin, (k + 1) * cin)
            for ref, img in ((oth, (1 - me) * m + k), (own, me * m + k)):
                ref[rows, :] = mm(order(geo, img, 1), rows_in[at(cin, img), :]).astype(BF16)

    dz_one, d_own, d_oth = run(
        images_kernel,
        [((rin, mid), BF16), ((m * cin, kin), BF16), ((m * cin, kin), BF16)],
        [geo],
        dz_own,
        dz_recv,
        w_r1,
        ds_own,
        ds_recv,
        scratch=[pltpu.VMEM((rin, kin), BF16)],
    )
    d_rows = home(d_own, core_swap(d_oth), [below, scatter_sum(group_te)], cin, in_h)
    (d_rows,), group_es, ops = together([d_rows], group_es, [masked, dz_one] + ops_t1)
    near = to_images(d_rows)
    group_es = scatter_near(*scatter_add(*group_es))
    group_t1 = scatter_far(
        *blocks_of([(shape_t, 2, 3), ((kin, mid), 0, 1)], [taps_entries, make_r1], ops)
    )
    group_t1, group_es = together(group_t1, group_es)
    group_t1 = scatter_near(*scatter_add(*group_t1))

    rows_t = 9 * mid_io
    last = scatter_sum(group_es, group_t1)
    (near,), (last,), totals = together(
        [near], [last], [sum_one, sum_two, sum_four, sum_five, sum_three, sum_six]
    )
    sum_one, sum_two, sum_four, sum_five, sum_three, sum_six = totals
    last = to_images(last)
    grad_images = near[:, :cin].astype(F32).reshape(images.shape)
    block_output = jnp.concatenate(
        [near[:, cin : cin + cout], near[:, cin + cout : cin + 2 * cout]], 2
    ).reshape(img_dev, ho, wo, out_part)
    parts_te = near[:, cin + 2 * cout :].reshape(no, -1, lanes)
    rows_es = group_es[0].shape[1]
    half_te = scatter_last(*[parts_te[k] for k in range(no)])

    def finished(half, parts):
        h = lanes // 2
        shapes = [(4 * n, h) if by_rows else (n, 2 * lanes) for _, n, by_rows in parts]

        def kernel(geo, x, y, *outs):
            for (first, n, by_rows), out in zip(parts, outs, strict=True):
                for ref, core in ((x, geo[2]), (y, 1 - geo[2])):
                    rows = slice(first, first + n)
                    if by_rows:
                        for side in range(2):
                            out[at(n, 2 * core + side), :] = ref[rows, side * h : (side + 1) * h]
                    else:
                        out[:, at(lanes, core)] = ref[rows, :]

        return run(kernel, [(s, F32) for s in shapes], [geo], *half)

    def taps_out(rows):
        return rows.reshape(9, mid_io, mid).transpose(0, 2, 1).reshape(first_taps.shape)

    rows_te = finished(half_te, [(0, rows_t, False), (rows_t, mid_i, False)])
    mids = jnp.stack([sum_one, sum_two, sum_four, sum_five], 1)
    mids = swap_full(mids, 2)
    wides = jnp.concatenate([sum_three, sum_six], 0).reshape(5, no, out_h)
    wides = swap_full(wides, 2).reshape(5, no * out_part)
    (last,), (grad_t2, grad_e2), (mids, wides), (grad_images, block_output) = together(
        [last], rows_te, [mids, wides], [grad_images, block_output]
    )
    half_rest = scatter_last(*[last[k] for k in range(no)])
    rows_r1, rows_r2 = in_h // 2, out_h // 2
    grad_r2, grad_e1, grad_s, grad_t1, grad_r1 = finished(
        half_rest,
        [
            (0, rows_r2, True),
            (rows_r2, mid_i, False),
            (rows_r2 + mid_i, in_part, False),
            (rows_es, rows_t, False),
            (rows_es + rows_t, rows_r1, True),
        ],
    )
    return (
        block_output,
        grad_images,
        grad_r1,
        taps_out(grad_t1),
        grad_e1,
        grad_s,
        grad_r2,
        taps_out(grad_t2),
        grad_e2,
        mids[1],
        mids[0],
        jnp.stack([wides[1], wides[2], wides[4]]),
        jnp.stack([wides[0], wides[0], wides[3]]),
    )


def solution(mesh):
    wide = P(("batch", "inner"), None, None, "outer")
    down = P("outer", "inner")
    up = P("inner", "outer")
    taps = P(None, None, None, ("inner", "outer"))
    whole = P()
    return jax.shard_map(
        shards,
        mesh=mesh,
        in_specs=(wide, whole, down, taps, up, down, down, taps, up)
        + (whole, whole, whole, whole, wide),
        out_specs=(wide, wide, down, taps, up, down, down, taps, up, whole, whole, whole, whole),
        check_vma=False,
    )
```

```python
import math

import jax
import jax.numpy as jnp
from jax import lax
from jax.experimental import pallas as pl
from jax.experimental.pallas import tpu as pltpu
from jax.sharding import PartitionSpec as P

EPS = 1e-05
ROOT = math.sqrt(2.0 / math.pi)
CUBE = 0.044715
F32 = jnp.float32
BF16 = jnp.bfloat16
XS = [(k, k ^ 1) for k in range(4)]
YS = [(k, k ^ 2) for k in range(4)]
DS = [(k, k ^ 3) for k in range(4)]
FAR = 3
GEO = 3
TAPS = [(p, r) for p in range(3) for r in range(3)]


def mm(left, right):
    return lax.dot_general(left, right, (((1,), (0,)), ((), ())), preferred_element_type=F32)


def mm_nt(left, right):
    return lax.dot_general(left, right, (((1,), (1,)), ((), ())), preferred_element_type=F32)


def mm_tn(left, right):
    return lax.dot_general(left, right, (((0,), (0,)), ((), ())), preferred_element_type=F32)


def gelu(v):
    return 0.5 * v * (1.0 + jnp.tanh(ROOT * (v + CUBE * v * v * v)))


def gelu_both(v):
    t = jnp.tanh(ROOT * (v + CUBE * v * v * v))
    half = 0.5 * (1.0 + t)
    return v * half, half + 0.5 * v * (1.0 - t * t) * (ROOT * (1.0 + 3.0 * CUBE * v * v))


def gelu_slope(v):
    return gelu_both(v)[1]


def halves(x, k):
    if k & (k - 1) == 0:
        s = k.bit_length() - 1
        return lax.shift_right_logical(x, jnp.int32(s)), lax.bitwise_and(x, jnp.int32(k - 1))
    return lax.div(x, jnp.int32(k)), lax.rem(x, jnp.int32(k))


def at(unit, index, size=None):
    return pl.ds(pl.multiple_of(index * unit, unit), unit if size is None else size)


def after(x, *done):
    return lax.optimization_barrier((x, done))[0]


def together(*groups):
    flat = [x for g in groups for x in g]
    flat = list(lax.optimization_barrier(tuple(flat)))
    out = []
    for g in groups:
        out.append(flat[: len(g)])
        flat = flat[len(g) :]
    return out


def run(kernel, outs, smem, *arrays, scratch=(), flops=0, limit=20 << 20):
    shapes = [jax.ShapeDtypeStruct(s, d) for s, d in outs]
    moved = sum(a.size * a.dtype.itemsize for a in arrays)
    moved += sum(math.prod(s) * jnp.dtype(d).itemsize for s, d in outs)
    return pl.pallas_call(
        kernel,
        out_shape=shapes,
        in_specs=[pl.BlockSpec(memory_space=pltpu.SMEM)] * len(smem)
        + [pl.BlockSpec(memory_space=pltpu.VMEM)] * len(arrays),
        out_specs=[pl.BlockSpec(memory_space=pltpu.VMEM)] * len(outs),
        scratch_shapes=list(scratch),
        compiler_params=pltpu.CompilerParams(vmem_limit_bytes=limit),
        cost_estimate=pl.CostEstimate(flops=flops, bytes_accessed=moved, transcendentals=0),
    )(*smem, *arrays)


def shards(
    images,
    extents,
    first_reduce,
    first_taps,
    first_expand,
    first_shortcut,
    second_reduce,
    second_taps,
    second_expand,
    mid_gains,
    mid_shifts,
    wide_gains,
    wide_shifts,
    cotangent,
):
    nb = lax.axis_size("batch")
    ni = lax.axis_size("inner")
    no = lax.axis_size("outer")
    b = lax.axis_index("batch")
    i = lax.axis_index("inner")
    o = lax.axis_index("outer")
    c = b % 2
    img_dev, hi, wi, in_part = images.shape
    ho, wo = hi // 2, wi // 2
    out_part = cotangent.shape[3]
    m = img_dev // no
    pair = 2 * m
    cin, cout = hi * wi, ho * wo
    rin, rout = pair * cin, pair * cout
    mid = mid_gains.shape[1]
    mh = mid // 2
    in_h = in_part // 2
    out_h = out_part // 2
    kin = no * in_h
    wide = no * out_h
    mid_i = mid // ni
    mid_io = mid // (ni * no)
    peers = ni * no
    lanes = out_h

    def core_swap(x):
        return lax.ppermute(x, "batch", [(k, k ^ 1) for k in range(nb)])

    def pick(low, high):
        return jnp.where(c == 0, low, high)

    def mine(x, axis):
        h = x.shape[axis] // 2
        return pick(lax.slice_in_dim(x, 0, h, axis=axis), lax.slice_in_dim(x, h, 2 * h, axis=axis))

    def other(x, axis):
        h = x.shape[axis] // 2
        return pick(lax.slice_in_dim(x, h, 2 * h, axis=axis), lax.slice_in_dim(x, 0, h, axis=axis))

    def swap_full(x, axis):
        recv = core_swap(x)
        return pick(jnp.concatenate([x, recv], axis), jnp.concatenate([recv, x], axis))

    def over_batch(x):
        total = x
        for k in range(1, nb // 2):
            total = total + lax.ppermute(x, "batch", [(j, (j + 2 * k) % nb) for j in range(nb)])
        return total

    def sync(copies):
        got = lax.all_to_all(copies, ("inner", "outer"), split_axis=0, concat_axis=0, tiled=True)
        return got if nb == 2 else over_batch(jnp.sum(got, 0, keepdims=True))

    def to_images(x):
        return lax.all_to_all(x, "outer", split_axis=0, concat_axis=0, tiled=True)

    def taps_entries(first, w):
        def entry(tap):
            place = lambda pi, po: (pi * no + po, mid_io, 0, tap, mh)
            return (first + tap * mid_io, mid_io, 0, mh, w, place)

        return [entry(tap) for tap in range(9)], 9 * mid_io

    def up_entries(first, w):
        place = lambda pi, po: (pi, mid_i, 0, po, out_h)
        return [(first, mid_i, 0, out_h, w, place)], mid_i

    def short_entries(first, w):
        quarter = in_part // 4

        def entry(k):
            place = lambda pi, po: (po, in_part, k * quarter, pi, out_h)
            return (first + k * quarter, quarter, 0, out_h, w, place)

        return [entry(k) for k in range(4)], in_part

    def down_entries(rows):
        def make(first, w):
            half = rows // 2

            def entry(side):
                place = lambda pi, po: (po, rows, side * half, pi, mid_i)
                return (first, half, side * mid_i, mid_i, w, place)

            return [entry(0), entry(1)], half

        return make

    def table(makers):
        entries, first = [], 0
        for w, make in enumerate(makers):
            got, used = make(first, w)
            entries += got
            first += used
        return entries, first

    def middle(makers):
        entries, rows = table(makers)
        return min(first + count for first, count, *_ in entries if 2 * (first + count) >= rows)

    def region(place, pi, po, count, width):
        row, row_unit, plus, col, col_unit = place(pi, po)
        return (
            pl.ds(pl.multiple_of(row * row_unit, row_unit) + plus, count),
            pl.ds(pl.multiple_of(col * col_unit, col_unit), width),
        )

    place_io = jnp.stack([i, o]).astype(jnp.int32)

    def shifted(x, k):
        return lax.ppermute(x, "outer", [(j, (j + k) % no) for j in range(no)])

    def along_outer(shard):
        return [shard] + [shifted(shard, k) for k in range(1, no)]

    def along_inner(pieces):
        whole = jnp.stack(pieces)
        return [whole] + [lax.ppermute(whole, "inner", perm) for perm in (XS, YS, DS)]

    def along_near(pieces):
        def kernel(*refs):
            for k in range(no):
                refs[no][k] = refs[k][...]

        (whole,) = run(kernel, [((no,) + pieces[0].shape, BF16)], [], *pieces)
        return whole, lax.ppermute(whole, "inner", XS), lax.ppermute(whole, "inner", YS)

    def along_far(whole, by_x, by_y, h):
        def kernel(x, y, low, high):
            low[...] = x[:, :h]
            high[...] = y[:, h:]

        rows, cols = whole.shape[1:]
        low, high = run(
            kernel, [((no, h, cols), BF16), ((no, rows - h, cols), BF16)], [], by_x, by_y
        )
        low, high = lax.ppermute(low, "inner", YS), lax.ppermute(high, "inner", XS)
        return whole, by_x, by_y, low, high

    def assembled(parts, makers, shapes):
        entries, _ = table(makers)
        h = middle(makers)

        def kernel(where, *refs):
            sources, targets = refs[: len(parts)], refs[len(parts) :]
            for far in range(ni):
                for d in range(no):
                    pi, po = where[0] ^ far, lax.rem(where[1] + (no - d), no)
                    for first, count, lane, width, w, place in entries:
                        source, start = sources[far], first
                        if len(parts) > ni and far == FAR and first >= h:
                            source, start = sources[ni], first - h
                        targets[w][region(place, pi, po, count, width)] = source[
                            d, start : start + count, lane : lane + width
                        ]

        return run(kernel, [(s, BF16) for s in shapes], [place_io], *parts)

    def blocks_of(products, makers, operands, split=True):
        entries, rows = table(makers)
        h = middle(makers)
        sizes = [rows, rows, rows] + ([h, rows - h] if split else [rows])
        n = len(operands)

        def kernel(where, *refs):
            ins, outs, grads = refs[:n], refs[n : n + len(sizes)], refs[n + len(sizes) :]
            for grad, (_, left, right) in zip(grads, products, strict=True):
                grad[...] = mm_tn(ins[left][...], ins[right][...]).astype(BF16)
            for far in range(ni):
                for po in range(no):
                    pi = where[0] ^ far
                    for first, count, lane, width, w, place in entries:
                        out, start = outs[far], first
                        if split and far == FAR and first >= h:
                            out, start = outs[ni], first - h
                        out[po, start : start + count, lane : lane + width] = grads[w][
                            region(place, pi, po, count, width)
                        ]

        return run(
            kernel,
            [((no, r, lanes), BF16) for r in sizes],
            [place_io],
            *operands,
            scratch=[pltpu.VMEM(prod[0], BF16) for prod in products],
        )

    def scatter_far(own, to_x, to_y, low, high):
        return own, to_x, to_y, lax.ppermute(low, "inner", XS), lax.ppermute(high, "inner", YS)

    def scatter_add(own, to_x, to_y, low, high):
        h = low.shape[1]

        def kernel(x, y, a, z, out_x, out_y):
            out_x[:, :h] = x[:, :h]
            out_x[:, h:] = (x[:, h:].astype(F32) + z[...].astype(F32)).astype(BF16)
            out_y[:, :h] = (y[:, :h].astype(F32) + a[...].astype(F32)).astype(BF16)
            out_y[:, h:] = y[:, h:]

        return [own] + list(run(kernel, [(own.shape, BF16)] * 2, [], to_x, to_y, low, high))

    def scatter_near(own, to_x, to_y):
        return [own, lax.ppermute(to_x, "inner", XS), lax.ppermute(to_y, "inner", YS)]

    def scatter_inner(own, *sends):
        return [own] + [
            lax.ppermute(x, "inner", perm) for x, perm in zip(sends, (XS, YS, DS), strict=True)
        ]

    def scatter_sum(*groups):
        rows = [g[0].shape[1] for g in groups]

        def kernel(*refs):
            row, refs, out = 0, list(refs[:-1]), refs[-1]
            for g, count in zip(groups, rows, strict=True):
                mine, refs = refs[: len(g)], refs[len(g) :]
                total = mine[0][...].astype(F32)
                for ref in mine[1:]:
                    total = total + ref[...].astype(F32)
                out[:, row : row + count, :] = total.astype(BF16)
                row += count

        flat = [x for g in groups for x in g]
        return run(kernel, [((no, sum(rows), lanes), BF16)], [], *flat)[0]

    def scatter_last(*parts):
        def kernel(*refs):
            total = refs[0][...].astype(F32)
            for ref in refs[1:-1]:
                total = total + ref[...].astype(F32)
            refs[-1][...] = total

        half = over_batch(run(kernel, [(parts[0].shape, F32)], [], *parts)[0])
        return half, core_swap(half)

    first_img = ((b - c) * ni + i) * img_dev + o * m
    ext = jnp.concatenate(
        [
            lax.dynamic_slice_in_dim(extents, first_img, m, 0),
            lax.dynamic_slice_in_dim(extents, first_img + ni * img_dev, m, 0),
        ],
        0,
    )
    geo = jnp.concatenate([jnp.stack([i, o, c]), ext[:, 0], ext[:, 1]]).astype(jnp.int32)
    area = jnp.sum(extents[:, 0] * extents[:, 1]).astype(F32)
    counts = jnp.stack([4.0 * area, area])

    def iota(shape, axis):
        return lax.broadcasted_iota(jnp.int32, shape, axis)

    def out_mask(geo):
        row, col = halves(iota((cout, 1), 0), wo)
        return jnp.concatenate(
            [
                ((row < geo[GEO + k]) & (col < geo[GEO + pair + k])).astype(F32)
                for k in range(pair)
            ],
            0,
        )

    def phase_cells(shape, axis):
        phase, cell = halves(iota(shape, axis), cout)
        row, col = halves(cell, wo)
        up, left = halves(phase, 2)
        return 2 * row + up, 2 * col + left

    def in_mask(geo):
        row, col = phase_cells((cin, 1), 0)
        return jnp.concatenate(
            [
                ((row < 2 * geo[GEO + k]) & (col < 2 * geo[GEO + pair + k])).astype(F32)
                for k in range(pair)
            ],
            0,
        )

    def order(geo, k, axis):
        shape = (cin, 1) if axis == 0 else (1, cin)
        row, col = phase_cells(shape, axis)
        inside = (row < 2 * geo[GEO + k]) & (col < 2 * geo[GEO + pair + k])
        source = jnp.where(inside, row * wi + col, -1)
        return (source == iota((cin, cin), 1 - axis)).astype(F32).astype(BF16)

    def shift(dr, dc):
        row, col = halves(iota((cout, 1), 0), wo)
        row, col = row + dr, col + dc
        inside = (row >= 0) & (row < ho) & (col >= 0) & (col < wo)
        source = jnp.where(inside, row * wo + col, -1)
        return (source == iota((cout, cout), 1)).astype(F32).astype(BF16)

    def taps_shard(w):
        return mine(w, 2).transpose(0, 1, 3, 2).reshape(9 * mid_io, mh)

    def side_by_side(w):
        h = w.shape[0] // 2
        return jnp.concatenate([w[:h], w[h:]], 1)

    make_r1, make_r2 = down_entries(in_h), down_entries(out_h)
    shape_t = (mid, 9 * mh)
    makers_1 = [make_r1, taps_entries, make_r2]
    makers_2 = [up_entries, short_entries]
    makers_3 = [taps_entries, up_entries]
    shard_1 = jnp.concatenate(
        [
            side_by_side(mine(first_reduce, 0)),
            taps_shard(first_taps),
            side_by_side(mine(second_reduce, 0)),
        ],
        0,
    )
    shard_2 = jnp.concatenate([mine(first_expand, 1), mine(first_shortcut, 1)], 0)
    shard_3 = jnp.concatenate([taps_shard(second_taps), mine(second_expand, 1)], 0)
    def both_cores(x):
        own, recv = mine(x, 2), core_swap(other(x, 2))
        return jnp.stack([pick(own, recv), pick(recv, own)], 1)

    both_rows = both_cores(images.reshape(img_dev, cin, in_part))
    cot_rows = both_cores(cotangent.reshape(img_dev, cout, out_part)).reshape(
        no, m, 2, cout, out_h
    )
    cots = [
        lax.dynamic_index_in_dim(cot_rows, (o + k) % no, 0, keepdims=False).reshape(
            pair * cout, out_h
        )
        for k in range(no)
    ]
    pieces_1, (shard_2, shard_3), (both_rows,), cots = together(
        along_outer(shard_1), [shard_2, shard_3], [both_rows], cots
    )
    got_rows = to_images(both_rows)
    parts_1 = along_far(*along_near(pieces_1), middle(makers_1))
    (got_rows,), parts_1, (shard_2,) = together([got_rows], parts_1, [shard_2])
    pieces_2 = along_outer(shard_2)
    w_r1, w_t1, w_r2 = assembled(parts_1, makers_1, [(kin, mid), shape_t, (wide, mid)])

    pm = mine(jnp.concatenate([mid_gains, mid_shifts], 0), 1)
    pw = mine(
        jnp.concatenate([wide_gains, wide_shifts], 0).reshape(6, no, out_part), 2
    ).reshape(6, wide)
    (got_rows,), (pm, pw, counts, geo) = together([got_rows], [pm, pw, counts, geo])

    def moments(got, counts, which, row=0):
        total = jnp.sum(got[...], 0)
        mean = total[row : row + 1] / counts[which]
        square = total[row + 1 : row + 2] / counts[which]
        return mean, lax.rsqrt(square - mean * mean + EPS)

    def send_all(copies, rows):
        value = jnp.concatenate(rows, 0)
        for k in range(peers):
            copies[k] = value

    def sums(z, valid=None):
        zv = z if valid is None else z * valid
        return [jnp.sum(zv, 0, keepdims=True), jnp.sum(zv * z, 0, keepdims=True)]

    def copies_shape(rows, width):
        return ((peers, rows, width), F32)

    mid_f = ((rout, mh), F32)
    wide_f = ((rout, wide), F32)
    wide_b = ((rout, wide), BF16)
    mid_b = ((rout, mh), BF16)

    def one_kernel(geo, got, w, masked, strided, own, oth, raw):
        me = geo[2]
        for k in range(m):
            for j in range(no):
                for p in range(2):
                    raw[p * m + k, :, j * in_h : (j + 1) * in_h] = got[j * m + k, p, :cin, :]
        for k in range(pair):
            rows = slice(k * cin, (k + 1) * cin)
            masked[rows, :] = mm(order(geo, k, 0), raw[k]).astype(BF16)
            strided[k * cout : (k + 1) * cout, :] = masked[k * cin : k * cin + cout, :]
        own[...] = mm(masked[...], w[:, at(mh, me)])
        oth[...] = mm(masked[...], w[:, at(mh, 1 - me)])

    masked, strided_h, z_own, z_oth = run(
        one_kernel,
        [((rin, kin), BF16), ((rout, kin), BF16), ((rin, mh), F32), ((rin, mh), F32)],
        [geo],
        got_rows,
        w_r1,
        scratch=[pltpu.VMEM((pair, cin, kin), BF16)],
    )

    def one_sums(x, y, z, copies):
        z[...] = x[...] + y[...]
        send_all(copies, sums(z[...]))

    z_one, copies = run(
        one_sums, [((rin, mh), F32), copies_shape(2, mh)], [], z_own, core_swap(z_oth)
    )
    (got_one,), pieces_2, (shard_3,) = together([sync(copies)], pieces_2, [shard_3])
    parts_2 = along_near(pieces_2)
    odd = [shifted(shard_3, k) for k in range(1, no, 2)]

    def mid_sums(geo, x, y, z, copies):
        z[...] = x[...] + y[...]
        send_all(copies, sums(z[...], out_mask(geo)))

    def mid_partial(kernel, z, got, w):
        win, own, oth = run(
            kernel,
            [((rout, 9 * mh), BF16), mid_f, mid_f],
            [geo, counts],
            z,
            got,
            pm,
            w,
            scratch=[pltpu.VMEM(z.shape, BF16)],
        )
        z_next, copies = run(
            mid_sums, [mid_f, copies_shape(2, mh)], [geo], own, core_swap(oth)
        )
        return win, z_next, copies

    def normed(z, st, gains, g, s):
        return (z - st[0]) * st[1] * gains[g : g + 1] + gains[s : s + 1]

    def two_kernel(geo, counts, z, got, pm, w, win, own, oth, act):
        st = moments(got, counts, 0)
        act[...] = (gelu(normed(z[...], st, pm, 0, 4)) * in_mask(geo)).astype(BF16)
        moves = {}
        for tap, (p, r) in enumerate(TAPS):
            key = (-int(p == 0), -int(r == 0))
            plane = 2 * int(p != 1) + int(r != 1)
            if key != (0, 0) and key not in moves:
                moves[key] = shift(*key)
            for k in range(pair):
                x = act[k * cin + plane * cout : k * cin + (plane + 1) * cout, :]
                if key != (0, 0):
                    x = mm(moves[key], x).astype(BF16)
                win[k * cout : (k + 1) * cout, tap * mh : (tap + 1) * mh] = x
        own[...] = mm_nt(win[...], w[at(mh, geo[2]), :])
        oth[...] = mm_nt(win[...], w[at(mh, 1 - geo[2]), :])

    win_one, z_two, copies = mid_partial(two_kernel, z_one, got_one, w_t1)
    (got_two,), parts_2, odd, (shard_3,) = together([sync(copies)], parts_2, odd, [shard_3])
    parts_2 = along_far(*parts_2, middle(makers_2))
    even = [shifted(shard_3, k) for k in range(2, no, 2)]
    w_e1, w_s = assembled(parts_2, makers_2, [(mid, wide), (no * in_part, wide)])

    strided_r = core_swap(strided_h)

    def short_kernel(geo, x, y, w, full, z):
        me = geo[2]
        for j in range(no):
            part = slice(j * in_h, (j + 1) * in_h)
            full[:, pl.ds(pl.multiple_of(j * in_part + me * in_h, in_h), in_h)] = x[:, part]
            full[:, pl.ds(pl.multiple_of(j * in_part + (1 - me) * in_h, in_h), in_h)] = y[:, part]
        z[...] = mm(full[...], w[...])

    strided, z_short = run(
        short_kernel, [((rout, no * in_part), BF16), wide_f], [geo], strided_h, strided_r, w_s
    )

    def act_of(row, z, got):
        def kernel(geo, counts, z, got, pm, act):
            st = moments(got, counts, 1)
            act[...] = (gelu(normed(z[...], st, pm, row, row + 4)) * out_mask(geo)).astype(BF16)

        (act,) = run(kernel, [mid_b], [geo, counts], z, got, pm)
        return act, core_swap(act)

    def join_to(full, geo, x, y):
        full[:, at(mh, geo[2])] = x[...]
        full[:, at(mh, 1 - geo[2])] = y[...]

    def three_kernel(geo, x, y, w, zs, full, z, copies):
        join_to(full, geo, x, y)
        z[...] = mm(full[...], w[...])
        send_all(copies, sums(z[...]) + sums(zs[...]))

    act_own, act_recv = act_of(1, z_two, got_two)
    act_two, z_three, copies = run(
        three_kernel,
        [((rout, mid), BF16), wide_f, copies_shape(4, wide)],
        [geo],
        act_own,
        act_recv,
        w_e1,
        z_short,
    )
    (copies,), odd, even, cots = together([copies], odd, even, cots)
    cots = cots[:1] + [shifted(x, k) for k, x in enumerate(cots) if k]
    pieces_3 = [shard_3] + [(odd if k % 2 else even)[(k - 1) // 2] for k in range(1, no)]
    (got_three,), parts_3, cots = together([sync(copies)], along_near(pieces_3), cots)
    parts_3 = along_far(*parts_3, middle(makers_3))

    def four_kernel(geo, counts, z3, zs, got, pw, w, hidden, slope, low, own, oth):
        st3, sts = moments(got, counts, 1), moments(got, counts, 1, 2)
        joined = normed(z3[...], st3, pw, 0, 3) + normed(zs[...], sts, pw, 1, 4)
        value, rise = gelu_both(joined)
        valid = out_mask(geo)
        hidden[...] = value * valid
        slope[...] = rise * valid
        low[...] = hidden[...].astype(BF16)
        own[...] = mm(low[...], w[:, at(mh, geo[2])])
        oth[...] = mm(low[...], w[:, at(mh, 1 - geo[2])])

    hidden, slope_one, hidden_low, z_own, z_oth = run(
        four_kernel,
        [wide_f, wide_f, wide_b, mid_f, mid_f],
        [geo, counts],
        z_three,
        z_short,
        got_three,
        pw,
        w_r2,
    )
    z_four, copies = run(
        mid_sums, [mid_f, copies_shape(2, mh)], [geo], z_own, core_swap(z_oth)
    )
    (got_four,), parts_3 = together([sync(copies)], parts_3)
    w_t2, w_e2 = assembled(parts_3, makers_3, [shape_t, (mid, wide)])

    def five_kernel(geo, counts, z, got, pm, w, win, own, oth, act):
        st = moments(got, counts, 1)
        act[...] = (gelu(normed(z[...], st, pm, 2, 6)) * out_mask(geo)).astype(BF16)
        for tap, (p, r) in enumerate(TAPS):
            key = (p - 1, r - 1)
            move = None if key == (0, 0) else shift(*key)
            for k in range(pair):
                x = act[k * cout : (k + 1) * cout, :]
                if move is not None:
                    x = mm(move, x).astype(BF16)
                win[k * cout : (k + 1) * cout, tap * mh : (tap + 1) * mh] = x
        own[...] = mm_nt(win[...], w[at(mh, geo[2]), :])
        oth[...] = mm_nt(win[...], w[at(mh, 1 - geo[2]), :])

    win_two, z_five, copies = mid_partial(five_kernel, z_four, got_four, w_t2)
    got_five = sync(copies)
    act_own, act_recv = act_of(3, z_five, got_five)

    def six_kernel(geo, x, y, w, full, z, copies):
        join_to(full, geo, x, y)
        z[...] = mm(full[...], w[...])
        send_all(copies, sums(z[...]))

    act_five, z_six, copies = run(
        six_kernel,
        [((rout, mid), BF16), wide_f, copies_shape(2, wide)],
        [geo],
        act_own,
        act_recv,
        w_e2,
    )
    got_six = sync(copies)

    def loss_kernel(geo, counts, z, got, pw, hidden, *refs):
        cots, (own, oth, dy, copies, value) = refs[:no], refs[no:]
        me = geo[2]
        st = moments(got, counts, 1)
        xhat = (z[...] - st[0]) * st[1]
        out, rise = gelu_both(xhat * pw[2:3] + pw[5:6] + hidden[...])
        valid = out_mask(geo)
        value[...] = (out * valid).astype(BF16)
        own[...] = value[at(m * cout, me), :]
        oth[...] = value[at(m * cout, 1 - me), :]
        for d in range(no):
            part = at(out_h, lax.rem(geo[1] + (no - d), no))
            for k in range(m):
                for p in range(2):
                    rows = slice((p * m + k) * cout, (p * m + k + 1) * cout)
                    source = slice((k * 2 + p) * cout, (k * 2 + p + 1) * cout)
                    dy[rows, part] = cots[d][source, :].astype(F32)
        dy[...] = dy[...] * (rise * valid)
        send_all(copies, dy_sums(dy[...], xhat))

    def dy_sums(dy, *xhats):
        return [jnp.sum(dy, 0, keepdims=True)] + [
            jnp.sum(dy * x, 0, keepdims=True) for x in xhats
        ]

    out_own, out_oth, dy_six, copies = run(
        loss_kernel,
        [((m * cout, wide), BF16), ((m * cout, wide), BF16), wide_f, copies_shape(2, wide)],
        [geo, counts],
        z_six,
        got_six,
        pw,
        hidden,
        *cots,
        scratch=[pltpu.VMEM((rout, wide), BF16)],
    )
    (got_g6,), (out_own, out_oth) = together([sync(copies)], [out_own, out_oth])

    def home(own, recv, others, cells, part_h):
        mores = [z.shape[1] // m for z in others]
        more = sum(mores)

        def kernel(geo, x, y, *refs):
            out, row = refs[-1], cells
            for z, count in zip(refs[:-1], mores, strict=True):
                for j in range(img_dev):
                    out[j, row : row + count, :] = z[j // m, (j % m) * count : (j % m + 1) * count]
                row += count
            for k in range(m):
                rows = slice(k * cells, (k + 1) * cells)
                for j in range(no):
                    part = slice(j * part_h, (j + 1) * part_h)
                    out[j * m + k, :cells, at(part_h, geo[2])] = x[rows, part]
                    out[j * m + k, :cells, at(part_h, 1 - geo[2])] = y[rows, part]

        shape = (img_dev, cells + more, 2 * part_h)
        return run(kernel, [(shape, BF16)], [geo], own, recv, *others)[0]

    def home_sides(own, recv):
        def kernel(geo, x, y, out):
            for j in range(no):
                part = slice(j * out_h, (j + 1) * out_h)
                for k in range(m):
                    rows = slice(k * cout, (k + 1) * cout)
                    out[j, at(cout, 2 * k + geo[2]), :] = x[rows, part]
                    out[j, at(cout, 2 * k + 1 - geo[2]), :] = y[rows, part]

        return run(kernel, [((no, pair * cout, out_h), BF16)], [geo], own, recv)[0]

    def back(dy, xhat, gain, st, valid, total, row, shift_row, count):
        shift_sum, gain_sum = total[shift_row : shift_row + 1], total[row : row + 1]
        return (
            gain * st[1] * (dy - valid * ((shift_sum + xhat * gain_sum) / count))
        ).astype(BF16)

    def back_six(geo, counts, dy, z, got, grads, pw, w, dz, own, oth, total):
        st = moments(got, counts, 1)
        total[...] = jnp.sum(grads[...], 0)
        xhat = (z[...] - st[0]) * st[1]
        dz[...] = back(dy[...], xhat, pw[2:3], st, out_mask(geo), total, 1, 0, counts[1])
        own[...] = mm_nt(dz[...], w[at(mh, geo[2]), :])
        oth[...] = mm_nt(dz[...], w[at(mh, 1 - geo[2]), :])

    dz_six, da_own, da_oth, sum_six = run(
        back_six,
        [wide_b, mid_f, mid_f, ((2, wide), F32)],
        [geo, counts],
        dy_six,
        z_six,
        got_six,
        got_g6,
        pw,
        w_e2,
    )

    def mid_dy(row, own, recv, z, got):
        def kernel(geo, counts, x, y, z, got, pm, dy, copies):
            st = moments(got, counts, 1)
            xhat = (z[...] - st[0]) * st[1]
            rise = gelu_slope(xhat * pm[row : row + 1] + pm[row + 4 : row + 5])
            dy[...] = (x[...] + y[...]) * (out_mask(geo) * rise)
            send_all(copies, dy_sums(dy[...], xhat))

        dy, copies = run(
            kernel, [mid_f, copies_shape(2, mh)], [geo, counts], own, recv, z, got, pm
        )
        return dy, copies

    def mid_dz(row, dy, z, got, grads):
        which = 0 if row == 0 else 1

        def kernel(geo, counts, dy, z, got, grads, pm, dz, total):
            st = moments(got, counts, which)
            total[...] = jnp.sum(grads[...], 0)
            xhat = (z[...] - st[0]) * st[1]
            valid = in_mask(geo) if row == 0 else out_mask(geo)
            dz[...] = back(
                dy[...], xhat, pm[row : row + 1], st, valid, total, 1, 0, counts[which]
            )

        dz, total = run(
            kernel, [(z.shape, BF16), ((2, mh), F32)], [geo, counts], dy, z, got, grads, pm
        )
        return dz, core_swap(dz), total

    dy_five, copies = mid_dy(3, da_own, core_swap(da_oth), z_five, got_five)
    got_g5 = sync(copies)
    dz_own, dz_recv, sum_five = mid_dz(3, dy_five, z_five, got_five, got_g5)

    def four_dy(geo, counts, x, y, z, got, pm, w, full, dy, copies, moved):
        join_to(full, geo, x, y)
        total = None
        for tap, (p, r) in enumerate(TAPS):
            key = (1 - p, 1 - r)
            if key == (0, 0):
                left = full[...]
            else:
                move = shift(*key)
                for k in range(pair):
                    rows = slice(k * cout, (k + 1) * cout)
                    moved[rows, :] = mm(move, full[rows, :]).astype(BF16)
                left = moved[...]
            term = mm(left, w[:, tap * mh : (tap + 1) * mh])
            total = term if total is None else total + term
        st = moments(got, counts, 1)
        xhat = (z[...] - st[0]) * st[1]
        dy[...] = total * (out_mask(geo) * gelu_slope(xhat * pm[2:3] + pm[6:7]))
        send_all(copies, dy_sums(dy[...], xhat))

    dz_five, dy_four, copies = run(
        four_dy,
        [((rout, mid), BF16), mid_f, copies_shape(2, mh)],
        [geo, counts],
        dz_own,
        dz_recv,
        z_four,
        got_four,
        pm,
        w_t2,
        scratch=[pltpu.VMEM((rout, mid), BF16)],
    )
    (got_g4,), ops_te = together([sync(copies)], [dz_five, win_two, act_five, dz_six])
    group_te = scatter_far(
        *blocks_of([(shape_t, 0, 1), ((mid, wide), 2, 3)], makers_3, ops_te)
    )
    dz_own, dz_recv, sum_four = mid_dz(2, dy_four, z_four, got_four, got_g4)

    def joined_dy(geo, counts, x, y, w, dy6, slope, z3, zs, got, full, dy, copies):
        join_to(full, geo, x, y)
        dy[...] = (dy6[...] + mm_nt(full[...], w[...])) * slope[...]
        st3, sts = moments(got, counts, 1), moments(got, counts, 1, 2)
        send_all(
            copies,
            dy_sums(dy[...], (z3[...] - st3[0]) * st3[1], (zs[...] - sts[0]) * sts[1]),
        )

    dz_four, dy_joined, copies = run(
        joined_dy,
        [((rout, mid), BF16), wide_f, copies_shape(3, wide)],
        [geo, counts],
        dz_own,
        dz_recv,
        w_r2,
        dy_six,
        slope_one,
        z_three,
        z_short,
        got_three,
    )
    (copies,), group_te = together([copies], group_te)
    (got_g3,), group_te = together([sync(copies)], group_te)
    group_te = scatter_near(*scatter_add(*group_te))

    def back_three(geo, counts, dy, z3, zs, got, grads, pw, w, dz3, dzs, own, oth, total):
        st3, sts = moments(got, counts, 1), moments(got, counts, 1, 2)
        total[...] = jnp.sum(grads[...], 0)
        valid = out_mask(geo)
        x3, xs = (z3[...] - st3[0]) * st3[1], (zs[...] - sts[0]) * sts[1]
        dz3[...] = back(dy[...], x3, pw[0:1], st3, valid, total, 1, 0, counts[1])
        dzs[...] = back(dy[...], xs, pw[1:2], sts, valid, total, 2, 0, counts[1])
        own[...] = mm_nt(dz3[...], w[at(mh, geo[2]), :])
        oth[...] = mm_nt(dz3[...], w[at(mh, 1 - geo[2]), :])

    dz_three, dz_short, da_own, da_oth, sum_three = run(
        back_three,
        [wide_b, wide_b, mid_f, mid_f, ((3, wide), F32)],
        [geo, counts],
        dy_joined,
        z_three,
        z_short,
        got_three,
        got_g3,
        pw,
        w_e1,
    )
    dy_two, copies = mid_dy(1, da_own, core_swap(da_oth), z_two, got_two)
    got_g2 = sync(copies)

    def short_back(geo, dz, w, own, oth):
        me = geo[2]
        for j in range(no):
            part = slice(j * in_h, (j + 1) * in_h)
            rows = pl.ds(pl.multiple_of(j * in_part + me * in_h, in_h), in_h)
            own[:, part] = mm_nt(dz[...], w[rows, :])
            rows = pl.ds(pl.multiple_of(j * in_part + (1 - me) * in_h, in_h), in_h)
            oth[:, part] = mm_nt(dz[...], w[rows, :])

    dz_own, dz_recv, sum_two = mid_dz(1, dy_two, z_two, got_two, got_g2)
    (dz_own,), group_te = together([dz_own], group_te)

    def one_dy(geo, counts, x, y, z, got, pm, w, full, dy, copies, moved):
        join_to(full, geo, x, y)
        for n, key in enumerate([(0, 1), (1, 0), (1, 1)]):
            move = shift(*key)
            for k in range(pair):
                rows = slice(k * cout, (k + 1) * cout)
                moved[n, rows, :] = mm(move, full[rows, :]).astype(BF16)
        for plane in range(4):
            total = None
            for p in (1,) if plane < 2 else (0, 2):
                for r in (1,) if plane % 2 == 0 else (0, 2):
                    n = 2 * int(p == 0) + int(r == 0)
                    left = full[...] if n == 0 else moved[n - 1]
                    tap = 3 * p + r
                    term = mm(left, w[:, tap * mh : (tap + 1) * mh])
                    total = term if total is None else total + term
            for k in range(pair):
                dy[k * cin + plane * cout : k * cin + (plane + 1) * cout, :] = total[
                    k * cout : (k + 1) * cout
                ]
        st = moments(got, counts, 0)
        xhat = (z[...] - st[0]) * st[1]
        dy[...] = dy[...] * (in_mask(geo) * gelu_slope(xhat * pm[0:1] + pm[4:5]))
        send_all(copies, dy_sums(dy[...], xhat))

    dz_two, dy_one, copies = run(
        one_dy,
        [((rout, mid), BF16), ((rin, mh), F32), copies_shape(2, mh)],
        [geo, counts],
        dz_own,
        dz_recv,
        z_one,
        got_one,
        pm,
        w_t1,
        scratch=[pltpu.VMEM((3, rout, mid), BF16)],
    )
    (got_g1,), ops = together(
        [sync(copies)],
        [dz_short, hidden_low, dz_four, act_two, dz_three, strided, dz_two, win_one],
    )
    dz_short = ops[0]
    ops_es, ops_t1 = ops[1:6] + ops[:1], ops[6:]
    ds_own, ds_oth = run(short_back, [((rout, kin), F32)] * 2, [geo], dz_short, w_s)
    ds_recv = core_swap(ds_oth)
    dz_own, dz_recv, sum_one = mid_dz(0, dy_one, z_one, got_one, got_g1)
    group_es = blocks_of(
        [((wide, mid), 0, 1), ((mid, wide), 2, 3), ((no * in_part, wide), 4, 5)],
        [make_r2] + makers_2,
        ops_es,
    )
    (dz_own,), group_es, group_te, outs = together(
        [dz_own], group_es, group_te, [out_own, out_oth]
    )
    group_es = scatter_far(*group_es)
    below = home_sides(outs[0], core_swap(outs[1]))

    def images_kernel(geo, x, y, w, ds, dr, full, own, oth, rows_in):
        join_to(full, geo, x, y)
        me = geo[2]
        for k in range(pair):
            rows = slice(k * cin, (k + 1) * cin)
            first = slice(k * cin, k * cin + cout)
            rest = slice(k * cin + cout, (k + 1) * cin)
            outs = slice(k * cout, (k + 1) * cout)
            rows_in[first, :] = (
                mm_nt(full[first, :], w[...]) + (ds[outs, :] + dr[outs, :])
            ).astype(BF16)
            rows_in[rest, :] = mm_nt(full[rest, :], w[...]).astype(BF16)
        for k in range(m):
            rows = slice(k * cin, (k + 1) * cin)
            for ref, img in ((oth, (1 - me) * m + k), (own, me * m + k)):
                ref[rows, :] = mm(order(geo, img, 1), rows_in[at(cin, img), :]).astype(BF16)

    dz_one, d_own, d_oth = run(
        images_kernel,
        [((rin, mid), BF16), ((m * cin, kin), BF16), ((m * cin, kin), BF16)],
        [geo],
        dz_own,
        dz_recv,
        w_r1,
        ds_own,
        ds_recv,
        scratch=[pltpu.VMEM((rin, kin), BF16)],
    )
    d_rows = home(d_own, core_swap(d_oth), [below, scatter_sum(group_te)], cin, in_h)
    (d_rows,), group_es, ops = together([d_rows], group_es, [masked, dz_one] + ops_t1)
    near = to_images(d_rows)
    group_es = scatter_near(*scatter_add(*group_es))
    group_t1 = scatter_far(
        *blocks_of([(shape_t, 2, 3), ((kin, mid), 0, 1)], [taps_entries, make_r1], ops)
    )
    group_t1, group_es = together(group_t1, group_es)
    group_t1 = scatter_near(*scatter_add(*group_t1))

    rows_t = 9 * mid_io
    last = scatter_sum(group_es, group_t1)
    (near,), (last,), totals = together(
        [near], [last], [sum_one, sum_two, sum_four, sum_five, sum_three, sum_six]
    )
    sum_one, sum_two, sum_four, sum_five, sum_three, sum_six = totals
    last = to_images(last)
    grad_images = near[:, :cin].astype(F32).reshape(images.shape)
    block_output = jnp.concatenate(
        [near[:, cin : cin + cout], near[:, cin + cout : cin + 2 * cout]], 2
    ).reshape(img_dev, ho, wo, out_part)
    parts_te = near[:, cin + 2 * cout :].reshape(no, -1, lanes)
    rows_es = group_es[0].shape[1]
    half_te = scatter_last(*[parts_te[k] for k in range(no)])

    def finished(half, parts):
        h = lanes // 2
        shapes = [(4 * n, h) if by_rows else (n, 2 * lanes) for _, n, by_rows in parts]

        def kernel(geo, x, y, *outs):
            for (first, n, by_rows), out in zip(parts, outs, strict=True):
                for ref, core in ((x, geo[2]), (y, 1 - geo[2])):
                    rows = slice(first, first + n)
                    if by_rows:
                        for side in range(2):
                            out[at(n, 2 * core + side), :] = ref[rows, side * h : (side + 1) * h]
                    else:
                        out[:, at(lanes, core)] = ref[rows, :]

        return run(kernel, [(s, F32) for s in shapes], [geo], *half)

    def taps_out(rows):
        return rows.reshape(9, mid_io, mid).transpose(0, 2, 1).reshape(first_taps.shape)

    rows_te = finished(half_te, [(0, rows_t, False), (rows_t, mid_i, False)])
    mids = jnp.stack([sum_one, sum_two, sum_four, sum_five], 1)
    mids = swap_full(mids, 2)
    wides = jnp.concatenate([sum_three, sum_six], 0).reshape(5, no, out_h)
    wides = swap_full(wides, 2).reshape(5, no * out_part)
    (last,), (grad_t2, grad_e2), (mids, wides), (grad_images, block_output) = together(
        [last], rows_te, [mids, wides], [grad_images, block_output]
    )
    half_rest = scatter_last(*[last[k] for k in range(no)])
    rows_r1, rows_r2 = in_h // 2, out_h // 2
    grad_r2, grad_e1, grad_s, grad_t1, grad_r1 = finished(
        half_rest,
        [
            (0, rows_r2, True),
            (rows_r2, mid_i, False),
            (rows_r2 + mid_i, in_part, False),
            (rows_es, rows_t, False),
            (rows_es + rows_t, rows_r1, True),
        ],
    )
    return (
        block_output,
        grad_images,
        grad_r1,
        taps_out(grad_t1),
        grad_e1,
        grad_s,
        grad_r2,
        taps_out(grad_t2),
        grad_e2,
        mids[1],
        mids[0],
        jnp.stack([wides[1], wides[2], wides[4]]),
        jnp.stack([wides[0], wides[0], wides[3]]),
    )


def solution(mesh):
    wide = P(("batch", "inner"), None, None, "outer")
    down = P("outer", "inner")
    up = P("inner", "outer")
    taps = P(None, None, None, ("inner", "outer"))
    whole = P()
    return jax.shard_map(
        shards,
        mesh=mesh,
        in_specs=(wide, whole, down, taps, up, down, down, taps, up)
        + (whole, whole, whole, whole, wide),
        out_specs=(wide, wide, down, taps, up, down, down, taps, up, whole, whole, whole, whole),
        check_vma=False,
    )
```
